512 devices in a mesh: pipe: 16 (over z, core), expert: 32 (over x, y).
Axes of the slice: x: 4, y: 8, z: 8, core: 2. Of those that a mesh axis runs over, the one named last changes fastest.
Arguments:
- section_acts: bfloat16 [16, 2048, 3584], P('pipe', 'expert'), may hold values from -6 to 6
- fwd_routes: int32 [16, 2048, 1], P('pipe', 'expert'), may hold values from 0 to 7; in each aligned block of 64 rows (0 to 63, 64 to 127, ..., all dimensions but the last counted through in order) at most 16 rows name the same one
- fwd_gates: float32 [16, 2048, 1], P('pipe', 'expert'), may hold values from 0.1 to 1
- section_grads: bfloat16 [16, 2048, 3584], P('pipe', 'expert'), may hold values from -6 to 6
- bwd_routes: int32 [16, 2048, 1], P('pipe', 'expert'), may hold values from 0 to 7; in each aligned block of 64 rows (0 to 63, 64 to 127, ..., all dimensions but the last counted through in order) at most 16 rows name the same one
- bwd_gates: float32 [16, 2048, 1], P('pipe', 'expert'), may hold values from 0.1 to 1
- saved_proj: bfloat16 [16, 32, 32, 16, 256], P('pipe', None, 'expert'), may hold values from -6 to 6
- w_gate: bfloat16 [16, 32, 3584, 128], P('pipe', 'expert'), may hold values from -0.09375 to 0.09375
- w_up: bfloat16 [16, 32, 3584, 128], P('pipe', 'expert'), may hold values from -0.09375 to 0.09375
- w_down: bfloat16 [16, 32, 128, 3584], P('pipe', 'expert'), may hold values from -0.1875 to 0.1875
Outputs:
- fwd_out: bfloat16 [16, 2048, 3584], P('pipe', 'expert')
- bwd_out: bfloat16 [16, 2048, 3584], P('pipe', 'expert')
- gate_grad: float32 [16, 2048, 1], P('pipe', 'expert')
The draws below stay inside these ranges and needn't reach their ends.
Inputs may be any that keep to these rules, and one draw needn't show every extreme that they name: `fwd_routes`: in every section, among the 64 tokens of one index of expert no value is named by more than 16 of them, a bound that some block reaches.
All inputs are finite; a program needn't handle non-finite values.
Results may differ from the reference program's by a relative error of at most 0.009.
Values may be sent and summed in bfloat16 or wider, within the bound.
A program may use at most 64 MiB of HBM per device.

```python
import math
import jax
import jax.numpy as jnp
import numpy as np

D = 3584
HID = 128
GROUP = 8
EXPERTS = 4
TOPK = 1
TOK_DEV = 64
CAP = 16
TOKENS = 2048
SOURCES = 32
SECTIONS = 16


def shard_levels(rng, shape, split, smallest, largest):
    def one(axis_at, shards_of):
        heights = jax.random.uniform(jax.random.fold_in(jax.random.fold_in(rng, 6), axis_at), (shards_of,), jnp.float32, smallest / len(split), largest / len(split))
        return jnp.repeat(jnp.exp(heights), shape[axis_at] // shards_of).reshape((-1,) + (1,) * (len(shape) - axis_at - 1))

    level = one(*split[0])
    for cut in split[1:]:
        level = level * one(*cut)
    return level


def deal_out(own_key, own, number, rows, number_of, top, bound, lean):
    order = jax.random.permutation(own_key, number_of)
    heavy_load, common = portions_of(number_of, rows * top, bound, lean, True), portions_of(number_of, rows * top, bound, lean, False)
    places = jnp.arange(number_of)

    def named(tallies, turn):
        used = int((tallies > 0).sum())
        fixed = max(1, used // 4)
        moved = fixed + (places - fixed + turn * (used - fixed)) % max(1, number_of - fixed)
        return jnp.zeros((number_of,), jnp.int32).at[order[jnp.where(places < fixed, places, moved)]].set(jnp.asarray(tallies, jnp.int32))

    tallies = jnp.where(number % 4 == 0, named(heavy_load, number // 4), named(common, number - number // 4 - 1))
    mixed = jax.random.permutation(jax.random.fold_in(own, 3), number_of)
    giver, sink = mixed[0:number_of // 2 * 2:2], mixed[1:number_of // 2 * 2:2]
    room = jnp.minimum(tallies[giver] - 1, bound - tallies[sink]) // 2
    room = jnp.where((giver == order[0]) | (sink == order[0]) | (tallies[sink] == 0), 0, jnp.maximum(room, 0))
    moved = jax.random.randint(jax.random.fold_in(own, 4), (number_of // 2,), 0, 1 << 20) % (room + 1)
    tallies = tallies.at[giver].add(-moved).at[sink].add(moved)
    items = jnp.searchsorted(jnp.cumsum(tallies), jnp.arange(rows * top), side="right").astype(jnp.int32)
    listing = items.reshape(top, rows).T
    listing = listing[jax.random.permutation(jax.random.fold_in(own, 1), rows)]
    turn = jax.random.randint(jax.random.fold_in(own, 2), (rows, 1), 0, top)
    return jnp.take_along_axis(listing, (jnp.arange(top)[None, :] + turn) % top, axis=1)


def portions_of(count, total, bound, slope, full):
    loads = [(1 << 20) // math.isqrt(grade ** slope) + 1 for grade in range(1, count + 1)]
    largest = bound if full else min(bound, max(-(-total // count), total * loads[0] // sum(loads)))
    least = 1 if total - largest >= count - 1 else 0
    given, surplus = [largest] + [least] * (count - 1), total - largest - least * (count - 1)
    while surplus > 0:
        free = [i for i in range(1, count) if given[i] < largest] or [i for i in range(1, count) if given[i] < bound]
        whole, remaining = sum([loads[i] for i in free]), surplus
        for i in free:
            addition = min(bound - given[i], max(1, remaining * loads[i] // whole), surplus)
            given[i] = given[i] + addition
            surplus = surplus - addition
    return np.array(given)


def bell_draw(stream_key, extent, deviation, most, pieces=(), held_as=jnp.bfloat16):
    array = deviation * jax.random.normal(stream_key, extent, jnp.float32)
    if pieces:
        array = array * shard_levels(stream_key, extent, pieces, -0.22, 0.18)
    return jnp.clip(array, -most, most).astype(held_as)


def setup_inputs(seed: int = 0) -> dict:
    keys = jax.random.split(jax.random.key(seed), 11)
    section_acts = bell_draw(keys[0], (SECTIONS, TOKENS, D), 1.0, 6.0, ((0, 16), (1, 32)))
    fwd_routes_keys = jax.random.split(jax.random.fold_in(keys[1], 1), SECTIONS * TOKENS // TOK_DEV)
    fwd_routes_turns = jax.random.permutation(jax.random.fold_in(keys[1], 3), SECTIONS * TOKENS // TOK_DEV)
    fwd_routes = jax.vmap(lambda own, number: deal_out(jax.random.fold_in(keys[1], 2), own, number, TOK_DEV, 2 * EXPERTS, TOPK, CAP, 2))(fwd_routes_keys, fwd_routes_turns).reshape((SECTIONS, TOKENS, TOPK))
    fwd_gates = jnp.clip(jnp.exp(math.log(1.0) - 2.3025851 * jax.random.uniform(keys[2], (SECTIONS, TOKENS, TOPK), jnp.float32) ** shard_levels(keys[2], (SECTIONS, TOKENS, TOPK), ((0, 16), (1, 32)), -0.2, 0.2)), 0.1, 1.0)
    section_grads = bell_draw(keys[3], (SECTIONS, TOKENS, D), 1.0, 6.0, ((0, 16), (1, 32)))
    bwd_routes_keys = jax.random.split(jax.random.fold_in(keys[4], 1), SECTIONS * TOKENS // TOK_DEV)
    bwd_routes_turns = jax.random.permutation(jax.random.fold_in(keys[4], 3), SECTIONS * TOKENS // TOK_DEV)
    bwd_routes = jax.vmap(lambda own, number: deal_out(jax.random.fold_in(keys[4], 2), own, number, TOK_DEV, 2 * EXPERTS, TOPK, CAP, 2))(bwd_routes_keys, bwd_routes_turns).reshape((SECTIONS, TOKENS, TOPK))
    bwd_gates = jnp.clip(jnp.exp(math.log(1.0) - 2.3025851 * jax.random.uniform(keys[5], (SECTIONS, TOKENS, TOPK), jnp.float32) ** shard_levels(keys[5], (SECTIONS, TOKENS, TOPK), ((0, 16), (1, 32)), -0.2, 0.2)), 0.1, 1.0)
    saved_proj = bell_draw(keys[6], (SECTIONS, SOURCES, EXPERTS * GROUP, CAP, 2 * HID), 1.0, 6.0, ((0, 16), (2, 32)))
    w_gate = bell_draw(keys[7], (SECTIONS, EXPERTS * GROUP, D, HID), D ** -0.5, 0.09375, ((0, 16), (1, 32)))
    w_up = bell_draw(keys[8], (SECTIONS, EXPERTS * GROUP, D, HID), D ** -0.5, 0.09375, ((0, 16), (1, 32)))
    w_down = bell_draw(keys[9], (SECTIONS, EXPERTS * GROUP, HID, D), (GROUP * HID) ** -0.5, 0.1875, ((0, 16), (1, 32)))
    return {"section_acts": section_acts, "fwd_routes": fwd_routes, "fwd_gates": fwd_gates, "section_grads": section_grads, "bwd_routes": bwd_routes, "bwd_gates": bwd_gates, "saved_proj": saved_proj, "w_gate": w_gate, "w_up": w_up, "w_down": w_down}


def pair_places(routes):
    blocks = routes.reshape(SOURCES, TOK_DEV, TOPK)
    expert_ids = jnp.arange(EXPERTS, dtype=jnp.int32)
    chosen = (blocks[..., None] == expert_ids).astype(jnp.int32).sum(axis=2)
    before = jnp.cumsum(chosen, axis=1) - chosen
    clipped = jnp.clip(blocks, 0, EXPERTS - 1).astype(jnp.int32)
    slot = jnp.take_along_axis(before, clipped, axis=2)
    source = jnp.arange(SOURCES, dtype=jnp.int32)[:, None, None]
    place = (source * EXPERTS + clipped) * CAP + slot
    sentinel = jnp.full(place.shape, SOURCES * EXPERTS * CAP, jnp.int32)
    place = jnp.where(blocks < EXPERTS, place.astype(jnp.int32), sentinel)
    return place.reshape(TOKENS, TOPK).astype(jnp.int32)


def scatter_rows(values, place):
    spread = jnp.repeat(values, TOPK, axis=0)
    buffer = jnp.zeros((SOURCES * EXPERTS * CAP + 1, D), values.dtype)
    buffer = buffer.at[place.reshape(-1)].set(spread)
    return buffer[:-1].reshape(SOURCES, EXPERTS, CAP, D)


def padded_rows(rows):
    flat = rows.reshape(-1, rows.shape[-1])
    return jnp.concatenate([flat, jnp.zeros((1, flat.shape[1]), flat.dtype)], axis=0)


def reference(section_acts, fwd_routes, fwd_gates, section_grads, bwd_routes, bwd_gates, saved_proj, w_gate, w_up, w_down):
    f32 = jnp.float32
    outs_a, outs_b, outs_g = [], [], []
    for section in range(SECTIONS):
        wg = w_gate[section].astype(f32).reshape(EXPERTS, GROUP, D, HID)
        wu = w_up[section].astype(f32).reshape(EXPERTS, GROUP, D, HID)
        wd = w_down[section].astype(f32).reshape(EXPERTS, GROUP, HID, D)
        inputs = section_acts[(section - 1) % SECTIONS]
        place = pair_places(fwd_routes[section])
        rows_a = scatter_rows(inputs, place).astype(f32)
        pre_g = jnp.einsum("secd,egdh->segch", rows_a, wg)
        pre_u = jnp.einsum("secd,egdh->segch", rows_a, wu)
        hid_a = (pre_g * jax.nn.sigmoid(pre_g) * pre_u).astype(jnp.bfloat16)
        part_a = jnp.einsum("segch,eghd->segcd", hid_a.astype(f32), wd).astype(jnp.bfloat16)
        out_a = jnp.sum(part_a.astype(f32), axis=2)
        picked = padded_rows(out_a)[place]
        total = inputs.astype(f32) + jnp.sum(fwd_gates[section][..., None] * picked, axis=1)
        outs_a.append(total.astype(jnp.bfloat16))

        cotan = section_grads[(section + 1) % SECTIONS]
        place_b = pair_places(bwd_routes[section])
        rows_b = scatter_rows(cotan, place_b).astype(f32)
        gate_flat = jnp.zeros((SOURCES * EXPERTS * CAP + 1,), f32).at[place_b.reshape(-1)].set(bwd_gates[section].reshape(-1))
        gate_b = gate_flat[:-1].reshape(SOURCES, EXPERTS, CAP).astype(jnp.bfloat16).astype(f32)
        kept = saved_proj[section].astype(f32).reshape(SOURCES, EXPERTS, GROUP, CAP, 2 * HID)
        sg = kept[..., :HID]
        su = kept[..., HID:]
        sig = jax.nn.sigmoid(sg)
        act = sg * sig
        hid_b = (act * su).astype(jnp.bfloat16)
        out_b = jnp.einsum("segch,eghd->segcd", hid_b.astype(f32), wd)
        slot_part = jnp.sum(rows_b[:, :, None] * out_b, axis=-1).astype(jnp.bfloat16)
        slot_gg = jnp.sum(slot_part.astype(f32), axis=2)
        scaled = (gate_b[..., None] * rows_b).astype(jnp.bfloat16)
        dhid = jnp.einsum("secd,eghd->segch", scaled.astype(f32), wd)
        d_g = (dhid * su * sig * (1.0 + sg * (1.0 - sig))).astype(jnp.bfloat16)
        d_u = (dhid * act).astype(jnp.bfloat16)
        dx_part = jnp.einsum("segch,egdh->segcd", d_g.astype(f32), wg) + jnp.einsum("segch,egdh->segcd", d_u.astype(f32), wu)
        dx_part = dx_part.astype(jnp.bfloat16)
        dx_rows = jnp.sum(dx_part.astype(f32), axis=2)
        back = padded_rows(dx_rows)[place_b]
        outs_b.append((cotan.astype(f32) + jnp.sum(back, axis=1)).astype(jnp.bfloat16))
        slot_flat = jnp.concatenate([slot_gg.reshape(-1), jnp.zeros((1,), f32)])
        outs_g.append(slot_flat[place_b])
    return jnp.stack(outs_a), jnp.stack(outs_b), jnp.stack(outs_g)
```

```python
import functools

import jax
import jax.numpy as jnp
from jax import lax
from jax.experimental import pallas as pl
from jax.experimental.pallas import tpu as pltpu
from jax.sharding import PartitionSpec as P

GROUP = 8
CHUNKS = 4
PAIRS = GROUP // 2
HOPS = 4
MESH = pl.DeviceIdType.MESH
WAYS = ((0, 1), (1, -1))
f32 = jnp.float32
bf16 = jnp.bfloat16


def nt_dot(a, b):
    return lax.dot_general(a, b, (((1,), (1,)), ((), ())), preferred_element_type=f32)


def column_of(row):
    count = row.shape[1]
    shape = (count, count)
    eye = lax.broadcasted_iota(jnp.int32, shape, 0) == lax.broadcasted_iota(jnp.int32, shape, 1)
    return jnp.sum(jnp.where(eye, jnp.broadcast_to(row, shape), 0.0), axis=1, keepdims=True)


def row_of(column):
    count = column.shape[0]
    shape = (count, count)
    eye = lax.broadcasted_iota(jnp.int32, shape, 0) == lax.broadcasted_iota(jnp.int32, shape, 1)
    return jnp.sum(jnp.where(eye, jnp.broadcast_to(column, shape), 0.0), axis=0, keepdims=True)


def place_matrices(route_row, experts, cap):
    tokens = route_row.shape[1]
    slots = experts * cap
    routes = route_row.astype(f32)
    column = column_of(routes)
    at = lax.broadcasted_iota(jnp.int32, (tokens, tokens), 0)
    other = lax.broadcasted_iota(jnp.int32, (tokens, tokens), 1)
    slot = lax.broadcasted_iota(jnp.int32, (slots, tokens), 0)
    named = jnp.broadcast_to(routes, (slots, tokens)) == (slot // cap).astype(f32)
    before = jnp.dot(
        jnp.where(named, 1.0, 0.0).astype(bf16),
        jnp.where(at < other, 1.0, 0.0).astype(bf16),
        preferred_element_type=f32,
    )
    pack = jnp.where(named & (before == (slot % cap).astype(f32)), 1.0, 0.0).astype(bf16)
    slot = lax.broadcasted_iota(jnp.int32, (tokens, slots), 1)
    named = jnp.broadcast_to(column, (tokens, slots)) == (slot // cap).astype(f32)
    before = jnp.dot(
        jnp.where(other < at, 1.0, 0.0).astype(bf16),
        jnp.where(named, 1.0, 0.0).astype(bf16),
        preferred_element_type=f32,
    )
    unpack = jnp.where(named & (before == (slot % cap).astype(f32)), 1.0, 0.0).astype(bf16)
    return pack, unpack


def kernel(
    acts,
    grads,
    routes_a,
    gates_a,
    routes_b,
    gates_b,
    kept,
    w_gate,
    w_up,
    w_down,
    out_a,
    out_b,
    out_g,
    in_a,
    in_b,
    packed_a,
    packed_b,
    rows_a,
    rows_b,
    part_a,
    part_b,
    sums_a,
    sums_b,
    back_a,
    back_b,
    whole_a,
    whole_b,
    wide,
    down,
    saved,
    slot_own,
    slot_sent,
    slot_got,
    slot_fold,
    slot_back,
    load_sem,
    save_sem,
    pipe_send,
    pipe_recv,
    spread_send,
    spread_recv,
    ring_send,
    ring_recv,
    fold_send,
    fold_recv,
    home_send,
    home_recv,
    slot_send,
    slot_recv,
    last_send,
    last_recv,
):
    stage = lax.axis_index("pipe")
    stages = lax.axis_size("pipe")
    index = lax.axis_index("expert")
    x = index // GROUP
    y = index % GROUP
    chunks, experts, cap, width = packed_a.shape
    hidden = down.shape[1]
    half = experts // 2
    spread = experts * cap

    def column(xx):
        return {"expert": xx * GROUP + y}

    def ring(by):
        return {"expert": x * GROUP + (y + GROUP + by) % GROUP}

    def along(by):
        return {"pipe": (stage + stages + by) % stages}

    def remote(src, dst, send, recv, device):
        return pltpu.make_async_remote_copy(
            src_ref=src,
            dst_ref=dst,
            send_sem=send,
            recv_sem=recv,
            device_id=device,
            device_id_type=MESH,
        )

    def start_of(c):
        return c * width if isinstance(c, int) else pl.multiple_of(c * width, 128)

    def each_chunk(body):
        lax.fori_loop(0, chunks, lambda c, carry: (body(c), carry)[1], 0)

    loads = [
        pltpu.make_async_copy(w_gate.at[0, 0], wide.at[:, pl.ds(0, hidden)], load_sem.at[0]),
        pltpu.make_async_copy(w_up.at[0, 0], wide.at[:, pl.ds(hidden, hidden)], load_sem.at[1]),
        pltpu.make_async_copy(kept.at[0, :, 0], saved, load_sem.at[2]),
    ]
    for c in range(chunks):
        loads.append(
            pltpu.make_async_copy(
                w_down.at[0, 0, :, pl.ds(c * width, width)], down.at[c], load_sem.at[3 + c]
            )
        )

    barrier = pltpu.get_barrier_semaphore()
    partners = [along(1), along(-1), ring(1), ring(-1)]
    partners += [column((x + j) % experts) for j in range(1, experts)]
    for partner in partners:
        pl.semaphore_signal(barrier, inc=1, device_id=partner, device_id_type=MESH)
    pl.semaphore_wait(barrier, len(partners))

    def pipe_copy(ab, c):
        source, target = ((acts, in_a), (grads, in_b))[ab]
        return remote(
            source.at[0, :, pl.ds(start_of(c), width)],
            target.at[c],
            pipe_send.at[ab, c],
            pipe_recv.at[ab, c],
            along(1 - 2 * ab),
        )

    for ab in (0, 1):
        for c in range(chunks):
            pipe_copy(ab, c).start()
    for load in loads:
        load.start()

    pack_a, unpack_a = place_matrices(routes_a[...], experts, cap)
    pack_b, unpack_b = place_matrices(routes_b[...], experts, cap)
    gate_a = column_of(gates_a[...])
    gate_b = column_of(gates_b[...].astype(bf16).astype(f32))

    def spread_copy(ab, c, j):
        packed, rows = ((packed_a, rows_a), (packed_b, rows_b))[ab]
        to = (x + j) % experts
        return remote(
            packed.at[c, to],
            rows.at[y, c, x],
            spread_send.at[ab, c, j - 1],
            spread_recv.at[ab, c, j - 1],
            column(to),
        )

    def pack_chunk(ab, c):
        source, packed, rows = ((in_a, packed_a, rows_a), (in_b, packed_b, rows_b))[ab]
        pack = (pack_a, pack_b)[ab]
        remote(
            source.at[c], source.at[c], pipe_send.at[ab, c], pipe_recv.at[ab, c], along(1)
        ).wait_recv()
        chosen = jnp.dot(pack, source[c], preferred_element_type=f32).astype(bf16)
        packed[c] = chosen.reshape(experts, cap, width)
        for j in range(1, experts):
            spread_copy(ab, c, j).start()
        rows[y, c, x] = packed[c, x]

    def spread_wait(ab, c):
        rows = (rows_a, rows_b)[ab]
        for j in range(1, experts):
            got = rows.at[y, c, (x + experts - j) % experts]
            remote(
                got, got, spread_send.at[ab, c, j - 1], spread_recv.at[ab, c, j - 1], column(x)
            ).wait_recv()

    def halves(ref, d, t, far):
        return ref.at[pl.ds(d * half, half)] if t == far else ref

    def ring_copy(ab, t, c, d, sign):
        rows = (rows_a, rows_b)[ab]
        block = halves(rows.at[(y + GROUP - sign * t) % GROUP, c], d, t, HOPS - 1)
        return remote(
            block,
            block,
            ring_send.at[ab, d, t * chunks + c],
            ring_recv.at[ab, d, t * chunks + c],
            ring(sign),
        )

    def ring_wait(ab, t, c, d, sign):
        rows = (rows_a, rows_b)[ab]
        block = halves(rows.at[(y + GROUP - sign * (t + 1)) % GROUP, c], d, t, HOPS - 1)
        remote(
            block,
            block,
            ring_send.at[ab, d, t * chunks + c],
            ring_recv.at[ab, d, t * chunks + c],
            ring(sign),
        ).wait_recv()

    def ring_step(ab, t, c):
        for d, sign in WAYS:
            if t:
                ring_wait(ab, t - 1, c, d, sign)
            ring_copy(ab, t, c, d, sign).start()

    def ring_last(ab, c):
        for d, sign in WAYS:
            ring_wait(ab, HOPS - 1, c, d, sign)

    def fold_copy(ab, t, c, d, sign):
        part, sums = ((part_a, sums_a), (part_b, sums_b))[ab]
        block = part.at[(y + GROUP + sign * (HOPS - t)) % GROUP, c]
        return remote(
            halves(block, d, t, 0),
            halves(sums.at[d, t, c], d, t, 0),
            fold_send.at[ab, d, t * chunks + c],
            fold_recv.at[ab, d, t * chunks + c],
            ring(sign),
        )

    def fold_wait(ab, t, c, d, sign):
        sums = (sums_a, sums_b)[ab]
        got = halves(sums.at[d, t, c], d, t, 0)
        remote(
            got,
            got,
            fold_send.at[ab, d, t * chunks + c],
            fold_recv.at[ab, d, t * chunks + c],
            ring(sign),
        ).wait_recv()

    def fold_step(ab, t, c):
        part, sums = ((part_a, sums_a), (part_b, sums_b))[ab]
        for d, sign in WAYS:
            block = (y + GROUP + sign * (HOPS - t)) % GROUP
            if t:
                fold_wait(ab, t - 1, c, d, sign)
                at = pl.ds(d * half, half) if t == 1 else pl.ds(0, experts)
                part[block, c, at] = (
                    part[block, c, at].astype(f32) + sums[d, t - 1, c, at].astype(f32)
                ).astype(bf16)
            fold_copy(ab, t, c, d, sign).start()

    def home_copy(ab, c, j):
        part, back = ((part_a, back_a), (part_b, back_b))[ab]
        to = (x + j) % experts
        return remote(
            part.at[y, c, to],
            back.at[c, x],
            home_send.at[ab, c, j - 1],
            home_recv.at[ab, c, j - 1],
            column(to),
        )

    def fold_last(ab, c):
        part, sums, back = ((part_a, sums_a, back_a), (part_b, sums_b, back_b))[ab]
        for d, sign in WAYS:
            fold_wait(ab, HOPS - 1, c, d, sign)
        part[y, c] = (
            part[y, c].astype(f32)
            + sums[0, HOPS - 1, c].astype(f32)
            + sums[1, HOPS - 1, c].astype(f32)
        ).astype(bf16)
        for j in range(1, experts):
            home_copy(ab, c, j).start()
        back[c, x] = part[y, c, x]

    def save_copy(ab, c):
        whole, out = ((whole_a, out_a), (whole_b, out_b))[ab]
        return pltpu.make_async_copy(
            whole.at[c], out.at[0, :, pl.ds(start_of(c), width)], save_sem.at[ab, c]
        )

    def finish(ab, c):
        source, back, whole = ((in_a, back_a, whole_a), (in_b, back_b, whole_b))[ab]
        unpack, gate = ((unpack_a, gate_a), (unpack_b, gate_b))[ab]
        for j in range(1, experts):
            got = back.at[c, (x + experts - j) % experts]
            remote(
                got, got, home_send.at[ab, c, j - 1], home_recv.at[ab, c, j - 1], column(x)
            ).wait_recv()
        picked = jnp.dot(unpack, back[c].reshape(spread, width), preferred_element_type=f32)
        whole[c] = (source[c].astype(f32) + gate * picked).astype(bf16)
        save_copy(ab, c).start()

    def pair_rows(rows, p, c):
        return rows[pl.ds(2 * p, 2), c].reshape(2 * spread, width)

    def forward(p):
        pre = jnp.zeros((2 * spread, 2 * hidden), f32)
        for c in range(chunks):
            pre += jnp.dot(
                pair_rows(rows_a, p, c),
                wide[pl.ds(c * width, width), :],
                preferred_element_type=f32,
            )
        pre_g, pre_u = pre[:, :hidden], pre[:, hidden:]
        hid = (pre_g * jax.nn.sigmoid(pre_g) * pre_u).astype(bf16)
        for c in range(chunks):
            part_a[pl.ds(2 * p, 2), c] = (
                jnp.dot(hid, down[c], preferred_element_type=f32)
                .astype(bf16)
                .reshape(2, experts, cap, width)
            )

    def backward(p):
        dhid = jnp.zeros((2 * spread, hidden), f32)
        for c in range(chunks):
            dhid += nt_dot(pair_rows(rows_b, p, c), down[c])
        both = jnp.concatenate(
            [saved[j * GROUP + 2 * p + i] for i in (0, 1) for j in range(experts)], axis=0
        ).astype(f32)
        sg, su = both[:, :hidden], both[:, hidden:]
        sig = jax.nn.sigmoid(sg)
        act = sg * sig
        hid = (act * su).astype(bf16).astype(f32)
        slot_row = jnp.sum((hid * dhid).T, axis=0, keepdims=True)
        slot_own[p] = jnp.broadcast_to(slot_row, slot_own.shape[1:])
        d_g = (dhid * su * sig * (1.0 + sg * (1.0 - sig))).astype(bf16)
        d_u = (dhid * act).astype(bf16)
        d_both = jnp.concatenate([d_g, d_u], axis=1)
        for c in range(chunks):
            part_b[pl.ds(2 * p, 2), c] = (
                nt_dot(d_both, wide[pl.ds(c * width, width), :])
                .astype(bf16)
                .reshape(2, experts, cap, width)
            )

    def slot_copy(d, t, sign):
        return remote(
            slot_sent.at[d, t],
            slot_got.at[d, t],
            slot_send.at[d, t],
            slot_recv.at[d, t],
            ring(sign),
        )

    def slot_step(t):
        for d, sign in WAYS:
            if t < d:
                continue
            pair = ((y + GROUP + sign * (HOPS - t)) % GROUP) // 2
            if t > d:
                slot_copy(d, t - 1, sign).wait_recv()
                slot_sent[d, t] = slot_own[pair] + slot_got[d, t - 1]
            else:
                slot_sent[d, t] = slot_own[pair]
            slot_copy(d, t, sign).start()

    def last_copy(j):
        return remote(
            slot_fold,
            slot_back.at[x],
            last_send.at[j - 1],
            last_recv.at[j - 1],
            column((x + j) % experts),
        )

    def slot_last():
        for d, sign in WAYS:
            slot_copy(d, HOPS - 1, sign).wait_recv()
        slot_fold[...] = slot_own[y // 2] + slot_got[0, HOPS - 1] + slot_got[1, HOPS - 1]
        for j in range(1, experts):
            last_copy(j).start()
        slot_back[x] = slot_fold[...]

    def slot_finish():
        for j in range(1, experts):
            got = slot_back.at[(x + experts - j) % experts]
            remote(
                got, got, last_send.at[j - 1], last_recv.at[j - 1], column(x)
            ).wait_recv()
        tokens = routes_b.shape[1]
        lanes = slot_back.shape[2]
        routes = column_of(routes_b[...].astype(f32))
        lane = lax.broadcasted_iota(jnp.int32, (tokens, spread), 1)
        taken = jnp.where(unpack_b > 0, (lane % cap).astype(f32), 0.0)
        slot = jnp.sum(taken, axis=1, keepdims=True)
        lane = lax.broadcasted_iota(jnp.int32, (tokens, lanes), 1)
        first = (y % 2) * spread + x * cap
        here = jnp.broadcast_to(slot, (tokens, lanes)) == (lane - first).astype(f32)
        total = jnp.zeros((tokens, lanes), f32)
        for e in range(experts):
            values = jnp.broadcast_to(slot_back[e][0:1], (tokens, lanes))
            total += jnp.where(here & (routes == float(e)), values, 0.0)
        out_g[...] = row_of(jnp.sum(total, axis=1, keepdims=True))

    for c in range(chunks):
        pack_chunk(0, c)
        if c:
            spread_wait(0, c - 1)
            ring_step(0, 0, c - 1)
    spread_wait(0, chunks - 1)
    ring_step(0, 0, chunks - 1)

    def body(c):
        ring_step(0, 1, c)
        pack_chunk(1, c)

    each_chunk(body)

    def body(c):
        ring_step(0, 2, c)
        spread_wait(1, c)

    each_chunk(body)
    each_chunk(lambda c: ring_step(0, 3, c))

    each_chunk(lambda c: ring_step(1, 0, c))
    each_chunk(lambda c: ring_last(0, c))
    for load in loads:
        load.wait()

    def body(c):
        ring_step(1, 1, c)
        forward(c)

    each_chunk(body)
    each_chunk(lambda c: ring_step(1, 2, c))
    each_chunk(lambda c: ring_step(1, 3, c))

    each_chunk(lambda c: fold_step(0, 0, c))
    each_chunk(lambda c: ring_last(1, c))

    def body(c):
        fold_step(0, 1, c)
        backward(c)

    each_chunk(body)
    each_chunk(lambda c: fold_step(0, 2, c))
    each_chunk(lambda c: fold_step(0, 3, c))

    each_chunk(lambda c: fold_step(1, 0, c))
    each_chunk(lambda c: fold_last(0, c))
    slot_step(0)

    def body(c):
        fold_step(1, 1, c)
        finish(0, c)

    each_chunk(body)
    slot_step(1)

    each_chunk(lambda c: fold_step(1, 2, c))
    slot_step(2)
    each_chunk(lambda c: fold_step(1, 3, c))
    slot_step(3)

    def body(c):
        for ab in (0, 1):
            pipe_copy(ab, c).wait_send()
            for j in range(1, experts):
                spread_copy(ab, c, j).wait_send()
            for t in range(HOPS):
                for d, sign in WAYS:
                    ring_copy(ab, t, c, d, sign).wait_send()
        for t in range(HOPS):
            for d, sign in WAYS:
                fold_copy(0, t, c, d, sign).wait_send()
        for j in range(1, experts):
            home_copy(0, c, j).wait_send()
        save_copy(0, c).wait()

    each_chunk(body)

    slot_last()
    fold_last(1, 0)

    def body(c):
        fold_last(1, c)
        finish(1, c - 1)

    lax.fori_loop(1, chunks, lambda c, carry: (body(c), carry)[1], 0)
    slot_finish()
    finish(1, chunks - 1)

    def body(c):
        for t in range(HOPS):
            for d, sign in WAYS:
                fold_copy(1, t, c, d, sign).wait_send()
        for j in range(1, experts):
            home_copy(1, c, j).wait_send()
        save_copy(1, c).wait()

    each_chunk(body)
    for d, sign in WAYS:
        for t in range(d, HOPS):
            slot_copy(d, t, sign).wait_send()
    for j in range(1, experts):
        last_copy(j).wait_send()


def on_device(
    section_acts,
    fwd_routes,
    fwd_gates,
    section_grads,
    bwd_routes,
    bwd_gates,
    saved_proj,
    w_gate,
    w_up,
    w_down,
):
    experts = lax.axis_size("expert") // GROUP
    _, tokens, model = section_acts.shape
    cap, hidden = saved_proj.shape[3], w_gate.shape[3]
    width = model // CHUNKS
    sources = saved_proj.shape[1]
    rows = (CHUNKS, experts, cap, width)
    lanes = 2 * experts * cap
    dma = pltpu.SemaphoreType.DMA
    hbm = pl.BlockSpec(memory_space=pl.ANY)
    vmem = pl.BlockSpec(memory_space=pltpu.VMEM)

    def as_row(array):
        return array.reshape(1, tokens)

    out_a, out_b, out_g = pl.pallas_call(
        kernel,
        out_shape=(
            jax.ShapeDtypeStruct(section_acts.shape, bf16),
            jax.ShapeDtypeStruct(section_grads.shape, bf16),
            jax.ShapeDtypeStruct((1, tokens), f32),
        ),
        in_specs=[hbm, hbm, vmem, vmem, vmem, vmem, hbm, hbm, hbm, hbm],
        out_specs=(hbm, hbm, vmem),
        scratch_shapes=[
            pltpu.VMEM((CHUNKS, tokens, width), bf16),
            pltpu.VMEM((CHUNKS, tokens, width), bf16),
            pltpu.VMEM(rows, bf16),
            pltpu.VMEM(rows, bf16),
            pltpu.VMEM((GROUP,) + rows, bf16),
            pltpu.VMEM((GROUP,) + rows, bf16),
            pltpu.VMEM((GROUP,) + rows, bf16),
            pltpu.VMEM((GROUP,) + rows, bf16),
            pltpu.VMEM((2, HOPS) + rows, bf16),
            pltpu.VMEM((2, HOPS) + rows, bf16),
            pltpu.VMEM(rows, bf16),
            pltpu.VMEM(rows, bf16),
            pltpu.VMEM((CHUNKS, tokens, width), bf16),
            pltpu.VMEM((CHUNKS, tokens, width), bf16),
            pltpu.VMEM((model, 2 * hidden), bf16),
            pltpu.VMEM((CHUNKS, hidden, width), bf16),
            pltpu.VMEM((sources, cap, 2 * hidden), bf16),
            pltpu.VMEM((PAIRS, 8, lanes), f32),
            pltpu.VMEM((2, HOPS, 8, lanes), f32),
            pltpu.VMEM((2, HOPS, 8, lanes), f32),
            pltpu.VMEM((8, lanes), f32),
            pltpu.VMEM((experts, 8, lanes), f32),
            dma((3 + CHUNKS,)),
            dma((2, CHUNKS)),
            dma((2, CHUNKS)),
            dma((2, CHUNKS)),
            dma((2, CHUNKS, experts - 1)),
            dma((2, CHUNKS, experts - 1)),
            dma((2, 2, HOPS * CHUNKS)),
            dma((2, 2, HOPS * CHUNKS)),
            dma((2, 2, HOPS * CHUNKS)),
            dma((2, 2, HOPS * CHUNKS)),
            dma((2, CHUNKS, experts - 1)),
            dma((2, CHUNKS, experts - 1)),
            dma((2, HOPS)),
            dma((2, HOPS)),
            dma((experts - 1,)),
            dma((experts - 1,)),
        ],
        compiler_params=pltpu.CompilerParams(
            collective_id=0, has_side_effects=True, vmem_limit_bytes=56 * 2**20
        ),
        cost_estimate=pl.CostEstimate(
            flops=2 * 2 * GROUP * experts * cap * model * 3 * hidden,
            bytes_accessed=2 * 3 * model * hidden + 8 * tokens * model,
            transcendentals=2 * GROUP * experts * cap * hidden,
        ),
        name="relay_experts",
    )(
        section_acts,
        section_grads,
        as_row(fwd_routes),
        as_row(fwd_gates),
        as_row(bwd_routes),
        as_row(bwd_gates),
        saved_proj,
        w_gate,
        w_up,
        w_down,
    )
    return out_a, out_b, out_g.reshape(1, tokens, 1)


def solution(mesh):
    tokens = P("pipe", "expert", None)
    weights = P("pipe", "expert", None, None)
    placed = (tokens,) * 6 + (P("pipe", None, "expert", None, None),) + (weights,) * 3
    return jax.shard_map(
        on_device, mesh=mesh, in_specs=placed, out_specs=(tokens,) * 3, check_vma=False
    )
```

```python
import functools

import jax
import jax.numpy as jnp
from jax import lax
from jax.experimental import pallas as pl
from jax.experimental.pallas import tpu as pltpu
from jax.sharding import PartitionSpec as P

GROUP = 8
CHUNKS = 7
PAIRS = GROUP // 2
LANES = 128
HOPS = 4
MESH = pl.DeviceIdType.MESH
WAYS = ((0, 1), (1, -1))
f32 = jnp.float32
bf16 = jnp.bfloat16


def nt_dot(a, b):
    return lax.dot_general(a, b, (((1,), (1,)), ((), ())), preferred_element_type=f32)


def column_of(row):
    count = row.shape[1]
    shape = (count, count)
    eye = lax.broadcasted_iota(jnp.int32, shape, 0) == lax.broadcasted_iota(jnp.int32, shape, 1)
    return jnp.sum(jnp.where(eye, jnp.broadcast_to(row, shape), 0.0), axis=1, keepdims=True)


def row_of(column):
    count = column.shape[0]
    shape = (count, count)
    eye = lax.broadcasted_iota(jnp.int32, shape, 0) == lax.broadcasted_iota(jnp.int32, shape, 1)
    return jnp.sum(jnp.where(eye, jnp.broadcast_to(column, shape), 0.0), axis=0, keepdims=True)


def place_matrices(route_row, experts, cap):
    tokens = route_row.shape[1]
    slots = experts * cap
    routes = route_row.astype(f32)
    column = column_of(routes)
    at = lax.broadcasted_iota(jnp.int32, (tokens, tokens), 0)
    other = lax.broadcasted_iota(jnp.int32, (tokens, tokens), 1)
    slot = lax.broadcasted_iota(jnp.int32, (slots, tokens), 0)
    named = jnp.broadcast_to(routes, (slots, tokens)) == (slot // cap).astype(f32)
    before = jnp.dot(
        jnp.where(named, 1.0, 0.0).astype(bf16),
        jnp.where(at < other, 1.0, 0.0).astype(bf16),
        preferred_element_type=f32,
    )
    pack = jnp.where(named & (before == (slot % cap).astype(f32)), 1.0, 0.0).astype(bf16)
    slot = lax.broadcasted_iota(jnp.int32, (tokens, slots), 1)
    named = jnp.broadcast_to(column, (tokens, slots)) == (slot // cap).astype(f32)
    before = jnp.dot(
        jnp.where(other < at, 1.0, 0.0).astype(bf16),
        jnp.where(named, 1.0, 0.0).astype(bf16),
        preferred_element_type=f32,
    )
    unpack = jnp.where(named & (before == (slot % cap).astype(f32)), 1.0, 0.0).astype(bf16)
    return pack, unpack


def slices_of(model):
    tiles = model // LANES
    wide, slim = -(-tiles // GROUP) * LANES, tiles // GROUP * LANES
    many = tiles % GROUP
    starts = [min(r, many) * wide + max(r - many, 0) * slim for r in range(GROUP)]
    return [(start, wide if r < many else slim) for r, start in enumerate(starts)], many


def kernel(
    acts,
    grads,
    routes_a,
    gates_a,
    routes_b,
    gates_b,
    kept,
    w_gate,
    w_up,
    w_down,
    out_a,
    out_b,
    out_g,
    in_a,
    in_b,
    packed_a,
    packed_b,
    rows_a,
    local_b,
    cot_b,
    held,
    dhid_part,
    dhid_sums,
    hid_all,
    slice_part,
    slice_got,
    part_b,
    sums_b,
    back_a,
    back_b,
    whole_a,
    whole_b,
    both_w,
    saved,
    slot_own,
    slot_sent,
    slot_got,
    slot_fold,
    slot_back,
    load_sem,
    save_a_sem,
    save_b_sem,
    pipe_send,
    pipe_recv,
    spread_send,
    spread_recv,
    deal_send,
    deal_recv,
    cot_send,
    cot_recv,
    rows_send,
    rows_recv,
    dhid_send,
    dhid_recv,
    hid_send,
    hid_recv,
    slice_send,
    slice_recv,
    home_a_send,
    home_a_recv,
    fold_send,
    fold_recv,
    home_b_send,
    home_b_recv,
    slot_send,
    slot_recv,
    last_send,
    last_recv,
):
    stage = lax.axis_index("pipe")
    stages = lax.axis_size("pipe")
    index = lax.axis_index("expert")
    x = index // GROUP
    y = index % GROUP
    experts, chunks, cap, width = packed_a.shape
    model, hidden = both_w.shape[0], both_w.shape[1] // 2
    spread = experts * cap
    slices, many = slices_of(model)
    wide, slim = slices[0][1], slices[-1][1]
    shift = stage % 2 * many

    def slice_at(yy):
        return (yy + shift) % GROUP

    mine = slice_at(y)

    def with_slice(r, act):
        @pl.when(r < many)
        def _():
            act(pl.multiple_of(r * wide, LANES), wide)

        @pl.when(r >= many)
        def _():
            act(pl.multiple_of(many * wide + (r - many) * slim, LANES), slim)

    def column(xx):
        return {"expert": xx * GROUP + y}

    def ring(by):
        return {"expert": x * GROUP + (y + GROUP + by) % GROUP}

    def along(by):
        return {"pipe": (stage + stages + by) % stages}

    def remote(src, dst, send, recv, device):
        return pltpu.make_async_remote_copy(
            src_ref=src,
            dst_ref=dst,
            send_sem=send,
            recv_sem=recv,
            device_id=device,
            device_id_type=MESH,
        )

    def each(count, body, first=0):
        lax.fori_loop(first, count, lambda c, carry: (body(c), carry)[1], 0)

    def columns(c):
        return pl.ds(c * width if isinstance(c, int) else pl.multiple_of(c * width, LANES), width)

    barrier = pltpu.get_barrier_semaphore()
    partners = [along(1), along(-1)] + [ring(j) for j in range(1, GROUP)]
    partners += [column((x + j) % experts) for j in range(1, experts)]
    for partner in partners:
        pl.semaphore_signal(barrier, inc=1, device_id=partner, device_id_type=MESH)
    pl.semaphore_wait(barrier, len(partners))

    def pipe_copy(ab):
        source, target = ((acts, in_a), (grads, in_b))[ab]
        return remote(
            source.at[0], target, pipe_send.at[ab], pipe_recv.at[ab], along(1 - 2 * ab)
        )

    for ab in (1, 0):
        pipe_copy(ab).start()

    def deal_copy(j, start, size):
        return remote(
            w_down.at[0, 0, :, pl.ds(start, size)],
            held.at[y, :, pl.ds(0, size)],
            deal_send.at[j],
            deal_recv.at[j],
            ring(j),
        )

    def deal_own(start, size):
        return pltpu.make_async_copy(
            w_down.at[0, 0, :, pl.ds(start, size)], held.at[y, :, pl.ds(0, size)], deal_send.at[0]
        )

    def deal(j):
        with_slice(slice_at(y + j), lambda start, size: deal_copy(j, start, size).start())

    def deal_sent(j):
        with_slice(slice_at(y + j), lambda start, size: deal_copy(j, start, size).wait_send())

    def deal_got(start, size):
        def body(j):
            got = held.at[(y + GROUP - j) % GROUP, :, pl.ds(0, size)]
            remote(got, got, deal_send.at[j], deal_recv.at[j], ring(j)).wait_recv()

        deal_own(start, size).wait()
        each(GROUP, body, 1)

    each(GROUP, deal, 1)
    with_slice(mine, lambda start, size: deal_own(start, size).start())
    loads = [
        pltpu.make_async_copy(w_gate.at[0, 0], both_w.at[:, pl.ds(0, hidden)], load_sem.at[0]),
        pltpu.make_async_copy(w_up.at[0, 0], both_w.at[:, pl.ds(hidden, hidden)], load_sem.at[1]),
        pltpu.make_async_copy(kept.at[0, :, 0], saved, load_sem.at[2]),
    ]
    for load in loads:
        load.start()

    @pl.when(mine >= many)
    def _():
        held[:, :, slim:] = jnp.zeros((GROUP, hidden, wide - slim), bf16)
        cot_b[:, :, :, slim:] = jnp.zeros((GROUP, experts, cap, wide - slim), bf16)

    pack_a, unpack_a = place_matrices(routes_a[...], experts, cap)
    pack_b, unpack_b = place_matrices(routes_b[...], experts, cap)
    gate_a = column_of(gates_a[...])
    gate_b = column_of(gates_b[...].astype(bf16).astype(f32))

    def spread_copy(ab, j):
        to = (x + j) % experts
        return remote(
            (packed_a, packed_b)[ab].at[to],
            (rows_a.at[y, :, x], local_b.at[x])[ab],
            spread_send.at[ab, j - 1],
            spread_recv.at[ab, j - 1],
            column(to),
        )

    def spread_wait(ab):
        for j in range(1, experts):
            sender = (x + experts - j) % experts
            got = (rows_a.at[y, :, sender], local_b.at[sender])[ab]
            remote(
                got, got, spread_send.at[ab, j - 1], spread_recv.at[ab, j - 1], column(x)
            ).wait_recv()

    def packed_rows(pack, source, start, size):
        chosen = jnp.dot(pack, source[:, start : start + size], preferred_element_type=f32)
        return chosen.astype(bf16).reshape(experts, cap, size)

    pipe_copy(1).wait_recv()
    packed_b[:, many:, :, slim:] = jnp.zeros((experts, GROUP - many, cap, wide - slim), bf16)
    for r, (start, size) in enumerate(slices):
        packed_b[:, r, :, :size] = packed_rows(pack_b, in_b, start, size)
    for j in range(1, experts):
        spread_copy(1, j).start()
    local_b[x] = packed_b[x]
    pipe_copy(0).wait_recv()
    for c in range(chunks):
        packed_a[:, c] = packed_rows(pack_a, in_a, c * width, width)
    for j in range(1, experts):
        spread_copy(0, j).start()
    rows_a[y, :, x] = packed_a[x]

    def cot_copy(j, size):
        return remote(
            local_b.at[:, slice_at(y + j), :, pl.ds(0, size)],
            cot_b.at[y, :, :, pl.ds(0, size)],
            cot_send.at[j],
            cot_recv.at[j],
            ring(j),
        )

    def cot_own(size):
        return pltpu.make_async_copy(
            local_b.at[:, mine, :, pl.ds(0, size)],
            cot_b.at[y, :, :, pl.ds(0, size)],
            cot_send.at[0],
        )

    def cot_got(start, size):
        def body(j):
            got = cot_b.at[(y + GROUP - j) % GROUP, :, :, pl.ds(0, size)]
            remote(got, got, cot_send.at[j], cot_recv.at[j], ring(j)).wait_recv()

        cot_own(size).wait()
        each(GROUP, body, 1)

    def cot(j):
        with_slice(slice_at(y + j), lambda start, size: cot_copy(j, size).start())

    def cot_sent(j):
        with_slice(slice_at(y + j), lambda start, size: cot_copy(j, size).wait_send())

    def halves(ref, d, t, far):
        half = ref.shape[0] // 2
        return ref.at[pl.ds(d * half, half)] if t == far else ref

    class Gather:
        def __init__(self, blocks, send, recv):
            self.blocks, self.send, self.recv = blocks, send, recv
            self.count = blocks.shape[1]

        def copy(self, t, c, d, sign, on=0):
            at = self.blocks.at[(y + GROUP - sign * (t + on)) % GROUP, c]
            at = halves(at, d, t, HOPS - 1)
            k = t * self.count + c
            return remote(at, at, self.send.at[d, k], self.recv.at[d, k], ring(sign))

        def step(self, t, c):
            for d, sign in WAYS:
                if t:
                    self.copy(t - 1, c, d, sign, 1).wait_recv()
                self.copy(t, c, d, sign).start()

        def last(self, c):
            for d, sign in WAYS:
                self.copy(HOPS - 1, c, d, sign, 1).wait_recv()

        def sent(self, c):
            for t in range(HOPS):
                for d, sign in WAYS:
                    self.copy(t, c, d, sign).wait_send()

    class Fold:
        def __init__(self, part, sums, send, recv):
            self.part, self.sums, self.send, self.recv = part, sums, send, recv
            self.count = part.shape[1]

        def copy(self, t, c, d, sign):
            at = self.part.at[(y + GROUP + sign * (HOPS - t)) % GROUP, c]
            k = t * self.count + c
            return remote(
                halves(at, d, t, 0),
                halves(self.sums.at[d, t, c], d, t, 0),
                self.send.at[d, k],
                self.recv.at[d, k],
                ring(sign),
            )

        def step(self, t, c):
            half = self.part.shape[2] // 2
            for d, sign in WAYS:
                block = (y + GROUP + sign * (HOPS - t)) % GROUP
                if t:
                    self.copy(t - 1, c, d, sign).wait_recv()
                    at = pl.ds(d * half, half) if t == 1 else pl.ds(0, 2 * half)
                    self.part[block, c, at] = (
                        self.part[block, c, at].astype(f32)
                        + self.sums[d, t - 1, c, at].astype(f32)
                    ).astype(bf16)
                self.copy(t, c, d, sign).start()

        def total(self, c):
            for d, sign in WAYS:
                self.copy(HOPS - 1, c, d, sign).wait_recv()
            return (
                self.part[y, c].astype(f32)
                + self.sums[0, HOPS - 1, c].astype(f32)
                + self.sums[1, HOPS - 1, c].astype(f32)
            )

        def sent(self, c):
            for t in range(HOPS):
                for d, sign in WAYS:
                    self.copy(t, c, d, sign).wait_send()

    rows = Gather(rows_a, rows_send, rows_recv)
    hids = Gather(hid_all, hid_send, hid_recv)
    dhids = Fold(dhid_part, dhid_sums, dhid_send, dhid_recv)
    grads_x = Fold(part_b, sums_b, fold_send, fold_recv)

    def dhid_partial(p):
        here = cot_b[pl.ds(2 * p, 2)].reshape(2 * spread, wide)
        dhid = nt_dot(here, held[...].reshape(GROUP * hidden, wide)).astype(bf16)
        for g in range(GROUP):
            dhid_part[g, p] = dhid[:, g * hidden : (g + 1) * hidden].reshape(2, spread, hidden)

    def forward(p):
        pre = jnp.zeros((2 * spread, 2 * hidden), f32)
        for c in range(chunks):
            pre += jnp.dot(
                rows_a[pl.ds(2 * p, 2), c].reshape(2 * spread, width),
                both_w[pl.ds(c * width, width), :],
                preferred_element_type=f32,
            )
        pre_g, pre_u = pre[:, :hidden], pre[:, hidden:]
        hid = (pre_g * jax.nn.sigmoid(pre_g) * pre_u).astype(bf16)
        hid_all[y, p] = hid.reshape(2, spread, hidden)

    def forward_out(p):
        hid = jnp.concatenate(
            [hid_all[g, p].reshape(2 * spread, hidden) for g in range(GROUP)], axis=1
        )
        done = jnp.dot(
            hid, held[...].reshape(GROUP * hidden, wide), preferred_element_type=f32
        )
        slice_part[pl.ds(2 * p, 2)] = done.astype(bf16).reshape(2, experts, cap, wide)

    def backward(p):
        dhid = dhids.total(p).reshape(2 * spread, hidden)
        both = jnp.concatenate(
            [saved[j * GROUP + 2 * p + i] for i in (0, 1) for j in range(experts)], axis=0
        ).astype(f32)
        sg, su = both[:, :hidden], both[:, hidden:]
        sig = jax.nn.sigmoid(sg)
        act = sg * sig
        hid = (act * su).astype(bf16).astype(f32)
        slot_row = jnp.sum((hid * dhid).T, axis=0, keepdims=True)
        slot_own[p] = jnp.broadcast_to(slot_row, slot_own.shape[1:])
        d_g = (dhid * su * sig * (1.0 + sg * (1.0 - sig))).astype(bf16)
        d_u = (dhid * act).astype(bf16)
        d_both = jnp.concatenate([d_g, d_u], axis=1)
        for c in range(chunks):
            part_b[pl.ds(2 * p, 2), c] = (
                nt_dot(d_both, both_w[pl.ds(c * width, width), :])
                .astype(bf16)
                .reshape(2, experts, cap, width)
            )

    def slice_copy(j, size):
        return remote(
            slice_part.at[(y + j) % GROUP, :, :, pl.ds(0, size)],
            slice_got.at[mine, :, :, pl.ds(0, size)],
            slice_send.at[j],
            slice_recv.at[j],
            ring(j),
        )

    def home_a_copy(r, j):
        to = (x + j) % experts
        at = pl.ds(0, slices[r][1])
        return remote(
            slice_got.at[r, to, :, at],
            back_a.at[r, x, :, at],
            home_a_send.at[r, j - 1],
            home_a_recv.at[r, j - 1],
            column(to),
        )

    def home_a(r):
        off = (y + GROUP - (r + GROUP - shift) % GROUP) % GROUP

        @pl.when(off != 0)
        def _():
            got = slice_got.at[r, :, :, pl.ds(0, slices[r][1])]
            remote(got, got, slice_send.at[off], slice_recv.at[off], ring(1)).wait_recv()

        for j in range(1, experts):
            home_a_copy(r, j).start()
        back_a[r, x] = slice_got[r, x]

    def save_a(r):
        at = pl.ds(*slices[r])
        return pltpu.make_async_copy(whole_a.at[:, at], out_a.at[0, :, at], save_a_sem.at[r])

    def finish_a(r):
        start, size = slices[r]
        for j in range(1, experts):
            got = back_a.at[r, (x + experts - j) % experts, :, pl.ds(0, size)]
            remote(
                got, got, home_a_send.at[r, j - 1], home_a_recv.at[r, j - 1], column(x)
            ).wait_recv()
        picked = jnp.dot(
            unpack_a, back_a[r, :, :, :size].reshape(spread, size), preferred_element_type=f32
        )
        at = slice(start, start + size)
        whole_a[:, at] = (in_a[:, at].astype(f32) + gate_a * picked).astype(bf16)
        save_a(r).start()

    def home_b_copy(c, j):
        to = (x + j) % experts
        return remote(
            part_b.at[y, c, to],
            back_b.at[c, x],
            home_b_send.at[c, j - 1],
            home_b_recv.at[c, j - 1],
            column(to),
        )

    def home_b(c):
        part_b[y, c] = grads_x.total(c).astype(bf16)
        for j in range(1, experts):
            home_b_copy(c, j).start()
        back_b[c, x] = part_b[y, c, x]

    def save_b(c):
        return pltpu.make_async_copy(
            whole_b.at[:, columns(c)], out_b.at[0, :, columns(c)], save_b_sem.at[c]
        )

    def finish_b(c):
        for j in range(1, experts):
            got = back_b.at[c, (x + experts - j) % experts]
            remote(
                got, got, home_b_send.at[c, j - 1], home_b_recv.at[c, j - 1], column(x)
            ).wait_recv()
        picked = jnp.dot(unpack_b, back_b[c].reshape(spread, width), preferred_element_type=f32)
        whole_b[:, columns(c)] = (in_b[:, columns(c)].astype(f32) + gate_b * picked).astype(bf16)
        save_b(c).start()

    def slot_copy(d, t, sign):
        return remote(
            slot_sent.at[d, t],
            slot_got.at[d, t],
            slot_send.at[d, t],
            slot_recv.at[d, t],
            ring(sign),
        )

    def slot_step(t):
        for d, sign in WAYS:
            if t < d:
                continue
            pair = ((y + GROUP + sign * (HOPS - t)) % GROUP) // 2
            if t > d:
                slot_copy(d, t - 1, sign).wait_recv()
                slot_sent[d, t] = slot_own[pair] + slot_got[d, t - 1]
            else:
                slot_sent[d, t] = slot_own[pair]
            slot_copy(d, t, sign).start()

    def last_copy(j):
        return remote(
            slot_fold,
            slot_back.at[x],
            last_send.at[j - 1],
            last_recv.at[j - 1],
            column((x + j) % experts),
        )

    def slot_last():
        for d, sign in WAYS:
            slot_copy(d, HOPS - 1, sign).wait_recv()
        slot_fold[...] = slot_own[y // 2] + slot_got[0, HOPS - 1] + slot_got[1, HOPS - 1]
        for j in range(1, experts):
            last_copy(j).start()
        slot_back[x] = slot_fold[...]

    def slot_finish():
        for j in range(1, experts):
            got = slot_back.at[(x + experts - j) % experts]
            remote(
                got, got, last_send.at[j - 1], last_recv.at[j - 1], column(x)
            ).wait_recv()
        tokens = routes_b.shape[1]
        lanes = slot_back.shape[2]
        routes = column_of(routes_b[...].astype(f32))
        lane = lax.broadcasted_iota(jnp.int32, (tokens, spread), 1)
        taken = jnp.where(unpack_b > 0, (lane % cap).astype(f32), 0.0)
        slot = jnp.sum(taken, axis=1, keepdims=True)
        lane = lax.broadcasted_iota(jnp.int32, (tokens, lanes), 1)
        first = (y % 2) * spread + x * cap
        here = jnp.broadcast_to(slot, (tokens, lanes)) == (lane - first).astype(f32)
        total = jnp.zeros((tokens, lanes), f32)
        for e in range(experts):
            values = jnp.broadcast_to(slot_back[e][0:1], (tokens, lanes))
            total += jnp.where(here & (routes == float(e)), values, 0.0)
        out_g[...] = row_of(jnp.sum(total, axis=1, keepdims=True))

    spread_wait(1)
    each(GROUP, cot, 1)
    with_slice(mine, lambda start, size: cot_own(size).start())
    spread_wait(0)
    each(chunks, lambda c: rows.step(0, c))
    with_slice(mine, deal_got)
    with_slice(mine, cot_got)

    def body(c):
        rows.step(1, c)
        pl.when(c < PAIRS)(lambda: dhid_partial(c))

    each(chunks, body)

    def body(c):
        rows.step(2, c)
        pl.when(c < PAIRS)(lambda: dhids.step(0, c))

    each(chunks, body)

    def body(c):
        rows.step(3, c)
        pl.when(c < PAIRS)(lambda: dhids.step(1, c))

    each(chunks, body)
    each(PAIRS, lambda c: dhids.step(2, c))
    each(chunks, rows.last)
    for load in loads:
        load.wait()

    def body(p):
        forward(p)
        hids.step(0, p)
        dhids.step(3, p)

    each(PAIRS, body)

    def far_first(k):
        return (y // 2 + PAIRS // 2 + k) % PAIRS

    backward(far_first(0))
    each(chunks, lambda c: grads_x.step(0, c))
    each(PAIRS, lambda c: hids.step(1, c))

    def body(k):
        backward(far_first(k))

        @pl.when(k == 1)
        def _():
            each(PAIRS, lambda c: hids.step(2, c))

        @pl.when(k == 2)
        def _():
            each(PAIRS, lambda c: hids.step(3, c))

    each(PAIRS, body, 1)
    slot_step(0)
    each(chunks, lambda c: grads_x.step(1, c))
    slot_step(1)

    each(PAIRS, hids.last)
    each(PAIRS, forward_out)

    def body(start, size):
        each(GROUP, lambda j: slice_copy(j, size).start(), 1)

    with_slice(mine, body)
    slice_got[mine] = slice_part[y]
    each(chunks, lambda c: grads_x.step(2, c))
    slot_step(2)
    for r in range(GROUP):
        home_a(r)
    for r in range(GROUP):
        finish_a(r)
    each(chunks, lambda c: grads_x.step(3, c))
    slot_step(3)

    for ab in (0, 1):
        pipe_copy(ab).wait_send()
        for j in range(1, experts):
            spread_copy(ab, j).wait_send()
    each(GROUP, deal_sent, 1)
    each(GROUP, cot_sent, 1)
    each(chunks, rows.sent)
    each(PAIRS, dhids.sent)
    each(PAIRS, hids.sent)

    def body(start, size):
        each(GROUP, lambda j: slice_copy(j, size).wait_send(), 1)

    with_slice(mine, body)
    for r in range(GROUP):
        for j in range(1, experts):
            home_a_copy(r, j).wait_send()
        save_a(r).wait()

    slot_last()
    home_b(0)

    def body(c):
        home_b(c)
        finish_b(c - 1)

    each(chunks, body, 1)
    slot_finish()
    finish_b(chunks - 1)

    def body(c):
        grads_x.sent(c)
        for j in range(1, experts):
            home_b_copy(c, j).wait_send()
        save_b(c).wait()

    each(chunks, body)
    for d, sign in WAYS:
        for t in range(d, HOPS):
            slot_copy(d, t, sign).wait_send()
    for j in range(1, experts):
        last_copy(j).wait_send()


def on_device(
    section_acts,
    fwd_routes,
    fwd_gates,
    section_grads,
    bwd_routes,
    bwd_gates,
    saved_proj,
    w_gate,
    w_up,
    w_down,
):
    experts = lax.axis_size("expert") // GROUP
    _, tokens, model = section_acts.shape
    cap, hidden = saved_proj.shape[3], w_gate.shape[3]
    width = model // CHUNKS
    sources = saved_proj.shape[1]
    spread = experts * cap
    lanes = 2 * spread
    wide = slices_of(model)[0][0][1]
    whole = (tokens, model)
    by_slice = (experts, GROUP, cap, wide)
    by_chunk = (experts, CHUNKS, cap, width)
    blocks = (CHUNKS, experts, cap, width)
    hids = (PAIRS, 2, spread, hidden)
    dma = pltpu.SemaphoreType.DMA
    hbm = pl.BlockSpec(memory_space=pl.ANY)
    vmem = pl.BlockSpec(memory_space=pltpu.VMEM)

    def as_row(array):
        return array.reshape(1, tokens)

    def two(*shape):
        return [dma(shape), dma(shape)]

    shapes = [
        whole,
        whole,
        by_chunk,
        by_slice,
        (GROUP,) + blocks,
        by_slice,
        (GROUP, experts, cap, wide),
        (GROUP, hidden, wide),
        (GROUP,) + hids,
        (2, HOPS) + hids,
        (GROUP,) + hids,
        (GROUP, experts, cap, wide),
        (GROUP, experts, cap, wide),
        (GROUP,) + blocks,
        (2, HOPS) + blocks,
        (GROUP, experts, cap, wide),
        blocks,
        whole,
        whole,
        (model, 2 * hidden),
        (sources, cap, 2 * hidden),
    ]
    slots = [(PAIRS, 8, lanes), (2, HOPS, 8, lanes), (2, HOPS, 8, lanes), (8, lanes)]
    slots.append((experts, 8, lanes))

    out_a, out_b, out_g = pl.pallas_call(
        kernel,
        out_shape=(
            jax.ShapeDtypeStruct(section_acts.shape, bf16),
            jax.ShapeDtypeStruct(section_grads.shape, bf16),
            jax.ShapeDtypeStruct((1, tokens), f32),
        ),
        in_specs=[hbm, hbm, vmem, vmem, vmem, vmem, hbm, hbm, hbm, hbm],
        out_specs=(hbm, hbm, vmem),
        scratch_shapes=[pltpu.VMEM(shape, bf16) for shape in shapes]
        + [pltpu.VMEM(shape, f32) for shape in slots]
        + [dma((3,)), dma((GROUP,)), dma((CHUNKS,))]
        + two(2)
        + two(2, experts - 1)
        + two(GROUP)
        + two(GROUP)
        + two(2, HOPS * CHUNKS)
        + two(2, HOPS * PAIRS)
        + two(2, HOPS * PAIRS)
        + two(GROUP)
        + two(GROUP, experts - 1)
        + two(2, HOPS * CHUNKS)
        + two(CHUNKS, experts - 1)
        + two(2, HOPS)
        + two(experts - 1),
        compiler_params=pltpu.CompilerParams(
            collective_id=0, has_side_effects=True, vmem_limit_bytes=56 * 2**20
        ),
        cost_estimate=pl.CostEstimate(
            flops=2 * 2 * GROUP * spread * model * 3 * hidden,
            bytes_accessed=2 * 3 * model * hidden + 8 * tokens * model,
            transcendentals=2 * GROUP * spread * hidden,
        ),
        name="relay_experts",
    )(
        section_acts,
        section_grads,
        as_row(fwd_routes),
        as_row(fwd_gates),
        as_row(bwd_routes),
        as_row(bwd_gates),
        saved_proj,
        w_gate,
        w_up,
        w_down,
    )
    return out_a, out_b, out_g.reshape(1, tokens, 1)


def solution(mesh):
    tokens = P("pipe", "expert", None)
    weights = P("pipe", "expert", None, None)
    placed = (tokens,) * 6 + (P("pipe", None, "expert", None, None),) + (weights,) * 3
    return jax.shard_map(
        on_device, mesh=mesh, in_specs=placed, out_specs=(tokens,) * 3, check_vma=False
    )
```

```python
import functools

import jax
import jax.numpy as jnp
from jax import lax
from jax.experimental import pallas as pl
from jax.experimental.pallas import tpu as pltpu
from jax.sharding import PartitionSpec as P

GROUP = 8
CHUNKS = 7
PAIRS = GROUP // 2
LANES = 128
HOPS = 4
MESH = pl.DeviceIdType.MESH
WAYS = ((0, 1), (1, -1))
f32 = jnp.float32
bf16 = jnp.bfloat16


def nt_dot(a, b):
    return lax.dot_general(a, b, (((1,), (1,)), ((), ())), preferred_element_type=f32)


def column_of(row):
    count = row.shape[1]
    shape = (count, count)
    eye = lax.broadcasted_iota(jnp.int32, shape, 0) == lax.broadcasted_iota(jnp.int32, shape, 1)
    return jnp.sum(jnp.where(eye, jnp.broadcast_to(row, shape), 0.0), axis=1, keepdims=True)


def row_of(column):
    count = column.shape[0]
    shape = (count, count)
    eye = lax.broadcasted_iota(jnp.int32, shape, 0) == lax.broadcasted_iota(jnp.int32, shape, 1)
    return jnp.sum(jnp.where(eye, jnp.broadcast_to(column, shape), 0.0), axis=0, keepdims=True)


def place_matrices(route_row, experts, cap):
    tokens = route_row.shape[1]
    slots = experts * cap
    routes = route_row.astype(f32)
    column = column_of(routes)
    at = lax.broadcasted_iota(jnp.int32, (tokens, tokens), 0)
    other = lax.broadcasted_iota(jnp.int32, (tokens, tokens), 1)
    slot = lax.broadcasted_iota(jnp.int32, (slots, tokens), 0)
    named = jnp.broadcast_to(routes, (slots, tokens)) == (slot // cap).astype(f32)
    before = jnp.dot(
        jnp.where(named, 1.0, 0.0).astype(bf16),
        jnp.where(at < other, 1.0, 0.0).astype(bf16),
        preferred_element_type=f32,
    )
    pack = jnp.where(named & (before == (slot % cap).astype(f32)), 1.0, 0.0).astype(bf16)
    slot = lax.broadcasted_iota(jnp.int32, (tokens, slots), 1)
    named = jnp.broadcast_to(column, (tokens, slots)) == (slot // cap).astype(f32)
    before = jnp.dot(
        jnp.where(other < at, 1.0, 0.0).astype(bf16),
        jnp.where(named, 1.0, 0.0).astype(bf16),
        preferred_element_type=f32,
    )
    unpack = jnp.where(named & (before == (slot % cap).astype(f32)), 1.0, 0.0).astype(bf16)
    return pack, unpack


def slices_of(model):
    tiles = model // LANES
    wide, slim = -(-tiles // GROUP) * LANES, tiles // GROUP * LANES
    many = tiles % GROUP
    starts = [min(r, many) * wide + max(r - many, 0) * slim for r in range(GROUP)]
    return [(start, wide if r < many else slim) for r, start in enumerate(starts)], many


def kernel(
    acts,
    grads,
    routes_a,
    gates_a,
    routes_b,
    gates_b,
    kept,
    w_gate,
    w_up,
    w_down,
    out_a,
    out_b,
    out_g,
    in_a,
    in_b,
    packed_a,
    packed_b,
    rows_a,
    local_b,
    cot_b,
    held,
    dhid_part,
    dhid_sums,
    hid_all,
    slice_part,
    slice_got,
    part_b,
    sums_b,
    back_a,
    straight,
    whole_a,
    whole_b,
    both_w,
    saved,
    slot_own,
    slot_sent,
    slot_got,
    slot_fold,
    slot_back,
    load_sem,
    save_a_sem,
    save_b_sem,
    pipe_send,
    pipe_recv,
    spread_send,
    spread_recv,
    deal_send,
    deal_recv,
    cot_send,
    cot_recv,
    rows_send,
    rows_recv,
    dhid_send,
    dhid_recv,
    hid_send,
    hid_recv,
    slice_send,
    slice_recv,
    home_a_send,
    home_a_recv,
    fold_send,
    fold_recv,
    straight_send,
    straight_recv,
    slot_send,
    slot_recv,
    last_send,
    last_recv,
):
    stage = lax.axis_index("pipe")
    stages = lax.axis_size("pipe")
    index = lax.axis_index("expert")
    x = index // GROUP
    y = index % GROUP
    experts, chunks, cap, width = packed_a.shape
    model, hidden = both_w.shape[0], both_w.shape[1] // 2
    spread = experts * cap
    slices, many = slices_of(model)
    wide, slim = slices[0][1], slices[-1][1]
    shift = stage % 2 * many

    def slice_at(yy):
        return (yy + shift) % GROUP

    mine = slice_at(y)

    def with_slice(r, act):
        @pl.when(r < many)
        def _():
            act(pl.multiple_of(r * wide, LANES), wide)

        @pl.when(r >= many)
        def _():
            act(pl.multiple_of(many * wide + (r - many) * slim, LANES), slim)

    def column(xx):
        return {"expert": xx * GROUP + y}

    def beside(j, by):
        return {"expert": (x + j) % experts * GROUP + (y + GROUP + by) % GROUP}

    def ring(by):
        return {"expert": x * GROUP + (y + GROUP + by) % GROUP}

    def along(by):
        return {"pipe": (stage + stages + by) % stages}

    def remote(src, dst, send, recv, device):
        return pltpu.make_async_remote_copy(
            src_ref=src,
            dst_ref=dst,
            send_sem=send,
            recv_sem=recv,
            device_id=device,
            device_id_type=MESH,
        )

    def each(count, body, first=0):
        lax.fori_loop(first, count, lambda c, carry: (body(c), carry)[1], 0)

    def columns(c):
        return pl.ds(c * width if isinstance(c, int) else pl.multiple_of(c * width, LANES), width)

    barrier = pltpu.get_barrier_semaphore()
    partners = [along(1), along(-1)] + [ring(j) for j in range(1, GROUP)]
    partners += [column((x + j) % experts) for j in range(1, experts)]
    partners += [beside(j, sign) for j in range(1, experts) for _, sign in WAYS]
    for partner in partners:
        pl.semaphore_signal(barrier, inc=1, device_id=partner, device_id_type=MESH)
    pl.semaphore_wait(barrier, len(partners))

    def pipe_copy(ab):
        source, target = ((acts, in_a), (grads, in_b))[ab]
        return remote(
            source.at[0], target, pipe_send.at[ab], pipe_recv.at[ab], along(1 - 2 * ab)
        )

    for ab in (0, 1):
        pipe_copy(ab).start()

    def deal_copy(j, start, size):
        return remote(
            w_down.at[0, 0, :, pl.ds(start, size)],
            held.at[y, :, pl.ds(0, size)],
            deal_send.at[j],
            deal_recv.at[j],
            ring(j),
        )

    def deal_own(start, size):
        return pltpu.make_async_copy(
            w_down.at[0, 0, :, pl.ds(start, size)], held.at[y, :, pl.ds(0, size)], deal_send.at[0]
        )

    def deal(j):
        with_slice(slice_at(y + j), lambda start, size: deal_copy(j, start, size).start())

    def deal_sent(j):
        with_slice(slice_at(y + j), lambda start, size: deal_copy(j, start, size).wait_send())

    def deal_got(start, size):
        def body(j):
            got = held.at[(y + GROUP - j) % GROUP, :, pl.ds(0, size)]
            remote(got, got, deal_send.at[j], deal_recv.at[j], ring(j)).wait_recv()

        deal_own(start, size).wait()
        each(GROUP, body, 1)

    each(GROUP, deal, 1)
    with_slice(mine, lambda start, size: deal_own(start, size).start())
    loads = [
        pltpu.make_async_copy(w_gate.at[0, 0], both_w.at[:, pl.ds(0, hidden)], load_sem.at[0]),
        pltpu.make_async_copy(w_up.at[0, 0], both_w.at[:, pl.ds(hidden, hidden)], load_sem.at[1]),
        pltpu.make_async_copy(kept.at[0, :, 0], saved, load_sem.at[2]),
    ]
    for load in loads:
        load.start()

    @pl.when(mine >= many)
    def _():
        held[:, :, slim:] = jnp.zeros((GROUP, hidden, wide - slim), bf16)
        cot_b[:, :, :, slim:] = jnp.zeros((GROUP, experts, cap, wide - slim), bf16)

    pack_a, unpack_a = place_matrices(routes_a[...], experts, cap)
    pack_b, unpack_b = place_matrices(routes_b[...], experts, cap)
    gate_a = column_of(gates_a[...])
    gate_b = column_of(gates_b[...].astype(bf16).astype(f32))

    def spread_copy(ab, j):
        to = (x + j) % experts
        return remote(
            (packed_a, packed_b)[ab].at[to],
            (rows_a.at[y, :, x], local_b.at[x])[ab],
            spread_send.at[ab, j - 1],
            spread_recv.at[ab, j - 1],
            column(to),
        )

    def spread_wait(ab):
        for j in range(1, experts):
            sender = (x + experts - j) % experts
            got = (rows_a.at[y, :, sender], local_b.at[sender])[ab]
            remote(
                got, got, spread_send.at[ab, j - 1], spread_recv.at[ab, j - 1], column(x)
            ).wait_recv()

    def packed_rows(pack, source, start, size):
        chosen = jnp.dot(pack, source[:, start : start + size], preferred_element_type=f32)
        return chosen.astype(bf16).reshape(experts, cap, size)

    pipe_copy(0).wait_recv()
    for c in range(chunks):
        packed_a[:, c] = packed_rows(pack_a, in_a, c * width, width)
    for j in range(1, experts):
        spread_copy(0, j).start()
    rows_a[y, :, x] = packed_a[x]
    pipe_copy(1).wait_recv()
    packed_b[:, many:, :, slim:] = jnp.zeros((experts, GROUP - many, cap, wide - slim), bf16)
    for r, (start, size) in enumerate(slices):
        packed_b[:, r, :, :size] = packed_rows(pack_b, in_b, start, size)
    for j in range(1, experts):
        spread_copy(1, j).start()
    local_b[x] = packed_b[x]

    def cot_copy(j, size):
        return remote(
            local_b.at[:, slice_at(y + j), :, pl.ds(0, size)],
            cot_b.at[y, :, :, pl.ds(0, size)],
            cot_send.at[j],
            cot_recv.at[j],
            ring(j),
        )

    def cot_own(size):
        return pltpu.make_async_copy(
            local_b.at[:, mine, :, pl.ds(0, size)],
            cot_b.at[y, :, :, pl.ds(0, size)],
            cot_send.at[0],
        )

    def cot_got(start, size):
        def body(j):
            got = cot_b.at[(y + GROUP - j) % GROUP, :, :, pl.ds(0, size)]
            remote(got, got, cot_send.at[j], cot_recv.at[j], ring(j)).wait_recv()

        cot_own(size).wait()
        each(GROUP, body, 1)

    def cot(j):
        with_slice(slice_at(y + j), lambda start, size: cot_copy(j, size).start())

    def cot_sent(j):
        with_slice(slice_at(y + j), lambda start, size: cot_copy(j, size).wait_send())

    def halves(ref, d, t, far):
        half = ref.shape[0] // 2
        return ref.at[pl.ds(d * half, half)] if t == far else ref

    class Gather:
        def __init__(self, blocks, send, recv):
            self.blocks, self.send, self.recv = blocks, send, recv
            self.count = blocks.shape[1]

        def copy(self, t, c, d, sign, on=0):
            at = self.blocks.at[(y + GROUP - sign * (t + on)) % GROUP, c]
            at = halves(at, d, t, HOPS - 1)
            k = t * self.count + c
            return remote(at, at, self.send.at[d, k], self.recv.at[d, k], ring(sign))

        def step(self, t, c):
            for d, sign in WAYS:
                if t:
                    self.copy(t - 1, c, d, sign, 1).wait_recv()
                self.copy(t, c, d, sign).start()

        def last(self, c):
            for d, sign in WAYS:
                self.copy(HOPS - 1, c, d, sign, 1).wait_recv()

        def sent(self, c):
            for t in range(HOPS):
                for d, sign in WAYS:
                    self.copy(t, c, d, sign).wait_send()

    class Fold:
        def __init__(self, part, sums, send, recv):
            self.part, self.sums, self.send, self.recv = part, sums, send, recv
            self.count = part.shape[1]

        def copy(self, t, c, d, sign):
            at = self.part.at[(y + GROUP + sign * (HOPS - t)) % GROUP, c]
            k = t * self.count + c
            return remote(
                halves(at, d, t, 0),
                halves(self.sums.at[d, t, c], d, t, 0),
                self.send.at[d, k],
                self.recv.at[d, k],
                ring(sign),
            )

        def step(self, t, c, straight=None):
            half = self.part.shape[2] // 2
            for d, sign in WAYS:
                block = (y + GROUP + sign * (HOPS - t)) % GROUP
                if t:
                    self.copy(t - 1, c, d, sign).wait_recv()
                    at = pl.ds(d * half, half) if t == 1 else pl.ds(0, 2 * half)
                    self.part[block, c, at] = (
                        self.part[block, c, at].astype(f32)
                        + self.sums[d, t - 1, c, at].astype(f32)
                    ).astype(bf16)
                if straight is None:
                    self.copy(t, c, d, sign).start()
                else:
                    straight(c, d, sign, block)

        def total(self, c):
            for d, sign in WAYS:
                self.copy(HOPS - 1, c, d, sign).wait_recv()
            return (
                self.part[y, c].astype(f32)
                + self.sums[0, HOPS - 1, c].astype(f32)
                + self.sums[1, HOPS - 1, c].astype(f32)
            )

        def sent(self, c, hops=HOPS):
            for t in range(hops):
                for d, sign in WAYS:
                    self.copy(t, c, d, sign).wait_send()

    rows = Gather(rows_a, rows_send, rows_recv)
    hids = Gather(hid_all, hid_send, hid_recv)
    dhids = Fold(dhid_part, dhid_sums, dhid_send, dhid_recv)
    grads_x = Fold(part_b, sums_b, fold_send, fold_recv)

    def dhid_partial(p):
        here = cot_b[pl.ds(2 * p, 2)].reshape(2 * spread, wide)
        dhid = nt_dot(here, held[...].reshape(GROUP * hidden, wide)).astype(bf16)
        for g in range(GROUP):
            dhid_part[g, p] = dhid[:, g * hidden : (g + 1) * hidden].reshape(2, spread, hidden)

    def forward(p):
        pre = jnp.zeros((2 * spread, 2 * hidden), f32)
        for c in range(chunks):
            pre += jnp.dot(
                rows_a[pl.ds(2 * p, 2), c].reshape(2 * spread, width),
                both_w[pl.ds(c * width, width), :],
                preferred_element_type=f32,
            )
        pre_g, pre_u = pre[:, :hidden], pre[:, hidden:]
        hid = (pre_g * jax.nn.sigmoid(pre_g) * pre_u).astype(bf16)
        hid_all[y, p] = hid.reshape(2, spread, hidden)

    def forward_out(p):
        hid = jnp.concatenate(
            [hid_all[g, p].reshape(2 * spread, hidden) for g in range(GROUP)], axis=1
        )
        done = jnp.dot(
            hid, held[...].reshape(GROUP * hidden, wide), preferred_element_type=f32
        )
        slice_part[pl.ds(2 * p, 2)] = done.astype(bf16).reshape(2, experts, cap, wide)

    def backward(p):
        dhid = dhids.total(p).reshape(2 * spread, hidden)
        both = jnp.concatenate(
            [saved[j * GROUP + 2 * p + i] for i in (0, 1) for j in range(experts)], axis=0
        ).astype(f32)
        sg, su = both[:, :hidden], both[:, hidden:]
        sig = jax.nn.sigmoid(sg)
        act = sg * sig
        hid = (act * su).astype(bf16).astype(f32)
        slot_row = jnp.sum((hid * dhid).T, axis=0, keepdims=True)
        slot_own[p] = jnp.broadcast_to(slot_row, slot_own.shape[1:])
        d_g = (dhid * su * sig * (1.0 + sg * (1.0 - sig))).astype(bf16)
        d_u = (dhid * act).astype(bf16)
        d_both = jnp.concatenate([d_g, d_u], axis=1)
        for c in range(chunks):
            part_b[pl.ds(2 * p, 2), c] = (
                nt_dot(d_both, both_w[pl.ds(c * width, width), :])
                .astype(bf16)
                .reshape(2, experts, cap, width)
            )

    def slice_copy(j, size):
        return remote(
            slice_part.at[(y + j) % GROUP, :, :, pl.ds(0, size)],
            slice_got.at[mine, :, :, pl.ds(0, size)],
            slice_send.at[j],
            slice_recv.at[j],
            ring(j),
        )

    def home_a_copy(r, j):
        to = (x + j) % experts
        at = pl.ds(0, slices[r][1])
        return remote(
            slice_got.at[r, to, :, at],
            back_a.at[r, x, :, at],
            home_a_send.at[r, j - 1],
            home_a_recv.at[r, j - 1],
            column(to),
        )

    def home_a(r):
        off = (y + GROUP - (r + GROUP - shift) % GROUP) % GROUP

        @pl.when(off != 0)
        def _():
            got = slice_got.at[r, :, :, pl.ds(0, slices[r][1])]
            remote(got, got, slice_send.at[off], slice_recv.at[off], ring(1)).wait_recv()

        for j in range(1, experts):
            home_a_copy(r, j).start()
        back_a[r, x] = slice_got[r, x]

    def save_a(r):
        at = pl.ds(*slices[r])
        return pltpu.make_async_copy(whole_a.at[:, at], out_a.at[0, :, at], save_a_sem.at[r])

    def finish_a(r):
        start, size = slices[r]
        for j in range(1, experts):
            got = back_a.at[r, (x + experts - j) % experts, :, pl.ds(0, size)]
            remote(
                got, got, home_a_send.at[r, j - 1], home_a_recv.at[r, j - 1], column(x)
            ).wait_recv()
        picked = jnp.dot(
            unpack_a, back_a[r, :, :, :size].reshape(spread, size), preferred_element_type=f32
        )
        at = slice(start, start + size)
        whole_a[:, at] = (in_a[:, at].astype(f32) + gate_a * picked).astype(bf16)
        save_a(r).start()

    def save_b(c):
        return pltpu.make_async_copy(
            whole_b.at[:, columns(c)], out_b.at[0, :, columns(c)], save_b_sem.at[c]
        )

    def straight_copy(c, d, j, sign, block):
        return remote(
            part_b.at[block, c, (x + j) % experts],
            straight.at[c, d, x],
            straight_send.at[c, d, j],
            straight_recv.at[c],
            beside(j, sign),
        )

    def straight_own(c):
        return pltpu.make_async_copy(
            part_b.at[y, c, x], straight.at[c, 2, x], straight_recv.at[c]
        )

    def straight_mine(c):
        straight_own(c).start()
        for j in range(1, experts):
            straight_copy(c, 2, j, 0, y).start()

    def straight_last(c, d, sign, block):
        for j in range(experts):
            straight_copy(c, d, j, sign, block).start()

    def straight_sent(c):
        for d, sign in WAYS:
            block = (y + GROUP + sign) % GROUP
            for j in range(experts):
                straight_copy(c, d, j, sign, block).wait_send()
        for j in range(1, experts):
            straight_copy(c, 2, j, 0, y).wait_send()

    def straight_finish(c):
        got = straight.at[c]
        remote(
            got, got, straight_send.at[c, 0, 0], straight_recv.at[c], column(x)
        ).wait_recv()
        picked = jnp.zeros((spread, width), f32)
        for d in range(3):
            rows_d = straight[c, d].reshape(spread, width)
            picked += jnp.dot(unpack_b, rows_d, preferred_element_type=f32)
        whole_b[:, columns(c)] = (in_b[:, columns(c)].astype(f32) + gate_b * picked).astype(bf16)
        save_b(c).start()

    def slot_copy(d, t, sign):
        return remote(
            slot_sent.at[d, t],
            slot_got.at[d, t],
            slot_send.at[d, t],
            slot_recv.at[d, t],
            ring(sign),
        )

    def slot_step(t):
        for d, sign in WAYS:
            if t < d:
                continue
            pair = ((y + GROUP + sign * (HOPS - t)) % GROUP) // 2
            if t > d:
                slot_copy(d, t - 1, sign).wait_recv()
                slot_sent[d, t] = slot_own[pair] + slot_got[d, t - 1]
            else:
                slot_sent[d, t] = slot_own[pair]
            slot_copy(d, t, sign).start()

    def last_copy(j):
        return remote(
            slot_fold,
            slot_back.at[x],
            last_send.at[j - 1],
            last_recv.at[j - 1],
            column((x + j) % experts),
        )

    def slot_last():
        for d, sign in WAYS:
            slot_copy(d, HOPS - 1, sign).wait_recv()
        slot_fold[...] = slot_own[y // 2] + slot_got[0, HOPS - 1] + slot_got[1, HOPS - 1]
        for j in range(1, experts):
            last_copy(j).start()
        slot_back[x] = slot_fold[...]

    def slot_finish():
        for j in range(1, experts):
            got = slot_back.at[(x + experts - j) % experts]
            remote(
                got, got, last_send.at[j - 1], last_recv.at[j - 1], column(x)
            ).wait_recv()
        tokens = routes_b.shape[1]
        lanes = slot_back.shape[2]
        routes = column_of(routes_b[...].astype(f32))
        lane = lax.broadcasted_iota(jnp.int32, (tokens, spread), 1)
        taken = jnp.where(unpack_b > 0, (lane % cap).astype(f32), 0.0)
        slot = jnp.sum(taken, axis=1, keepdims=True)
        lane = lax.broadcasted_iota(jnp.int32, (tokens, lanes), 1)
        first = (y % 2) * spread + x * cap
        here = jnp.broadcast_to(slot, (tokens, lanes)) == (lane - first).astype(f32)
        total = jnp.zeros((tokens, lanes), f32)
        for e in range(experts):
            values = jnp.broadcast_to(slot_back[e][0:1], (tokens, lanes))
            total += jnp.where(here & (routes == float(e)), values, 0.0)
        out_g[...] = row_of(jnp.sum(total, axis=1, keepdims=True))

    spread_wait(0)
    for t in range(HOPS):
        each(chunks, functools.partial(rows.step, t))
    spread_wait(1)
    each(GROUP, cot, 1)
    with_slice(mine, lambda start, size: cot_own(size).start())
    for load in loads:
        load.wait()
    each(chunks, rows.last)

    def body(p):
        forward(p)
        hids.step(0, p)

    each(PAIRS, body)
    with_slice(mine, deal_got)
    with_slice(mine, cot_got)

    def body(p):
        dhid_partial(p)
        dhids.step(0, p)
        hids.step(1, p)

    each(PAIRS, body)

    def body(p):
        hids.step(2, p)
        dhids.step(1, p)

    each(PAIRS, body)

    def body(p):
        hids.step(3, p)
        dhids.step(2, p)

    each(PAIRS, body)
    each(PAIRS, lambda p: dhids.step(3, p))

    each(PAIRS, hids.last)
    each(PAIRS, forward_out)

    def body(start, size):
        each(GROUP, lambda j: slice_copy(j, size).start(), 1)

    with_slice(mine, body)
    slice_got[mine] = slice_part[y]

    backward((y // 2 + PAIRS // 2) % PAIRS)
    each(chunks, lambda c: grads_x.step(0, c))
    backward((y // 2 + PAIRS // 2 + 3 - 2 * (y % 2)) % PAIRS)
    backward((y // 2 + PAIRS // 2 + 1 + 2 * (y % 2)) % PAIRS)
    backward(y // 2)
    slot_step(0)
    each(chunks, lambda c: grads_x.step(1, c))
    slot_step(1)
    each(chunks, straight_mine)
    for r in range(GROUP):
        home_a(r)
    each(chunks, lambda c: grads_x.step(2, c))
    slot_step(2)
    for r in range(GROUP):
        finish_a(r)
    each(chunks, lambda c: grads_x.step(3, c, straight_last))
    slot_step(3)

    for ab in (0, 1):
        pipe_copy(ab).wait_send()
        for j in range(1, experts):
            spread_copy(ab, j).wait_send()
    each(GROUP, deal_sent, 1)
    each(GROUP, cot_sent, 1)
    each(chunks, rows.sent)
    each(PAIRS, dhids.sent)
    each(PAIRS, hids.sent)

    def body(start, size):
        each(GROUP, lambda j: slice_copy(j, size).wait_send(), 1)

    with_slice(mine, body)

    slot_last()

    for r in range(GROUP):
        for j in range(1, experts):
            home_a_copy(r, j).wait_send()
        save_a(r).wait()
    each(chunks, lambda c: grads_x.sent(c, HOPS - 1))
    slot_finish()

    def body(c):
        straight_finish(c)
        straight_sent(c)

    each(chunks, body)
    for d, sign in WAYS:
        for t in range(d, HOPS):
            slot_copy(d, t, sign).wait_send()
    for j in range(1, experts):
        last_copy(j).wait_send()
    each(chunks, lambda c: save_b(c).wait())


def on_device(
    section_acts,
    fwd_routes,
    fwd_gates,
    section_grads,
    bwd_routes,
    bwd_gates,
    saved_proj,
    w_gate,
    w_up,
    w_down,
):
    experts = lax.axis_size("expert") // GROUP
    _, tokens, model = section_acts.shape
    cap, hidden = saved_proj.shape[3], w_gate.shape[3]
    width = model // CHUNKS
    sources = saved_proj.shape[1]
    spread = experts * cap
    lanes = 2 * spread
    wide = slices_of(model)[0][0][1]
    whole = (tokens, model)
    by_slice = (experts, GROUP, cap, wide)
    by_chunk = (experts, CHUNKS, cap, width)
    blocks = (CHUNKS, experts, cap, width)
    hids = (PAIRS, 2, spread, hidden)
    dma = pltpu.SemaphoreType.DMA
    hbm = pl.BlockSpec(memory_space=pl.ANY)
    vmem = pl.BlockSpec(memory_space=pltpu.VMEM)

    def as_row(array):
        return array.reshape(1, tokens)

    def two(*shape):
        return [dma(shape), dma(shape)]

    shapes = [
        whole,
        whole,
        by_chunk,
        by_slice,
        (GROUP,) + blocks,
        by_slice,
        (GROUP, experts, cap, wide),
        (GROUP, hidden, wide),
        (GROUP,) + hids,
        (2, HOPS) + hids,
        (GROUP,) + hids,
        (GROUP, experts, cap, wide),
        (GROUP, experts, cap, wide),
        (GROUP,) + blocks,
        (2, HOPS) + blocks,
        (GROUP, experts, cap, wide),
        (CHUNKS, 3, experts, cap, width),
        whole,
        whole,
        (model, 2 * hidden),
        (sources, cap, 2 * hidden),
    ]
    slots = [(PAIRS, 8, lanes), (2, HOPS, 8, lanes), (2, HOPS, 8, lanes), (8, lanes)]
    slots.append((experts, 8, lanes))

    out_a, out_b, out_g = pl.pallas_call(
        kernel,
        out_shape=(
            jax.ShapeDtypeStruct(section_acts.shape, bf16),
            jax.ShapeDtypeStruct(section_grads.shape, bf16),
            jax.ShapeDtypeStruct((1, tokens), f32),
        ),
        in_specs=[hbm, hbm, vmem, vmem, vmem, vmem, hbm, hbm, hbm, hbm],
        out_specs=(hbm, hbm, vmem),
        scratch_shapes=[pltpu.VMEM(shape, bf16) for shape in shapes]
        + [pltpu.VMEM(shape, f32) for shape in slots]
        + [dma((3,)), dma((GROUP,)), dma((CHUNKS,))]
        + two(2)
        + two(2, experts - 1)
        + two(GROUP)
        + two(GROUP)
        + two(2, HOPS * CHUNKS)
        + two(2, HOPS * PAIRS)
        + two(2, HOPS * PAIRS)
        + two(GROUP)
        + two(GROUP, experts - 1)
        + two(2, HOPS * CHUNKS)
        + [dma((CHUNKS, 3, experts)), dma((CHUNKS,))]
        + two(2, HOPS)
        + two(experts - 1),
        compiler_params=pltpu.CompilerParams(
            collective_id=0, has_side_effects=True, vmem_limit_bytes=56 * 2**20
        ),
        cost_estimate=pl.CostEstimate(
            flops=2 * 2 * GROUP * spread * model * 3 * hidden,
            bytes_accessed=2 * 3 * model * hidden + 8 * tokens * model,
            transcendentals=2 * GROUP * spread * hidden,
        ),
        name="relay_experts",
    )(
        section_acts,
        section_grads,
        as_row(fwd_routes),
        as_row(fwd_gates),
        as_row(bwd_routes),
        as_row(bwd_gates),
        saved_proj,
        w_gate,
        w_up,
        w_down,
    )
    return out_a, out_b, out_g.reshape(1, tokens, 1)


def solution(mesh):
    tokens = P("pipe", "expert", None)
    weights = P("pipe", "expert", None, None)
    placed = (tokens,) * 6 + (P("pipe", None, "expert", None, None),) + (weights,) * 3
    return jax.shard_map(
        on_device, mesh=mesh, in_specs=placed, out_specs=(tokens,) * 3, check_vma=False
    )
```

```python
import functools

import jax
import jax.numpy as jnp
from jax import lax
from jax.experimental import pallas as pl
from jax.experimental.pallas import tpu as pltpu
from jax.sharding import PartitionSpec as P

GROUP = 8
CHUNKS = 4
PAIRS = GROUP // 2
LANES = 128
HOPS = 4
MESH = pl.DeviceIdType.MESH
WAYS = ((0, 1), (1, -1))
f32 = jnp.float32
bf16 = jnp.bfloat16


def nt_dot(a, b):
    return lax.dot_general(a, b, (((1,), (1,)), ((), ())), preferred_element_type=f32)


def column_of(row):
    count = row.shape[1]
    shape = (count, count)
    eye = lax.broadcasted_iota(jnp.int32, shape, 0) == lax.broadcasted_iota(jnp.int32, shape, 1)
    return jnp.sum(jnp.where(eye, jnp.broadcast_to(row, shape), 0.0), axis=1, keepdims=True)


def row_of(column):
    count = column.shape[0]
    shape = (count, count)
    eye = lax.broadcasted_iota(jnp.int32, shape, 0) == lax.broadcasted_iota(jnp.int32, shape, 1)
    return jnp.sum(jnp.where(eye, jnp.broadcast_to(column, shape), 0.0), axis=0, keepdims=True)


def place_matrices(route_row, experts, cap):
    tokens = route_row.shape[1]
    slots = experts * cap
    routes = route_row.astype(f32)
    column = column_of(routes)
    at = lax.broadcasted_iota(jnp.int32, (tokens, tokens), 0)
    other = lax.broadcasted_iota(jnp.int32, (tokens, tokens), 1)
    slot = lax.broadcasted_iota(jnp.int32, (slots, tokens), 0)
    named = jnp.broadcast_to(routes, (slots, tokens)) == (slot // cap).astype(f32)
    before = jnp.dot(
        jnp.where(named, 1.0, 0.0).astype(bf16),
        jnp.where(at < other, 1.0, 0.0).astype(bf16),
        preferred_element_type=f32,
    )
    pack = jnp.where(named & (before == (slot % cap).astype(f32)), 1.0, 0.0).astype(bf16)
    slot = lax.broadcasted_iota(jnp.int32, (tokens, slots), 1)
    named = jnp.broadcast_to(column, (tokens, slots)) == (slot // cap).astype(f32)
    before = jnp.dot(
        jnp.where(other < at, 1.0, 0.0).astype(bf16),
        jnp.where(named, 1.0, 0.0).astype(bf16),
        preferred_element_type=f32,
    )
    unpack = jnp.where(named & (before == (slot % cap).astype(f32)), 1.0, 0.0).astype(bf16)
    return pack, unpack


def slices_of(model):
    tiles = model // LANES
    wide, slim = -(-tiles // GROUP) * LANES, tiles // GROUP * LANES
    many = tiles % GROUP
    starts = [min(r, many) * wide + max(r - many, 0) * slim for r in range(GROUP)]
    return [(start, wide if r < many else slim) for r, start in enumerate(starts)], many


def kernel(
    acts,
    grads,
    routes_a,
    gates_a,
    routes_b,
    gates_b,
    kept,
    w_gate,
    w_up,
    w_down,
    out_a,
    out_b,
    out_g,
    in_a,
    in_b,
    packed_a,
    packed_b,
    rows_a,
    local_b,
    cot_b,
    held,
    dhid_part,
    dhid_sums,
    hid_all,
    slice_part,
    slice_got,
    part_b,
    sums_b,
    back_a,
    straight,
    whole_a,
    whole_b,
    both_w,
    saved,
    slot_own,
    slot_sent,
    slot_got,
    slot_fold,
    slot_back,
    load_sem,
    save_a_sem,
    save_b_sem,
    pipe_send,
    pipe_recv,
    spread_send,
    spread_recv,
    deal_send,
    deal_recv,
    cot_send,
    cot_recv,
    rows_send,
    rows_recv,
    dhid_send,
    dhid_recv,
    hid_send,
    hid_recv,
    slice_send,
    slice_recv,
    home_a_send,
    home_a_recv,
    fold_send,
    fold_recv,
    straight_send,
    straight_recv,
    slot_send,
    slot_recv,
    last_send,
    last_recv,
):
    stage = lax.axis_index("pipe")
    stages = lax.axis_size("pipe")
    index = lax.axis_index("expert")
    x = index // GROUP
    y = index % GROUP
    experts, chunks, cap, width = packed_a.shape
    model, hidden = both_w.shape[0], both_w.shape[1] // 2
    spread = experts * cap
    slices, many = slices_of(model)
    wide, slim = slices[0][1], slices[-1][1]
    shift = stage % 2 * many

    def slice_at(yy):
        return (yy + shift) % GROUP

    mine = slice_at(y)

    def with_slice(r, act):
        @pl.when(r < many)
        def _():
            act(pl.multiple_of(r * wide, LANES), wide)

        @pl.when(r >= many)
        def _():
            act(pl.multiple_of(many * wide + (r - many) * slim, LANES), slim)

    def column(xx):
        return {"expert": xx * GROUP + y}

    def beside(j, by):
        return {"expert": (x + j) % experts * GROUP + (y + GROUP + by) % GROUP}

    def ring(by):
        return {"expert": x * GROUP + (y + GROUP + by) % GROUP}

    def along(by):
        return {"pipe": (stage + stages + by) % stages}

    def remote(src, dst, send, recv, device):
        return pltpu.make_async_remote_copy(
            src_ref=src,
            dst_ref=dst,
            send_sem=send,
            recv_sem=recv,
            device_id=device,
            device_id_type=MESH,
        )

    def each(count, body, first=0):
        lax.fori_loop(first, count, lambda c, carry: (body(c), carry)[1], 0)

    def columns(c):
        return pl.ds(c * width if isinstance(c, int) else pl.multiple_of(c * width, LANES), width)

    barrier = pltpu.get_barrier_semaphore()
    partners = [along(1), along(-1)] + [ring(j) for j in range(1, GROUP)]
    partners += [column((x + j) % experts) for j in range(1, experts)]
    partners += [beside(j, sign) for j in range(1, experts) for _, sign in WAYS]
    for partner in partners:
        pl.semaphore_signal(barrier, inc=1, device_id=partner, device_id_type=MESH)
    pl.semaphore_wait(barrier, len(partners))

    def pipe_copy(ab):
        source, target = ((acts, in_a), (grads, in_b))[ab]
        return remote(
            source.at[0], target, pipe_send.at[ab], pipe_recv.at[ab], along(1 - 2 * ab)
        )

    for ab in (0, 1):
        pipe_copy(ab).start()

    def deal_copy(j, start, size):
        return remote(
            w_down.at[0, 0, :, pl.ds(start, size)],
            held.at[y, :, pl.ds(0, size)],
            deal_send.at[j],
            deal_recv.at[j],
            ring(j),
        )

    def deal_own(start, size):
        return pltpu.make_async_copy(
            w_down.at[0, 0, :, pl.ds(start, size)], held.at[y, :, pl.ds(0, size)], deal_send.at[0]
        )

    def deal(j):
        with_slice(slice_at(y + j), lambda start, size: deal_copy(j, start, size).start())

    def deal_sent(j):
        with_slice(slice_at(y + j), lambda start, size: deal_copy(j, start, size).wait_send())

    def deal_got(start, size):
        def body(j):
            got = held.at[(y + GROUP - j) % GROUP, :, pl.ds(0, size)]
            remote(got, got, deal_send.at[j], deal_recv.at[j], ring(j)).wait_recv()

        deal_own(start, size).wait()
        each(GROUP, body, 1)

    each(GROUP, deal, 1)
    with_slice(mine, lambda start, size: deal_own(start, size).start())
    loads = [
        pltpu.make_async_copy(w_gate.at[0, 0], both_w.at[:, pl.ds(0, hidden)], load_sem.at[0]),
        pltpu.make_async_copy(w_up.at[0, 0], both_w.at[:, pl.ds(hidden, hidden)], load_sem.at[1]),
        pltpu.make_async_copy(kept.at[0, :, 0], saved, load_sem.at[2]),
    ]
    for load in loads:
        load.start()

    @pl.when(mine >= many)
    def _():
        held[:, :, slim:] = jnp.zeros((GROUP, hidden, wide - slim), bf16)
        cot_b[:, :, :, slim:] = jnp.zeros((GROUP, experts, cap, wide - slim), bf16)

    pack_a, unpack_a = place_matrices(routes_a[...], experts, cap)
    pack_b, unpack_b = place_matrices(routes_b[...], experts, cap)
    gate_a = column_of(gates_a[...])
    gate_b = column_of(gates_b[...].astype(bf16).astype(f32))

    def spread_copy(ab, j):
        to = (x + j) % experts
        return remote(
            (packed_a, packed_b)[ab].at[to],
            (rows_a.at[y, :, x], local_b.at[x])[ab],
            spread_send.at[ab, j - 1],
            spread_recv.at[ab, j - 1],
            column(to),
        )

    def spread_wait(ab):
        for j in range(1, experts):
            sender = (x + experts - j) % experts
            got = (rows_a.at[y, :, sender], local_b.at[sender])[ab]
            remote(
                got, got, spread_send.at[ab, j - 1], spread_recv.at[ab, j - 1], column(x)
            ).wait_recv()

    def packed_rows(pack, source, start, size):
        chosen = jnp.dot(pack, source[:, start : start + size], preferred_element_type=f32)
        return chosen.astype(bf16).reshape(experts, cap, size)

    pipe_copy(0).wait_recv()
    for c in range(chunks):
        packed_a[:, c] = packed_rows(pack_a, in_a, c * width, width)
    for j in range(1, experts):
        spread_copy(0, j).start()
    rows_a[y, :, x] = packed_a[x]
    pipe_copy(1).wait_recv()
    packed_b[:, many:, :, slim:] = jnp.zeros((experts, GROUP - many, cap, wide - slim), bf16)
    for r, (start, size) in enumerate(slices):
        packed_b[:, r, :, :size] = packed_rows(pack_b, in_b, start, size)
    for j in range(1, experts):
        spread_copy(1, j).start()
    local_b[x] = packed_b[x]

    def cot_copy(j, size):
        return remote(
            local_b.at[:, slice_at(y + j), :, pl.ds(0, size)],
            cot_b.at[y, :, :, pl.ds(0, size)],
            cot_send.at[j],
            cot_recv.at[j],
            ring(j),
        )

    def cot_own(size):
        return pltpu.make_async_copy(
            local_b.at[:, mine, :, pl.ds(0, size)],
            cot_b.at[y, :, :, pl.ds(0, size)],
            cot_send.at[0],
        )

    def cot_got(start, size):
        def body(j):
            got = cot_b.at[(y + GROUP - j) % GROUP, :, :, pl.ds(0, size)]
            remote(got, got, cot_send.at[j], cot_recv.at[j], ring(j)).wait_recv()

        cot_own(size).wait()
        each(GROUP, body, 1)

    def cot(j):
        with_slice(slice_at(y + j), lambda start, size: cot_copy(j, size).start())

    def cot_sent(j):
        with_slice(slice_at(y + j), lambda start, size: cot_copy(j, size).wait_send())

    def halves(ref, d, t, far):
        half = ref.shape[0] // 2
        return ref.at[pl.ds(d * half, half)] if t == far else ref

    class Gather:
        def __init__(self, blocks, send, recv):
            self.blocks, self.send, self.recv = blocks, send, recv
            self.count = blocks.shape[1]

        def copy(self, t, c, d, sign, on=0):
            at = self.blocks.at[(y + GROUP - sign * (t + on)) % GROUP, c]
            at = halves(at, d, t, HOPS - 1)
            k = t * self.count + c
            return remote(at, at, self.send.at[d, k], self.recv.at[d, k], ring(sign))

        def step(self, t, c):
            for d, sign in WAYS:
                if t:
                    self.copy(t - 1, c, d, sign, 1).wait_recv()
                self.copy(t, c, d, sign).start()

        def last(self, c):
            for d, sign in WAYS:
                self.copy(HOPS - 1, c, d, sign, 1).wait_recv()

        def sent(self, c):
            for t in range(HOPS):
                for d, sign in WAYS:
                    self.copy(t, c, d, sign).wait_send()

    class Fold:
        def __init__(self, part, sums, send, recv):
            self.part, self.sums, self.send, self.recv = part, sums, send, recv
            self.count = part.shape[1]

        def copy(self, t, c, d, sign):
            at = self.part.at[(y + GROUP + sign * (HOPS - t)) % GROUP, c]
            k = t * self.count + c
            return remote(
                halves(at, d, t, 0),
                halves(self.sums.at[d, t, c], d, t, 0),
                self.send.at[d, k],
                self.recv.at[d, k],
                ring(sign),
            )

        def step(self, t, c, straight=None):
            half = self.part.shape[2] // 2
            for d, sign in WAYS:
                block = (y + GROUP + sign * (HOPS - t)) % GROUP
                if t:
                    self.copy(t - 1, c, d, sign).wait_recv()
                    at = pl.ds(d * half, half) if t == 1 else pl.ds(0, 2 * half)
                    self.part[block, c, at] = (
                        self.part[block, c, at].astype(f32)
                        + self.sums[d, t - 1, c, at].astype(f32)
                    ).astype(bf16)
                if straight is None:
                    self.copy(t, c, d, sign).start()
                else:
                    straight(c, d, sign, block)

        def total(self, c):
            for d, sign in WAYS:
                self.copy(HOPS - 1, c, d, sign).wait_recv()
            return (
                self.part[y, c].astype(f32)
                + self.sums[0, HOPS - 1, c].astype(f32)
                + self.sums[1, HOPS - 1, c].astype(f32)
            )

        def sent(self, c, hops=HOPS):
            for t in range(hops):
                for d, sign in WAYS:
                    self.copy(t, c, d, sign).wait_send()

    rows = Gather(rows_a, rows_send, rows_recv)
    hids = Gather(hid_all, hid_send, hid_recv)
    dhids = Fold(dhid_part, dhid_sums, dhid_send, dhid_recv)
    grads_x = Fold(part_b, sums_b, fold_send, fold_recv)

    def dhid_partial(p):
        here = cot_b[pl.ds(2 * p, 2)].reshape(2 * spread, wide)
        dhid = nt_dot(here, held[...].reshape(GROUP * hidden, wide)).astype(bf16)
        for g in range(GROUP):
            dhid_part[g, p] = dhid[:, g * hidden : (g + 1) * hidden].reshape(2, spread, hidden)

    def forward(p):
        pre = jnp.zeros((2 * spread, 2 * hidden), f32)
        for c in range(chunks):
            pre += jnp.dot(
                rows_a[pl.ds(2 * p, 2), c].reshape(2 * spread, width),
                both_w[pl.ds(c * width, width), :],
                preferred_element_type=f32,
            )
        pre_g, pre_u = pre[:, :hidden], pre[:, hidden:]
        hid = (pre_g * jax.nn.sigmoid(pre_g) * pre_u).astype(bf16)
        hid_all[y, p] = hid.reshape(2, spread, hidden)

    def forward_out(p):
        hid = jnp.concatenate(
            [hid_all[g, p].reshape(2 * spread, hidden) for g in range(GROUP)], axis=1
        )
        done = jnp.dot(
            hid, held[...].reshape(GROUP * hidden, wide), preferred_element_type=f32
        )
        slice_part[pl.ds(2 * p, 2)] = done.astype(bf16).reshape(2, experts, cap, wide)

    def backward(p):
        dhid = dhids.total(p).reshape(2 * spread, hidden)
        both = jnp.concatenate(
            [saved[j * GROUP + 2 * p + i] for i in (0, 1) for j in range(experts)], axis=0
        ).astype(f32)
        sg, su = both[:, :hidden], both[:, hidden:]
        sig = jax.nn.sigmoid(sg)
        act = sg * sig
        hid = (act * su).astype(bf16).astype(f32)
        slot_row = jnp.sum((hid * dhid).T, axis=0, keepdims=True)
        slot_own[p] = jnp.broadcast_to(slot_row, slot_own.shape[1:])
        d_g = (dhid * su * sig * (1.0 + sg * (1.0 - sig))).astype(bf16)
        d_u = (dhid * act).astype(bf16)
        d_both = jnp.concatenate([d_g, d_u], axis=1)
        for c in range(chunks):
            part_b[pl.ds(2 * p, 2), c] = (
                nt_dot(d_both, both_w[pl.ds(c * width, width), :])
                .astype(bf16)
                .reshape(2, experts, cap, width)
            )

    def slice_copy(j, size):
        return remote(
            slice_part.at[(y + j) % GROUP, :, :, pl.ds(0, size)],
            slice_got.at[mine, :, :, pl.ds(0, size)],
            slice_send.at[j],
            slice_recv.at[j],
            ring(j),
        )

    def home_a_copy(r, j):
        to = (x + j) % experts
        at = pl.ds(0, slices[r][1])
        return remote(
            slice_got.at[r, to, :, at],
            back_a.at[r, x, :, at],
            home_a_send.at[r, j - 1],
            home_a_recv.at[r, j - 1],
            column(to),
        )

    def home_a(r):
        off = (y + GROUP - (r + GROUP - shift) % GROUP) % GROUP

        @pl.when(off != 0)
        def _():
            got = slice_got.at[r, :, :, pl.ds(0, slices[r][1])]
            remote(got, got, slice_send.at[off], slice_recv.at[off], ring(1)).wait_recv()

        for j in range(1, experts):
            home_a_copy(r, j).start()
        back_a[r, x] = slice_got[r, x]

    def save_a(r):
        at = pl.ds(*slices[r])
        return pltpu.make_async_copy(whole_a.at[:, at], out_a.at[0, :, at], save_a_sem.at[r])

    def finish_a(r):
        start, size = slices[r]
        for j in range(1, experts):
            got = back_a.at[r, (x + experts - j) % experts, :, pl.ds(0, size)]
            remote(
                got, got, home_a_send.at[r, j - 1], home_a_recv.at[r, j - 1], column(x)
            ).wait_recv()
        picked = jnp.dot(
            unpack_a, back_a[r, :, :, :size].reshape(spread, size), preferred_element_type=f32
        )
        at = slice(start, start + size)
        whole_a[:, at] = (in_a[:, at].astype(f32) + gate_a * picked).astype(bf16)
        save_a(r).start()

    def save_b(c):
        return pltpu.make_async_copy(
            whole_b.at[:, columns(c)], out_b.at[0, :, columns(c)], save_b_sem.at[c]
        )

    def straight_copy(c, d, j, sign, block):
        return remote(
            part_b.at[block, c, (x + j) % experts],
            straight.at[c, d, x],
            straight_send.at[c, d, j],
            straight_recv.at[c],
            beside(j, sign),
        )

    def straight_own(c):
        return pltpu.make_async_copy(
            part_b.at[y, c, x], straight.at[c, 2, x], straight_recv.at[c]
        )

    def straight_mine(c):
        straight_own(c).start()
        for j in range(1, experts):
            straight_copy(c, 2, j, 0, y).start()

    def straight_last(c, d, sign, block):
        for j in range(experts):
            straight_copy(c, d, j, sign, block).start()

    def straight_sent(c):
        for d, sign in WAYS:
            block = (y + GROUP + sign) % GROUP
            for j in range(experts):
                straight_copy(c, d, j, sign, block).wait_send()
        for j in range(1, experts):
            straight_copy(c, 2, j, 0, y).wait_send()

    def straight_finish(c):
        got = straight.at[c]
        remote(
            got, got, straight_send.at[c, 0, 0], straight_recv.at[c], column(x)
        ).wait_recv()
        picked = jnp.zeros((spread, width), f32)
        for d in range(3):
            rows_d = straight[c, d].reshape(spread, width)
            picked += jnp.dot(unpack_b, rows_d, preferred_element_type=f32)
        whole_b[:, columns(c)] = (in_b[:, columns(c)].astype(f32) + gate_b * picked).astype(bf16)
        save_b(c).start()

    def slot_copy(d, t, sign):
        return remote(
            slot_sent.at[d, t],
            slot_got.at[d, t],
            slot_send.at[d, t],
            slot_recv.at[d, t],
            ring(sign),
        )

    def slot_step(t):
        for d, sign in WAYS:
            if t < d:
                continue
            pair = ((y + GROUP + sign * (HOPS - t)) % GROUP) // 2
            if t > d:
                slot_copy(d, t - 1, sign).wait_recv()
                slot_sent[d, t] = slot_own[pair] + slot_got[d, t - 1]
            else:
                slot_sent[d, t] = slot_own[pair]
            slot_copy(d, t, sign).start()

    def last_copy(j):
        return remote(
            slot_fold,
            slot_back.at[x],
            last_send.at[j - 1],
            last_recv.at[j - 1],
            column((x + j) % experts),
        )

    def slot_last():
        for d, sign in WAYS:
            slot_copy(d, HOPS - 1, sign).wait_recv()
        slot_fold[...] = slot_own[y // 2] + slot_got[0, HOPS - 1] + slot_got[1, HOPS - 1]
        for j in range(1, experts):
            last_copy(j).start()
        slot_back[x] = slot_fold[...]

    def slot_finish():
        for j in range(1, experts):
            got = slot_back.at[(x + experts - j) % experts]
            remote(
                got, got, last_send.at[j - 1], last_recv.at[j - 1], column(x)
            ).wait_recv()
        tokens = routes_b.shape[1]
        lanes = slot_back.shape[2]
        routes = column_of(routes_b[...].astype(f32))
        lane = lax.broadcasted_iota(jnp.int32, (tokens, spread), 1)
        taken = jnp.where(unpack_b > 0, (lane % cap).astype(f32), 0.0)
        slot = jnp.sum(taken, axis=1, keepdims=True)
        lane = lax.broadcasted_iota(jnp.int32, (tokens, lanes), 1)
        first = (y % 2) * spread + x * cap
        here = jnp.broadcast_to(slot, (tokens, lanes)) == (lane - first).astype(f32)
        total = jnp.zeros((tokens, lanes), f32)
        for e in range(experts):
            values = jnp.broadcast_to(slot_back[e][0:1], (tokens, lanes))
            total += jnp.where(here & (routes == float(e)), values, 0.0)
        out_g[...] = row_of(jnp.sum(total, axis=1, keepdims=True))

    spread_wait(0)
    for t in range(HOPS):
        each(chunks, functools.partial(rows.step, t))
    spread_wait(1)
    each(GROUP, cot, 1)
    with_slice(mine, lambda start, size: cot_own(size).start())
    for load in loads:
        load.wait()
    each(chunks, rows.last)

    def body(p):
        forward(p)
        hids.step(0, p)

    each(PAIRS, body)
    with_slice(mine, deal_got)
    with_slice(mine, cot_got)

    def body(p):
        dhid_partial(p)
        dhids.step(0, p)
        hids.step(1, p)

    each(PAIRS, body)

    def body(p):
        hids.step(2, p)
        dhids.step(1, p)

    each(PAIRS, body)

    def body(p):
        hids.step(3, p)
        dhids.step(2, p)

    each(PAIRS, body)

    def body(p):
        dhids.step(3, p)
        hids.last(p)
        forward_out(p)
        for i in (0, 1):
            j = (2 * p + i + GROUP - y) % GROUP
            pl.when(j != 0)(
                lambda: with_slice(mine, lambda start, size: slice_copy(j, size).start())
            )

    each(PAIRS, body)
    slice_got[mine] = slice_part[y]

    backward((y // 2 + PAIRS // 2) % PAIRS)
    each(chunks, lambda c: grads_x.step(0, c))
    backward((y // 2 + PAIRS // 2 + 3 - 2 * (y % 2)) % PAIRS)
    backward((y // 2 + PAIRS // 2 + 1 + 2 * (y % 2)) % PAIRS)
    backward(y // 2)
    slot_step(0)
    each(chunks, straight_mine)
    each(chunks, lambda c: grads_x.step(1, c))
    slot_step(1)
    for r in range(GROUP):
        home_a(r)
    each(chunks, lambda c: grads_x.step(2, c))
    slot_step(2)
    each(chunks, lambda c: grads_x.step(3, c, straight_last))
    slot_step(3)
    for r in range(GROUP):
        finish_a(r)

    for ab in (0, 1):
        pipe_copy(ab).wait_send()
        for j in range(1, experts):
            spread_copy(ab, j).wait_send()
    each(GROUP, deal_sent, 1)
    each(GROUP, cot_sent, 1)
    each(chunks, rows.sent)
    each(PAIRS, dhids.sent)
    each(PAIRS, hids.sent)

    def body(start, size):
        each(GROUP, lambda j: slice_copy(j, size).wait_send(), 1)

    with_slice(mine, body)

    slot_last()

    for r in range(GROUP):
        for j in range(1, experts):
            home_a_copy(r, j).wait_send()
        save_a(r).wait()
    each(chunks, lambda c: grads_x.sent(c, HOPS - 1))
    slot_finish()

    def body(c):
        straight_finish(c)
        straight_sent(c)

    each(chunks, body)
    for d, sign in WAYS:
        for t in range(d, HOPS):
            slot_copy(d, t, sign).wait_send()
    for j in range(1, experts):
        last_copy(j).wait_send()
    each(chunks, lambda c: save_b(c).wait())


def on_device(
    section_acts,
    fwd_routes,
    fwd_gates,
    section_grads,
    bwd_routes,
    bwd_gates,
    saved_proj,
    w_gate,
    w_up,
    w_down,
):
    experts = lax.axis_size("expert") // GROUP
    _, tokens, model = section_acts.shape
    cap, hidden = saved_proj.shape[3], w_gate.shape[3]
    width = model // CHUNKS
    sources = saved_proj.shape[1]
    spread = experts * cap
    lanes = 2 * spread
    wide = slices_of(model)[0][0][1]
    whole = (tokens, model)
    by_slice = (experts, GROUP, cap, wide)
    by_chunk = (experts, CHUNKS, cap, width)
    blocks = (CHUNKS, experts, cap, width)
    hids = (PAIRS, 2, spread, hidden)
    dma = pltpu.SemaphoreType.DMA
    hbm = pl.BlockSpec(memory_space=pl.ANY)
    vmem = pl.BlockSpec(memory_space=pltpu.VMEM)

    def as_row(array):
        return array.reshape(1, tokens)

    def two(*shape):
        return [dma(shape), dma(shape)]

    shapes = [
        whole,
        whole,
        by_chunk,
        by_slice,
        (GROUP,) + blocks,
        by_slice,
        (GROUP, experts, cap, wide),
        (GROUP, hidden, wide),
        (GROUP,) + hids,
        (2, HOPS) + hids,
        (GROUP,) + hids,
        (GROUP, experts, cap, wide),
        (GROUP, experts, cap, wide),
        (GROUP,) + blocks,
        (2, HOPS) + blocks,
        (GROUP, experts, cap, wide),
        (CHUNKS, 3, experts, cap, width),
        whole,
        whole,
        (model, 2 * hidden),
        (sources, cap, 2 * hidden),
    ]
    slots = [(PAIRS, 8, lanes), (2, HOPS, 8, lanes), (2, HOPS, 8, lanes), (8, lanes)]
    slots.append((experts, 8, lanes))

    out_a, out_b, out_g = pl.pallas_call(
        kernel,
        out_shape=(
            jax.ShapeDtypeStruct(section_acts.shape, bf16),
            jax.ShapeDtypeStruct(section_grads.shape, bf16),
            jax.ShapeDtypeStruct((1, tokens), f32),
        ),
        in_specs=[hbm, hbm, vmem, vmem, vmem, vmem, hbm, hbm, hbm, hbm],
        out_specs=(hbm, hbm, vmem),
        scratch_shapes=[pltpu.VMEM(shape, bf16) for shape in shapes]
        + [pltpu.VMEM(shape, f32) for shape in slots]
        + [dma((3,)), dma((GROUP,)), dma((CHUNKS,))]
        + two(2)
        + two(2, experts - 1)
        + two(GROUP)
        + two(GROUP)
        + two(2, HOPS * CHUNKS)
        + two(2, HOPS * PAIRS)
        + two(2, HOPS * PAIRS)
        + two(GROUP)
        + two(GROUP, experts - 1)
        + two(2, HOPS * CHUNKS)
        + [dma((CHUNKS, 3, experts)), dma((CHUNKS,))]
        + two(2, HOPS)
        + two(experts - 1),
        compiler_params=pltpu.CompilerParams(
            collective_id=0, has_side_effects=True, vmem_limit_bytes=56 * 2**20
        ),
        cost_estimate=pl.CostEstimate(
            flops=2 * 2 * GROUP * spread * model * 3 * hidden,
            bytes_accessed=2 * 3 * model * hidden + 8 * tokens * model,
            transcendentals=2 * GROUP * spread * hidden,
        ),
        name="relay_experts",
    )(
        section_acts,
        section_grads,
        as_row(fwd_routes),
        as_row(fwd_gates),
        as_row(bwd_routes),
        as_row(bwd_gates),
        saved_proj,
        w_gate,
        w_up,
        w_down,
    )
    return out_a, out_b, out_g.reshape(1, tokens, 1)


def solution(mesh):
    tokens = P("pipe", "expert", None)
    weights = P("pipe", "expert", None, None)
    placed = (tokens,) * 6 + (P("pipe", None, "expert", None, None),) + (weights,) * 3
    return jax.shard_map(
        on_device, mesh=mesh, in_specs=placed, out_specs=(tokens,) * 3, check_vma=False
    )
```

```python
import functools

import jax
import jax.numpy as jnp
from jax import lax
from jax.experimental import pallas as pl
from jax.experimental.pallas import tpu as pltpu
from jax.sharding import PartitionSpec as P

GROUP = 8
CHUNKS = 4
PAIRS = GROUP // 2
LANES = 128
HOPS = 4
MESH = pl.DeviceIdType.MESH
WAYS = ((0, 1), (1, -1))
f32 = jnp.float32
bf16 = jnp.bfloat16


def nt_dot(a, b):
    return lax.dot_general(a, b, (((1,), (1,)), ((), ())), preferred_element_type=f32)


def column_of(row):
    count = row.shape[1]
    shape = (count, count)
    eye = lax.broadcasted_iota(jnp.int32, shape, 0) == lax.broadcasted_iota(jnp.int32, shape, 1)
    return jnp.sum(jnp.where(eye, jnp.broadcast_to(row, shape), 0.0), axis=1, keepdims=True)


def row_of(column):
    count = column.shape[0]
    shape = (count, count)
    eye = lax.broadcasted_iota(jnp.int32, shape, 0) == lax.broadcasted_iota(jnp.int32, shape, 1)
    return jnp.sum(jnp.where(eye, jnp.broadcast_to(column, shape), 0.0), axis=0, keepdims=True)


def place_matrices(route_row, experts, cap):
    tokens = route_row.shape[1]
    slots = experts * cap
    routes = route_row.astype(f32)
    column = column_of(routes)
    at = lax.broadcasted_iota(jnp.int32, (tokens, tokens), 0)
    other = lax.broadcasted_iota(jnp.int32, (tokens, tokens), 1)
    slot = lax.broadcasted_iota(jnp.int32, (slots, tokens), 0)
    named = jnp.broadcast_to(routes, (slots, tokens)) == (slot // cap).astype(f32)
    before = jnp.dot(
        jnp.where(named, 1.0, 0.0).astype(bf16),
        jnp.where(at < other, 1.0, 0.0).astype(bf16),
        preferred_element_type=f32,
    )
    pack = jnp.where(named & (before == (slot % cap).astype(f32)), 1.0, 0.0).astype(bf16)
    slot = lax.broadcasted_iota(jnp.int32, (tokens, slots), 1)
    named = jnp.broadcast_to(column, (tokens, slots)) == (slot // cap).astype(f32)
    before = jnp.dot(
        jnp.where(other < at, 1.0, 0.0).astype(bf16),
        jnp.where(named, 1.0, 0.0).astype(bf16),
        preferred_element_type=f32,
    )
    unpack = jnp.where(named & (before == (slot % cap).astype(f32)), 1.0, 0.0).astype(bf16)
    return pack, unpack


def slices_of(model):
    tiles = model // LANES
    wide, slim = -(-tiles // GROUP) * LANES, tiles // GROUP * LANES
    many = tiles % GROUP
    starts = [min(r, many) * wide + max(r - many, 0) * slim for r in range(GROUP)]
    return [(start, wide if r < many else slim) for r, start in enumerate(starts)], many


def kernel(
    acts,
    grads,
    routes_a,
    gates_a,
    routes_b,
    gates_b,
    kept,
    w_gate,
    w_up,
    w_down,
    out_a,
    out_b,
    out_g,
    in_a,
    in_b,
    packed_a,
    packed_b,
    rows_a,
    local_b,
    cot_b,
    held,
    dhid_part,
    dhid_sums,
    hid_all,
    slice_part,
    slice_got,
    part_b,
    sums_b,
    back_a,
    straight,
    both_w,
    saved,
    slot_own,
    slot_sent,
    slot_got,
    slot_fold,
    slot_back,
    load_sem,
    pipe_send,
    pipe_recv,
    spread_send,
    spread_recv,
    deal_send,
    deal_recv,
    cot_send,
    cot_recv,
    rows_send,
    rows_recv,
    dhid_send,
    dhid_recv,
    hid_send,
    hid_recv,
    slice_send,
    slice_recv,
    home_a_send,
    home_a_recv,
    fold_send,
    fold_recv,
    straight_send,
    straight_recv,
    slot_send,
    slot_recv,
    last_send,
    last_recv,
):
    stage = lax.axis_index("pipe")
    stages = lax.axis_size("pipe")
    index = lax.axis_index("expert")
    x = index // GROUP
    y = index % GROUP
    experts, chunks, cap, width = packed_a.shape
    model, hidden = both_w.shape[0], both_w.shape[1] // 2
    spread = experts * cap
    slices, many = slices_of(model)
    wide, slim = slices[0][1], slices[-1][1]
    shift = stage % 2 * many

    def slice_at(yy):
        return (yy + shift) % GROUP

    mine = slice_at(y)

    def with_slice(r, act):
        @pl.when(r < many)
        def _():
            act(pl.multiple_of(r * wide, LANES), wide)

        @pl.when(r >= many)
        def _():
            act(pl.multiple_of(many * wide + (r - many) * slim, LANES), slim)

    def column(xx):
        return {"expert": xx * GROUP + y}

    def beside(j, by):
        return {"expert": (x + j) % experts * GROUP + (y + GROUP + by) % GROUP}

    def ring(by):
        return {"expert": x * GROUP + (y + GROUP + by) % GROUP}

    def along(by):
        return {"pipe": (stage + stages + by) % stages}

    def remote(src, dst, send, recv, device):
        return pltpu.make_async_remote_copy(
            src_ref=src,
            dst_ref=dst,
            send_sem=send,
            recv_sem=recv,
            device_id=device,
            device_id_type=MESH,
        )

    def each(count, body, first=0):
        lax.fori_loop(first, count, lambda c, carry: (body(c), carry)[1], 0)

    def columns(c):
        return pl.ds(c * width if isinstance(c, int) else pl.multiple_of(c * width, LANES), width)

    barrier = pltpu.get_barrier_semaphore()
    partners = [along(1), along(-1)] + [ring(j) for j in range(1, GROUP)]
    partners += [column((x + j) % experts) for j in range(1, experts)]
    partners += [beside(j, sign) for j in range(1, experts) for _, sign in WAYS]
    for partner in partners:
        pl.semaphore_signal(barrier, inc=1, device_id=partner, device_id_type=MESH)
    pl.semaphore_wait(barrier, len(partners))

    def pipe_copy(ab):
        source, target = ((acts, in_a), (grads, in_b))[ab]
        return remote(
            source.at[0], target, pipe_send.at[ab], pipe_recv.at[ab], along(1 - 2 * ab)
        )

    for ab in (0, 1):
        pipe_copy(ab).start()

    def deal_copy(j, start, size):
        return remote(
            w_down.at[0, 0, :, pl.ds(start, size)],
            held.at[y, :, pl.ds(0, size)],
            deal_send.at[j],
            deal_recv.at[j],
            ring(j),
        )

    def deal_own(start, size):
        return pltpu.make_async_copy(
            w_down.at[0, 0, :, pl.ds(start, size)], held.at[y, :, pl.ds(0, size)], deal_send.at[0]
        )

    def deal(j):
        with_slice(slice_at(y + j), lambda start, size: deal_copy(j, start, size).start())

    def deal_sent(j):
        with_slice(slice_at(y + j), lambda start, size: deal_copy(j, start, size).wait_send())

    def deal_got(start, size):
        def body(j):
            got = held.at[(y + GROUP - j) % GROUP, :, pl.ds(0, size)]
            remote(got, got, deal_send.at[j], deal_recv.at[j], ring(j)).wait_recv()

        deal_own(start, size).wait()
        each(GROUP, body, 1)

    each(GROUP, deal, 1)
    with_slice(mine, lambda start, size: deal_own(start, size).start())
    loads = [
        pltpu.make_async_copy(w_gate.at[0, 0], both_w.at[:, pl.ds(0, hidden)], load_sem.at[0]),
        pltpu.make_async_copy(w_up.at[0, 0], both_w.at[:, pl.ds(hidden, hidden)], load_sem.at[1]),
        pltpu.make_async_copy(kept.at[0, :, 0], saved, load_sem.at[2]),
    ]
    for load in loads:
        load.start()

    @pl.when(mine >= many)
    def _():
        held[:, :, slim:] = jnp.zeros((GROUP, hidden, wide - slim), bf16)
        cot_b[:, :, :, slim:] = jnp.zeros((GROUP, experts, cap, wide - slim), bf16)

    pack_a, unpack_a = place_matrices(routes_a[...], experts, cap)
    pack_b, unpack_b = place_matrices(routes_b[...], experts, cap)
    gate_a = column_of(gates_a[...])
    gate_b = column_of(gates_b[...].astype(bf16).astype(f32))

    def spread_copy(ab, j):
        to = (x + j) % experts
        return remote(
            (packed_a, packed_b)[ab].at[to],
            (rows_a.at[y, :, x], local_b.at[x])[ab],
            spread_send.at[ab, j - 1],
            spread_recv.at[ab, j - 1],
            column(to),
        )

    def spread_wait(ab):
        for j in range(1, experts):
            sender = (x + experts - j) % experts
            got = (rows_a.at[y, :, sender], local_b.at[sender])[ab]
            remote(
                got, got, spread_send.at[ab, j - 1], spread_recv.at[ab, j - 1], column(x)
            ).wait_recv()

    def packed_rows(pack, source, start, size):
        chosen = jnp.dot(pack, source[:, start : start + size], preferred_element_type=f32)
        return chosen.astype(bf16).reshape(experts, cap, size)

    pipe_copy(0).wait_recv()
    for c in range(chunks):
        packed_a[:, c] = packed_rows(pack_a, in_a, c * width, width)
    for j in range(1, experts):
        spread_copy(0, j).start()
    rows_a[y, :, x] = packed_a[x]
    pipe_copy(1).wait_recv()
    packed_b[:, many:, :, slim:] = jnp.zeros((experts, GROUP - many, cap, wide - slim), bf16)
    for r, (start, size) in enumerate(slices):
        packed_b[:, r, :, :size] = packed_rows(pack_b, in_b, start, size)
    for j in range(1, experts):
        spread_copy(1, j).start()
    local_b[x] = packed_b[x]

    def cot_copy(j, size):
        return remote(
            local_b.at[:, slice_at(y + j), :, pl.ds(0, size)],
            cot_b.at[y, :, :, pl.ds(0, size)],
            cot_send.at[j],
            cot_recv.at[j],
            ring(j),
        )

    def cot_own(size):
        return pltpu.make_async_copy(
            local_b.at[:, mine, :, pl.ds(0, size)],
            cot_b.at[y, :, :, pl.ds(0, size)],
            cot_send.at[0],
        )

    def cot_got(start, size):
        def body(j):
            got = cot_b.at[(y + GROUP - j) % GROUP, :, :, pl.ds(0, size)]
            remote(got, got, cot_send.at[j], cot_recv.at[j], ring(j)).wait_recv()

        cot_own(size).wait()
        each(GROUP, body, 1)

    def cot(j):
        with_slice(slice_at(y + j), lambda start, size: cot_copy(j, size).start())

    def cot_sent(j):
        with_slice(slice_at(y + j), lambda start, size: cot_copy(j, size).wait_send())

    def halves(ref, d, t, far):
        half = ref.shape[0] // 2
        return ref.at[pl.ds(d * half, half)] if t == far else ref

    class Gather:
        def __init__(self, blocks, send, recv):
            self.blocks, self.send, self.recv = blocks, send, recv
            self.count = blocks.shape[1]

        def copy(self, t, c, d, sign, on=0):
            at = self.blocks.at[(y + GROUP - sign * (t + on)) % GROUP, c]
            at = halves(at, d, t, HOPS - 1)
            k = t * self.count + c
            return remote(at, at, self.send.at[d, k], self.recv.at[d, k], ring(sign))

        def step(self, t, c):
            for d, sign in WAYS:
                if t:
                    self.copy(t - 1, c, d, sign, 1).wait_recv()
                self.copy(t, c, d, sign).start()

        def last(self, c):
            for d, sign in WAYS:
                self.copy(HOPS - 1, c, d, sign, 1).wait_recv()

        def sent(self, c):
            for t in range(HOPS):
                for d, sign in WAYS:
                    self.copy(t, c, d, sign).wait_send()

    class Fold:
        def __init__(self, part, sums, send, recv):
            self.part, self.sums, self.send, self.recv = part, sums, send, recv
            self.count = part.shape[1]

        def copy(self, t, c, d, sign):
            at = self.part.at[(y + GROUP + sign * (HOPS - t)) % GROUP, c]
            k = t * self.count + c
            return remote(
                halves(at, d, t, 0),
                halves(self.sums.at[d, t, c], d, t, 0),
                self.send.at[d, k],
                self.recv.at[d, k],
                ring(sign),
            )

        def step(self, t, c, straight=None):
            half = self.part.shape[2] // 2
            for d, sign in WAYS:
                block = (y + GROUP + sign * (HOPS - t)) % GROUP
                if t:
                    self.copy(t - 1, c, d, sign).wait_recv()
                    at = pl.ds(d * half, half) if t == 1 else pl.ds(0, 2 * half)
                    self.part[block, c, at] = (
                        self.part[block, c, at].astype(f32)
                        + self.sums[d, t - 1, c, at].astype(f32)
                    ).astype(bf16)
                if straight is None:
                    self.copy(t, c, d, sign).start()
                else:
                    straight(c, d, sign, block)

        def total(self, c):
            for d, sign in WAYS:
                self.copy(HOPS - 1, c, d, sign).wait_recv()
            return (
                self.part[y, c].astype(f32)
                + self.sums[0, HOPS - 1, c].astype(f32)
                + self.sums[1, HOPS - 1, c].astype(f32)
            )

        def sent(self, c, hops=HOPS):
            for t in range(hops):
                for d, sign in WAYS:
                    self.copy(t, c, d, sign).wait_send()

    rows = Gather(rows_a, rows_send, rows_recv)
    hids = Gather(hid_all, hid_send, hid_recv)
    dhids = Fold(dhid_part, dhid_sums, dhid_send, dhid_recv)
    grads_x = Fold(part_b, sums_b, fold_send, fold_recv)

    def dhid_partial(p):
        here = cot_b[pl.ds(2 * p, 2)].reshape(2 * spread, wide)
        dhid = nt_dot(here, held[...].reshape(GROUP * hidden, wide)).astype(bf16)
        for g in range(GROUP):
            dhid_part[g, p] = dhid[:, g * hidden : (g + 1) * hidden].reshape(2, spread, hidden)

    def forward(p):
        pre = jnp.zeros((2 * spread, 2 * hidden), f32)
        for c in range(chunks):
            pre += jnp.dot(
                rows_a[pl.ds(2 * p, 2), c].reshape(2 * spread, width),
                both_w[pl.ds(c * width, width), :],
                preferred_element_type=f32,
            )
        pre_g, pre_u = pre[:, :hidden], pre[:, hidden:]
        hid = (pre_g * jax.nn.sigmoid(pre_g) * pre_u).astype(bf16)
        hid_all[y, p] = hid.reshape(2, spread, hidden)

    def forward_out(p):
        hid = jnp.concatenate(
            [hid_all[g, p].reshape(2 * spread, hidden) for g in range(GROUP)], axis=1
        )
        done = jnp.dot(
            hid, held[...].reshape(GROUP * hidden, wide), preferred_element_type=f32
        )
        slice_part[pl.ds(2 * p, 2)] = done.astype(bf16).reshape(2, experts, cap, wide)

    def backward(p):
        dhid = dhids.total(p).reshape(2 * spread, hidden)
        both = jnp.concatenate(
            [saved[j * GROUP + 2 * p + i] for i in (0, 1) for j in range(experts)], axis=0
        ).astype(f32)
        sg, su = both[:, :hidden], both[:, hidden:]
        sig = jax.nn.sigmoid(sg)
        act = sg * sig
        hid = (act * su).astype(bf16).astype(f32)
        slot_row = jnp.sum((hid * dhid).T, axis=0, keepdims=True)
        slot_own[p] = jnp.broadcast_to(slot_row, slot_own.shape[1:])
        d_g = (dhid * su * sig * (1.0 + sg * (1.0 - sig))).astype(bf16)
        d_u = (dhid * act).astype(bf16)
        d_both = jnp.concatenate([d_g, d_u], axis=1)
        for c in range(chunks):
            part_b[pl.ds(2 * p, 2), c] = (
                nt_dot(d_both, both_w[pl.ds(c * width, width), :])
                .astype(bf16)
                .reshape(2, experts, cap, width)
            )

    def slice_copy(j, size):
        return remote(
            slice_part.at[(y + j) % GROUP, :, :, pl.ds(0, size)],
            slice_got.at[mine, :, :, pl.ds(0, size)],
            slice_send.at[j],
            slice_recv.at[j],
            ring(j),
        )

    def home_a_copy(r, j):
        to = (x + j) % experts
        at = pl.ds(0, slices[r][1])
        return remote(
            slice_got.at[r, to, :, at],
            back_a.at[r, x, :, at],
            home_a_send.at[r, j - 1],
            home_a_recv.at[r, j - 1],
            column(to),
        )

    def home_a(r):
        off = (y + GROUP - (r + GROUP - shift) % GROUP) % GROUP

        @pl.when(off != 0)
        def _():
            got = slice_got.at[r, :, :, pl.ds(0, slices[r][1])]
            remote(got, got, slice_send.at[off], slice_recv.at[off], ring(1)).wait_recv()

        for j in range(1, experts):
            home_a_copy(r, j).start()
        back_a[r, x] = slice_got[r, x]

    def finish_a(r):
        start, size = slices[r]
        for j in range(1, experts):
            got = back_a.at[r, (x + experts - j) % experts, :, pl.ds(0, size)]
            remote(
                got, got, home_a_send.at[r, j - 1], home_a_recv.at[r, j - 1], column(x)
            ).wait_recv()
        picked = jnp.dot(
            unpack_a, back_a[r, :, :, :size].reshape(spread, size), preferred_element_type=f32
        )
        at = slice(start, start + size)
        out_a[0, :, at] = (in_a[:, at].astype(f32) + gate_a * picked).astype(bf16)

    def straight_copy(c, d, j, sign, block):
        return remote(
            part_b.at[block, c, (x + j) % experts],
            straight.at[c, d, x],
            straight_send.at[c, d, j],
            straight_recv.at[c],
            beside(j, sign),
        )

    def straight_own(c):
        return pltpu.make_async_copy(
            part_b.at[y, c, x], straight.at[c, 2, x], straight_recv.at[c]
        )

    def straight_mine(c):
        straight_own(c).start()
        for j in range(1, experts):
            straight_copy(c, 2, j, 0, y).start()

    def straight_last(c, d, sign, block):
        for j in range(experts):
            straight_copy(c, d, j, sign, block).start()

    def straight_sent(c):
        for d, sign in WAYS:
            block = (y + GROUP + sign) % GROUP
            for j in range(experts):
                straight_copy(c, d, j, sign, block).wait_send()
        for j in range(1, experts):
            straight_copy(c, 2, j, 0, y).wait_send()

    def straight_finish(c):
        got = straight.at[c]
        remote(
            got, got, straight_send.at[c, 0, 0], straight_recv.at[c], column(x)
        ).wait_recv()
        picked = jnp.zeros((spread, width), f32)
        for d in range(3):
            rows_d = straight[c, d].reshape(spread, width)
            picked += jnp.dot(unpack_b, rows_d, preferred_element_type=f32)
        out_b[0, :, columns(c)] = (in_b[:, columns(c)].astype(f32) + gate_b * picked).astype(bf16)

    def slot_copy(d, t, sign):
        return remote(
            slot_sent.at[d, t],
            slot_got.at[d, t],
            slot_send.at[d, t],
            slot_recv.at[d, t],
            ring(sign),
        )

    def slot_step(t):
        for d, sign in WAYS:
            if t < d:
                continue
            pair = ((y + GROUP + sign * (HOPS - t)) % GROUP) // 2
            if t > d:
                slot_copy(d, t - 1, sign).wait_recv()
                slot_sent[d, t] = slot_own[pair] + slot_got[d, t - 1]
            else:
                slot_sent[d, t] = slot_own[pair]
            slot_copy(d, t, sign).start()

    def last_copy(j):
        return remote(
            slot_fold,
            slot_back.at[x],
            last_send.at[j - 1],
            last_recv.at[j - 1],
            column((x + j) % experts),
        )

    def slot_last():
        for d, sign in WAYS:
            slot_copy(d, HOPS - 1, sign).wait_recv()
        slot_fold[...] = slot_own[y // 2] + slot_got[0, HOPS - 1] + slot_got[1, HOPS - 1]
        for j in range(1, experts):
            last_copy(j).start()
        slot_back[x] = slot_fold[...]

    def slot_finish():
        for j in range(1, experts):
            got = slot_back.at[(x + experts - j) % experts]
            remote(
                got, got, last_send.at[j - 1], last_recv.at[j - 1], column(x)
            ).wait_recv()
        tokens = routes_b.shape[1]
        lanes = slot_back.shape[2]
        routes = column_of(routes_b[...].astype(f32))
        lane = lax.broadcasted_iota(jnp.int32, (tokens, spread), 1)
        taken = jnp.where(unpack_b > 0, (lane % cap).astype(f32), 0.0)
        slot = jnp.sum(taken, axis=1, keepdims=True)
        lane = lax.broadcasted_iota(jnp.int32, (tokens, lanes), 1)
        first = (y % 2) * spread + x * cap
        here = jnp.broadcast_to(slot, (tokens, lanes)) == (lane - first).astype(f32)
        total = jnp.zeros((tokens, lanes), f32)
        for e in range(experts):
            values = jnp.broadcast_to(slot_back[e][0:1], (tokens, lanes))
            total += jnp.where(here & (routes == float(e)), values, 0.0)
        out_g[...] = row_of(jnp.sum(total, axis=1, keepdims=True))

    spread_wait(0)
    for t in range(HOPS):
        each(chunks, functools.partial(rows.step, t))
    spread_wait(1)
    each(GROUP, cot, 1)
    with_slice(mine, lambda start, size: cot_own(size).start())
    for load in loads:
        load.wait()
    each(chunks, rows.last)

    def body(p):
        forward(p)
        hids.step(0, p)

    each(PAIRS, body)
    with_slice(mine, deal_got)
    with_slice(mine, cot_got)

    def body(p):
        dhid_partial(p)
        dhids.step(0, p)
        hids.step(1, p)

    each(PAIRS, body)

    def body(p):
        hids.step(2, p)
        dhids.step(1, p)

    each(PAIRS, body)

    def body(p):
        hids.step(3, p)
        dhids.step(2, p)

    each(PAIRS, body)

    def body(p):
        dhids.step(3, p)
        hids.last(p)
        forward_out(p)
        for i in (0, 1):
            j = (2 * p + i + GROUP - y) % GROUP
            pl.when(j != 0)(
                lambda: with_slice(mine, lambda start, size: slice_copy(j, size).start())
            )

    each(PAIRS, body)
    slice_got[mine] = slice_part[y]

    backward((y // 2 + PAIRS // 2) % PAIRS)
    each(chunks, lambda c: grads_x.step(0, c))
    backward((y // 2 + PAIRS // 2 + 3 - 2 * (y % 2)) % PAIRS)
    backward((y // 2 + PAIRS // 2 + 1 + 2 * (y % 2)) % PAIRS)
    backward(y // 2)
    slot_step(0)
    each(chunks, straight_mine)
    each(chunks, lambda c: grads_x.step(1, c))
    slot_step(1)
    for r in range(GROUP):
        home_a(r)
    each(chunks, lambda c: grads_x.step(2, c))
    slot_step(2)
    each(chunks, lambda c: grads_x.step(3, c, straight_last))
    slot_step(3)
    for r in range(GROUP):
        finish_a(r)

    for ab in (0, 1):
        pipe_copy(ab).wait_send()
        for j in range(1, experts):
            spread_copy(ab, j).wait_send()
    each(GROUP, deal_sent, 1)
    each(GROUP, cot_sent, 1)
    each(chunks, rows.sent)
    each(PAIRS, dhids.sent)
    each(PAIRS, hids.sent)

    def body(start, size):
        each(GROUP, lambda j: slice_copy(j, size).wait_send(), 1)

    with_slice(mine, body)

    slot_last()

    for r in range(GROUP):
        for j in range(1, experts):
            home_a_copy(r, j).wait_send()
    each(chunks, lambda c: grads_x.sent(c, HOPS - 1))
    slot_finish()

    def body(c):
        straight_finish(c)
        straight_sent(c)

    each(chunks, body)
    for d, sign in WAYS:
        for t in range(d, HOPS):
            slot_copy(d, t, sign).wait_send()
    for j in range(1, experts):
        last_copy(j).wait_send()


def on_device(
    section_acts,
    fwd_routes,
    fwd_gates,
    section_grads,
    bwd_routes,
    bwd_gates,
    saved_proj,
    w_gate,
    w_up,
    w_down,
):
    experts = lax.axis_size("expert") // GROUP
    _, tokens, model = section_acts.shape
    cap, hidden = saved_proj.shape[3], w_gate.shape[3]
    width = model // CHUNKS
    sources = saved_proj.shape[1]
    spread = experts * cap
    lanes = 2 * spread
    wide = slices_of(model)[0][0][1]
    whole = (tokens, model)
    by_slice = (experts, GROUP, cap, wide)
    by_chunk = (experts, CHUNKS, cap, width)
    blocks = (CHUNKS, experts, cap, width)
    hids = (PAIRS, 2, spread, hidden)
    dma = pltpu.SemaphoreType.DMA
    hbm = pl.BlockSpec(memory_space=pltpu.HBM)
    vmem = pl.BlockSpec(memory_space=pltpu.VMEM)

    def as_row(array):
        return array.reshape(1, tokens)

    def two(*shape):
        return [dma(shape), dma(shape)]

    shapes = [
        whole,
        whole,
        by_chunk,
        by_slice,
        (GROUP,) + blocks,
        by_slice,
        (GROUP, experts, cap, wide),
        (GROUP, hidden, wide),
        (GROUP,) + hids,
        (2, HOPS) + hids,
        (GROUP,) + hids,
        (GROUP, experts, cap, wide),
        (GROUP, experts, cap, wide),
        (GROUP,) + blocks,
        (2, HOPS) + blocks,
        (GROUP, experts, cap, wide),
        (CHUNKS, 3, experts, cap, width),
        (model, 2 * hidden),
        (sources, cap, 2 * hidden),
    ]
    slots = [(PAIRS, 8, lanes), (2, HOPS, 8, lanes), (2, HOPS, 8, lanes), (8, lanes)]
    slots.append((experts, 8, lanes))

    out_a, out_b, out_g = pl.pallas_call(
        kernel,
        out_shape=(
            pltpu.VMEM(section_acts.shape, bf16),
            pltpu.VMEM(section_grads.shape, bf16),
            pltpu.VMEM((1, tokens), f32),
        ),
        in_specs=[hbm, hbm, vmem, vmem, vmem, vmem, hbm, hbm, hbm, hbm],
        out_specs=(vmem, vmem, vmem),
        scratch_shapes=[pltpu.VMEM(shape, bf16) for shape in shapes]
        + [pltpu.VMEM(shape, f32) for shape in slots]
        + [dma((3,))]
        + two(2)
        + two(2, experts - 1)
        + two(GROUP)
        + two(GROUP)
        + two(2, HOPS * CHUNKS)
        + two(2, HOPS * PAIRS)
        + two(2, HOPS * PAIRS)
        + two(GROUP)
        + two(GROUP, experts - 1)
        + two(2, HOPS * CHUNKS)
        + [dma((CHUNKS, 3, experts)), dma((CHUNKS,))]
        + two(2, HOPS)
        + two(experts - 1),
        compiler_params=pltpu.CompilerParams(
            collective_id=0, has_side_effects=True, vmem_limit_bytes=56 * 2**20
        ),
        cost_estimate=pl.CostEstimate(
            flops=2 * 2 * GROUP * spread * model * 3 * hidden,
            bytes_accessed=2 * 3 * model * hidden + 8 * tokens * model,
            transcendentals=2 * GROUP * spread * hidden,
        ),
        name="relay_experts",
    )(
        section_acts,
        section_grads,
        as_row(fwd_routes),
        as_row(fwd_gates),
        as_row(bwd_routes),
        as_row(bwd_gates),
        saved_proj,
        w_gate,
        w_up,
        w_down,
    )
    return out_a, out_b, out_g.reshape(1, tokens, 1)


def solution(mesh):
    tokens = P("pipe", "expert", None)
    weights = P("pipe", "expert", None, None)
    placed = (tokens,) * 6 + (P("pipe", None, "expert", None, None),) + (weights,) * 3
    return jax.shard_map(
        on_device, mesh=mesh, in_specs=placed, out_specs=(tokens,) * 3, check_vma=False
    )
```

```python
import functools

import jax
import jax.numpy as jnp
from jax import lax
from jax.experimental import pallas as pl
from jax.experimental.pallas import tpu as pltpu
from jax.sharding import PartitionSpec as P

GROUP = 8
CHUNKS = 4
PAIRS = GROUP // 2
LANES = 128
HOLDERS = GROUP // 2
HOPS = 4
MESH = pl.DeviceIdType.MESH
WAYS = ((0, 1), (1, -1))
f32 = jnp.float32
bf16 = jnp.bfloat16


def nt_dot(a, b):
    return lax.dot_general(a, b, (((1,), (1,)), ((), ())), preferred_element_type=f32)


def column_of(row):
    count = row.shape[1]
    shape = (count, count)
    eye = lax.broadcasted_iota(jnp.int32, shape, 0) == lax.broadcasted_iota(jnp.int32, shape, 1)
    return jnp.sum(jnp.where(eye, jnp.broadcast_to(row, shape), 0.0), axis=1, keepdims=True)


def row_of(column):
    count = column.shape[0]
    shape = (count, count)
    eye = lax.broadcasted_iota(jnp.int32, shape, 0) == lax.broadcasted_iota(jnp.int32, shape, 1)
    return jnp.sum(jnp.where(eye, jnp.broadcast_to(column, shape), 0.0), axis=0, keepdims=True)


def place_matrices(route_row, experts, cap):
    tokens = route_row.shape[1]
    slots = experts * cap
    routes = route_row.astype(f32)
    column = column_of(routes)
    at = lax.broadcasted_iota(jnp.int32, (tokens, tokens), 0)
    other = lax.broadcasted_iota(jnp.int32, (tokens, tokens), 1)
    slot = lax.broadcasted_iota(jnp.int32, (slots, tokens), 0)
    named = jnp.broadcast_to(routes, (slots, tokens)) == (slot // cap).astype(f32)
    before = jnp.dot(
        jnp.where(named, 1.0, 0.0).astype(bf16),
        jnp.where(at < other, 1.0, 0.0).astype(bf16),
        preferred_element_type=f32,
    )
    pack = jnp.where(named & (before == (slot % cap).astype(f32)), 1.0, 0.0).astype(bf16)
    slot = lax.broadcasted_iota(jnp.int32, (tokens, slots), 1)
    named = jnp.broadcast_to(column, (tokens, slots)) == (slot // cap).astype(f32)
    before = jnp.dot(
        jnp.where(other < at, 1.0, 0.0).astype(bf16),
        jnp.where(named, 1.0, 0.0).astype(bf16),
        preferred_element_type=f32,
    )
    unpack = jnp.where(named & (before == (slot % cap).astype(f32)), 1.0, 0.0).astype(bf16)
    return pack, unpack


def kernel(
    acts,
    grads,
    routes_a,
    gates_a,
    routes_b,
    gates_b,
    kept,
    w_gate,
    w_up,
    w_down,
    out_a,
    out_b,
    out_g,
    in_a,
    in_b,
    packed_a,
    packed_b,
    rows_a,
    local_b,
    cot_b,
    held,
    dhid_part,
    dhid_sums,
    hid_all,
    slice_part,
    slice_got,
    part_b,
    sums_b,
    back_a,
    straight,
    both_w,
    saved,
    slot_own,
    slot_sent,
    slot_got,
    slot_fold,
    slot_back,
    load_sem,
    pipe_send,
    pipe_recv,
    spread_send,
    spread_recv,
    deal_send,
    deal_recv,
    cot_send,
    cot_recv,
    rows_send,
    rows_recv,
    dhid_send,
    dhid_recv,
    hid_send,
    hid_recv,
    slice_send,
    slice_recv,
    home_a_send,
    home_a_recv,
    fold_send,
    fold_recv,
    straight_send,
    straight_recv,
    slot_send,
    slot_recv,
    last_send,
    last_recv,
):
    stage = lax.axis_index("pipe")
    stages = lax.axis_size("pipe")
    index = lax.axis_index("expert")
    x = index // GROUP
    y = index % GROUP
    experts, chunks, cap, width = packed_a.shape
    model, hidden = both_w.shape[0], both_w.shape[1] // 2
    spread = experts * cap
    size = model // HOLDERS
    turn = stage % 2
    holds = y % 2 == turn
    passes = y % 2 != turn
    mine = y // 2

    def holder(r):
        return 2 * r + turn

    def at_y(yy):
        return {"expert": x * GROUP + yy}

    def column(xx):
        return {"expert": xx * GROUP + y}

    def beside(j, by):
        return {"expert": (x + j) % experts * GROUP + (y + GROUP + by) % GROUP}

    def ring(by):
        return {"expert": x * GROUP + (y + GROUP + by) % GROUP}

    def along(by):
        return {"pipe": (stage + stages + by) % stages}

    def remote(src, dst, send, recv, device):
        return pltpu.make_async_remote_copy(
            src_ref=src,
            dst_ref=dst,
            send_sem=send,
            recv_sem=recv,
            device_id=device,
            device_id_type=MESH,
        )

    def each(count, body, first=0):
        lax.fori_loop(first, count, lambda c, carry: (body(c), carry)[1], 0)

    def columns(c):
        return pl.ds(c * width if isinstance(c, int) else pl.multiple_of(c * width, LANES), width)

    barrier = pltpu.get_barrier_semaphore()
    partners = [along(1), along(-1)] + [ring(j) for j in range(1, GROUP)]
    partners += [column((x + j) % experts) for j in range(1, experts)]
    partners += [beside(j, sign) for j in range(1, experts) for _, sign in WAYS]
    for partner in partners:
        pl.semaphore_signal(barrier, inc=1, device_id=partner, device_id_type=MESH)
    pl.semaphore_wait(barrier, len(partners))

    def pipe_copy(ab):
        source, target = ((acts, in_a), (grads, in_b))[ab]
        return remote(
            source.at[0], target, pipe_send.at[ab], pipe_recv.at[ab], along(1 - 2 * ab)
        )

    for ab in (0, 1):
        pipe_copy(ab).start()

    def to_holder(r, source, target, send, recv):
        return remote(source, target.at[y], send.at[r], recv.at[y], at_y(holder(r)))

    def to_self(r, source, target, send):
        return pltpu.make_async_copy(source, target.at[y], send.at[r])

    def hold_start(r, source, *rest):
        pl.when(holder(r) != y)(lambda: to_holder(r, source, *rest).start())
        pl.when(holder(r) == y)(lambda: to_self(r, source, *rest[:2]).start())

    def hold_sent(r, source, *rest):
        pl.when(holder(r) != y)(lambda: to_holder(r, source, *rest).wait_send())

    def hold_own(r, source, *rest):
        pl.when(holder(r) == y)(lambda: to_self(r, source, *rest[:2]).wait())

    def hold_got(target, send, recv):
        def body(g):
            got = target.at[g]
            pl.when(g != y)(
                lambda: remote(got, got, send.at[0], recv.at[g], at_y(g)).wait_recv()
            )

        pl.when(holds)(lambda: each(GROUP, body))

    def deal(r):
        source = w_down.at[0, 0, :, pl.ds(r * size, size)]
        return r, source, held, deal_send, deal_recv

    def cot(r):
        return r, local_b.at[:, r], cot_b, cot_send, cot_recv

    for r in range(HOLDERS):
        hold_start(*deal(r))
    loads = [
        pltpu.make_async_copy(w_gate.at[0, 0], both_w.at[:, pl.ds(0, hidden)], load_sem.at[0]),
        pltpu.make_async_copy(w_up.at[0, 0], both_w.at[:, pl.ds(hidden, hidden)], load_sem.at[1]),
        pltpu.make_async_copy(kept.at[0, :, 0], saved, load_sem.at[2]),
    ]
    for load in loads:
        load.start()

    @pl.when(passes)
    def _():
        dhid_part[y] = jnp.zeros(dhid_part.shape[1:], bf16)

    pack_a, unpack_a = place_matrices(routes_a[...], experts, cap)
    pack_b, unpack_b = place_matrices(routes_b[...], experts, cap)
    gate_a = column_of(gates_a[...])
    gate_b = column_of(gates_b[...].astype(bf16).astype(f32))

    def spread_copy(ab, j):
        to = (x + j) % experts
        return remote(
            (packed_a, packed_b)[ab].at[to],
            (rows_a.at[y, :, x], local_b.at[x])[ab],
            spread_send.at[ab, j - 1],
            spread_recv.at[ab, j - 1],
            column(to),
        )

    def spread_wait(ab):
        for j in range(1, experts):
            sender = (x + experts - j) % experts
            got = (rows_a.at[y, :, sender], local_b.at[sender])[ab]
            remote(
                got, got, spread_send.at[ab, j - 1], spread_recv.at[ab, j - 1], column(x)
            ).wait_recv()

    def packed_rows(pack, source, start, size):
        chosen = jnp.dot(pack, source[:, start : start + size], preferred_element_type=f32)
        return chosen.astype(bf16).reshape(experts, cap, size)

    pipe_copy(0).wait_recv()
    for c in range(chunks):
        packed_a[:, c] = packed_rows(pack_a, in_a, c * width, width)
    for j in range(1, experts):
        spread_copy(0, j).start()
    rows_a[y, :, x] = packed_a[x]
    pipe_copy(1).wait_recv()
    for r in range(HOLDERS):
        packed_b[:, r] = packed_rows(pack_b, in_b, r * size, size)
    for j in range(1, experts):
        spread_copy(1, j).start()
    local_b[x] = packed_b[x]

    def halves(ref, d, t, far):
        half = ref.shape[0] // 2
        return ref.at[pl.ds(d * half, half)] if t == far else ref

    class Gather:
        def __init__(self, blocks, send, recv):
            self.blocks, self.send, self.recv = blocks, send, recv
            self.count = blocks.shape[1]

        def copy(self, t, c, d, sign, on=0, part=False):
            at = self.blocks.at[(y + GROUP - sign * (t + on)) % GROUP, c]
            at = halves(at, d, t, t if part else HOPS - 1)
            k = t * self.count + c
            return remote(at, at, self.send.at[d, k], self.recv.at[d, k], ring(sign))

        def step(self, t, c):
            for d, sign in WAYS:
                if t:
                    self.copy(t - 1, c, d, sign, 1).wait_recv()
                self.copy(t, c, d, sign).start()

        def last(self, c):
            for d, sign in WAYS:
                self.copy(HOPS - 1, c, d, sign, 1).wait_recv()

        def sent(self, c):
            for t in range(HOPS):
                for d, sign in WAYS:
                    self.copy(t, c, d, sign).wait_send()

    class HolderGather(Gather):
        def step(self, t, c):
            for d, sign in WAYS:
                if t == 1 or t == 2:
                    self.copy(t - 1, c, d, sign, 1).wait_recv()
                if t < 2:
                    self.copy(t, c, d, sign).start()
                elif t == 2:
                    pl.when(holds)(lambda: self.copy(2, c, d, sign, 0, True).start())
                    pl.when(passes)(lambda: self.copy(2, c, d, sign).start())
                else:
                    pl.when(holds)(lambda: self.copy(2, c, d, sign, 1).wait_recv())

                    @pl.when(passes)
                    def _():
                        self.copy(2, c, d, sign, 1, True).wait_recv()
                        self.copy(3, c, d, sign, 0, True).start()

        def last(self, c):
            for d, sign in WAYS:
                pl.when(holds)(lambda: self.copy(3, c, d, sign, 1, True).wait_recv())

        def sent(self, c):
            for d, sign in WAYS:
                for t in (0, 1):
                    self.copy(t, c, d, sign).wait_send()
                pl.when(holds)(lambda: self.copy(2, c, d, sign, 0, True).wait_send())

                @pl.when(passes)
                def _():
                    self.copy(2, c, d, sign).wait_send()
                    self.copy(3, c, d, sign, 0, True).wait_send()

    class Fold:
        def __init__(self, part, sums, send, recv):
            self.part, self.sums, self.send, self.recv = part, sums, send, recv
            self.count = part.shape[1]

        def copy(self, t, c, d, sign):
            at = self.part.at[(y + GROUP + sign * (HOPS - t)) % GROUP, c]
            k = t * self.count + c
            return remote(
                halves(at, d, t, 0),
                halves(self.sums.at[d, t, c], d, t, 0),
                self.send.at[d, k],
                self.recv.at[d, k],
                ring(sign),
            )

        def step(self, t, c, straight=None):
            half = self.part.shape[2] // 2
            for d, sign in WAYS:
                block = (y + GROUP + sign * (HOPS - t)) % GROUP
                if t:
                    self.copy(t - 1, c, d, sign).wait_recv()
                    at = pl.ds(d * half, half) if t == 1 else pl.ds(0, 2 * half)
                    self.part[block, c, at] = (
                        self.part[block, c, at].astype(f32)
                        + self.sums[d, t - 1, c, at].astype(f32)
                    ).astype(bf16)
                if straight is None:
                    self.copy(t, c, d, sign).start()
                else:
                    straight(c, d, sign, block)

        def total(self, c):
            for d, sign in WAYS:
                self.copy(HOPS - 1, c, d, sign).wait_recv()
            return (
                self.part[y, c].astype(f32)
                + self.sums[0, HOPS - 1, c].astype(f32)
                + self.sums[1, HOPS - 1, c].astype(f32)
            )

        def sent(self, c, hops=HOPS):
            for t in range(hops):
                for d, sign in WAYS:
                    self.copy(t, c, d, sign).wait_send()

    class HolderFold(Fold):
        def onward(self, t, c, d, sign, part=False, at=None):
            k = t * self.count + c
            source = self.sums.at[d, t if at is None else at, c]
            target = self.sums.at[d, t, c]
            return remote(
                halves(source, d, t, t if part else HOPS),
                halves(target, d, t, t if part else HOPS),
                self.send.at[d, k],
                self.recv.at[d, k],
                ring(sign),
            )

        def step(self, t, c):
            half = self.part.shape[2] // 2
            for d, sign in WAYS:

                @pl.when(holds)
                def _():
                    if t >= 2:
                        self.onward(t - 1, c, d, sign, t == 2).wait_recv()
                        block = (y + GROUP + sign * (HOPS - t)) % GROUP
                        at = pl.ds(d * half, half) if t == 2 else pl.ds(0, 2 * half)
                        self.part[block, c, at] = (
                            self.part[block, c, at].astype(f32)
                            + self.sums[d, t - 1, c, at].astype(f32)
                        ).astype(bf16)
                    self.copy(t, c, d, sign).start()

                if t:

                    @pl.when(passes)
                    def _():
                        self.onward(t - 1, c, d, sign, t == 1).wait_recv()
                        self.onward(t, c, d, sign, t == 1, t - 1).start()

        def sent(self, c):
            for d, sign in WAYS:

                @pl.when(holds)
                def _():
                    for t in range(HOPS):
                        self.copy(t, c, d, sign).wait_send()

                @pl.when(passes)
                def _():
                    for t in range(1, HOPS):
                        self.onward(t, c, d, sign, t == 1, t - 1).wait_send()

    rows = Gather(rows_a, rows_send, rows_recv)
    hids = HolderGather(hid_all, hid_send, hid_recv)
    dhids = HolderFold(dhid_part, dhid_sums, dhid_send, dhid_recv)
    grads_x = Fold(part_b, sums_b, fold_send, fold_recv)

    def dhid_partial(p):
        here = cot_b[pl.ds(2 * p, 2)].reshape(2 * spread, size)
        dhid = nt_dot(here, held[...].reshape(GROUP * hidden, size)).astype(bf16)
        for g in range(GROUP):
            dhid_part[g, p] = dhid[:, g * hidden : (g + 1) * hidden].reshape(2, spread, hidden)

    def forward(p):
        pre = jnp.zeros((2 * spread, 2 * hidden), f32)
        for c in range(chunks):
            pre += jnp.dot(
                rows_a[pl.ds(2 * p, 2), c].reshape(2 * spread, width),
                both_w[pl.ds(c * width, width), :],
                preferred_element_type=f32,
            )
        pre_g, pre_u = pre[:, :hidden], pre[:, hidden:]
        hid = (pre_g * jax.nn.sigmoid(pre_g) * pre_u).astype(bf16)
        hid_all[y, p] = hid.reshape(2, spread, hidden)

    def forward_out(p):
        hid = jnp.concatenate(
            [hid_all[g, p].reshape(2 * spread, hidden) for g in range(GROUP)], axis=1
        )
        done = jnp.dot(
            hid, held[...].reshape(GROUP * hidden, size), preferred_element_type=f32
        )
        slice_part[pl.ds(2 * p, 2)] = done.astype(bf16).reshape(2, experts, cap, size)

    def backward(p):
        dhid = dhids.total(p).reshape(2 * spread, hidden)
        both = jnp.concatenate(
            [saved[j * GROUP + 2 * p + i] for i in (0, 1) for j in range(experts)], axis=0
        ).astype(f32)
        sg, su = both[:, :hidden], both[:, hidden:]
        sig = jax.nn.sigmoid(sg)
        act = sg * sig
        hid = (act * su).astype(bf16).astype(f32)
        slot_row = jnp.sum((hid * dhid).T, axis=0, keepdims=True)
        slot_own[p] = jnp.broadcast_to(slot_row, slot_own.shape[1:])
        d_g = (dhid * su * sig * (1.0 + sg * (1.0 - sig))).astype(bf16)
        d_u = (dhid * act).astype(bf16)
        d_both = jnp.concatenate([d_g, d_u], axis=1)
        for c in range(chunks):
            part_b[pl.ds(2 * p, 2), c] = (
                nt_dot(d_both, both_w[pl.ds(c * width, width), :])
                .astype(bf16)
                .reshape(2, experts, cap, width)
            )

    def slice_copy(b):
        return remote(
            slice_part.at[b], slice_got.at[mine], slice_send.at[b], slice_recv.at[mine], at_y(b)
        )

    def slice_out(p):
        forward_out(p)
        for b in (2 * p, 2 * p + 1):
            pl.when(b != y)(lambda: slice_copy(b).start())

    def home_a_copy(r, j):
        to = (x + j) % experts
        return remote(
            slice_got.at[r, to],
            back_a.at[r, x],
            home_a_send.at[r, j - 1],
            home_a_recv.at[r, j - 1],
            column(to),
        )

    def home_a(r):
        @pl.when(holder(r) != y)
        def _():
            got = slice_got.at[r]
            remote(got, got, slice_send.at[0], slice_recv.at[r], ring(1)).wait_recv()

        for j in range(1, experts):
            home_a_copy(r, j).start()
        back_a[r, x] = slice_got[r, x]

    def finish_a(r):
        for j in range(1, experts):
            got = back_a.at[r, (x + experts - j) % experts]
            remote(
                got, got, home_a_send.at[r, j - 1], home_a_recv.at[r, j - 1], column(x)
            ).wait_recv()
        picked = jnp.dot(
            unpack_a, back_a[r].reshape(spread, size), preferred_element_type=f32
        )
        at = slice(r * size, (r + 1) * size)
        out_a[0, :, at] = (in_a[:, at].astype(f32) + gate_a * picked).astype(bf16)

    def straight_copy(c, d, j, sign, block):
        return remote(
            part_b.at[block, c, (x + j) % experts],
            straight.at[c, d, x],
            straight_send.at[c, d, j],
            straight_recv.at[c],
            beside(j, sign),
        )

    def straight_own(c):
        return pltpu.make_async_copy(
            part_b.at[y, c, x], straight.at[c, 2, x], straight_recv.at[c]
        )

    def straight_mine(c):
        straight_own(c).start()
        for j in range(1, experts):
            straight_copy(c, 2, j, 0, y).start()

    def straight_last(c, d, sign, block):
        for j in range(experts):
            straight_copy(c, d, j, sign, block).start()

    def straight_sent(c):
        for d, sign in WAYS:
            block = (y + GROUP + sign) % GROUP
            for j in range(experts):
                straight_copy(c, d, j, sign, block).wait_send()
        for j in range(1, experts):
            straight_copy(c, 2, j, 0, y).wait_send()

    def straight_finish(c):
        got = straight.at[c]
        remote(
            got, got, straight_send.at[c, 0, 0], straight_recv.at[c], column(x)
        ).wait_recv()
        picked = jnp.zeros((in_b.shape[0], width), f32)
        for d in range(3):
            rows_d = straight[c, d].reshape(spread, width)
            picked += jnp.dot(unpack_b, rows_d, preferred_element_type=f32)
        out_b[0, :, columns(c)] = (in_b[:, columns(c)].astype(f32) + gate_b * picked).astype(bf16)

    def slot_copy(d, t, sign):
        return remote(
            slot_sent.at[d, t],
            slot_got.at[d, t],
            slot_send.at[d, t],
            slot_recv.at[d, t],
            ring(sign),
        )

    def slot_step(t):
        for d, sign in WAYS:
            if t < d:
                continue
            pair = ((y + GROUP + sign * (HOPS - t)) % GROUP) // 2
            if t > d:
                slot_copy(d, t - 1, sign).wait_recv()
                slot_sent[d, t] = slot_own[pair] + slot_got[d, t - 1]
            else:
                slot_sent[d, t] = slot_own[pair]
            slot_copy(d, t, sign).start()

    def last_copy(j):
        return remote(
            slot_fold,
            slot_back.at[x],
            last_send.at[j - 1],
            last_recv.at[j - 1],
            column((x + j) % experts),
        )

    def slot_last():
        for d, sign in WAYS:
            slot_copy(d, HOPS - 1, sign).wait_recv()
        slot_fold[...] = slot_own[y // 2] + slot_got[0, HOPS - 1] + slot_got[1, HOPS - 1]
        for j in range(1, experts):
            last_copy(j).start()
        slot_back[x] = slot_fold[...]

    def slot_finish():
        for j in range(1, experts):
            got = slot_back.at[(x + experts - j) % experts]
            remote(
                got, got, last_send.at[j - 1], last_recv.at[j - 1], column(x)
            ).wait_recv()
        tokens = routes_b.shape[1]
        lanes = slot_back.shape[2]
        routes = column_of(routes_b[...].astype(f32))
        lane = lax.broadcasted_iota(jnp.int32, (tokens, spread), 1)
        taken = jnp.where(unpack_b > 0, (lane % cap).astype(f32), 0.0)
        slot = jnp.sum(taken, axis=1, keepdims=True)
        lane = lax.broadcasted_iota(jnp.int32, (tokens, lanes), 1)
        first = (y % 2) * spread + x * cap
        here = jnp.broadcast_to(slot, (tokens, lanes)) == (lane - first).astype(f32)
        total = jnp.zeros((tokens, lanes), f32)
        for e in range(experts):
            values = jnp.broadcast_to(slot_back[e][0:1], (tokens, lanes))
            total += jnp.where(here & (routes == float(e)), values, 0.0)
        out_g[...] = row_of(jnp.sum(total, axis=1, keepdims=True))

    spread_wait(0)
    for t in range(HOPS):
        each(chunks, functools.partial(rows.step, t))
    spread_wait(1)
    for r in range(HOLDERS):
        hold_start(*cot(r))
    for load in loads:
        load.wait()
    each(chunks, rows.last)

    def body(p):
        forward(p)
        hids.step(0, p)

    each(PAIRS, body)
    for r in range(HOLDERS):
        hold_own(*deal(r))
        hold_own(*cot(r))
    hold_got(held, deal_send, deal_recv)
    hold_got(cot_b, cot_send, cot_recv)

    def body(p):
        pl.when(holds)(lambda: dhid_partial(p))
        dhids.step(0, p)
        hids.step(1, p)

    each(PAIRS, body)

    def body(p):
        hids.step(2, p)
        dhids.step(1, p)

    each(PAIRS, body)

    def body(p):
        hids.step(3, p)
        dhids.step(2, p)

    each(PAIRS, body)

    def body(p):
        dhids.step(3, p)
        hids.last(p)
        pl.when(holds)(lambda: slice_out(p))

    each(PAIRS, body)

    @pl.when(holds)
    def _():
        slice_got[mine] = slice_part[y]

    backward((y // 2 + PAIRS // 2) % PAIRS)
    each(chunks, lambda c: grads_x.step(0, c))
    backward((y // 2 + PAIRS // 2 + 3 - 2 * (y % 2)) % PAIRS)
    backward((y // 2 + PAIRS // 2 + 1 + 2 * (y % 2)) % PAIRS)
    backward(y // 2)
    slot_step(0)
    each(chunks, straight_mine)
    each(chunks, lambda c: grads_x.step(1, c))
    slot_step(1)
    for r in range(HOLDERS):
        home_a(r)
    each(chunks, lambda c: grads_x.step(2, c))
    slot_step(2)
    each(chunks, lambda c: grads_x.step(3, c, straight_last))
    slot_step(3)
    for r in range(HOLDERS):
        finish_a(r)

    for ab in (0, 1):
        pipe_copy(ab).wait_send()
        for j in range(1, experts):
            spread_copy(ab, j).wait_send()
    for r in range(HOLDERS):
        hold_sent(*deal(r))
        hold_sent(*cot(r))
    each(chunks, rows.sent)
    each(PAIRS, dhids.sent)
    each(PAIRS, hids.sent)

    def body(b):
        pl.when(b != y)(lambda: slice_copy(b).wait_send())

    pl.when(holds)(lambda: each(GROUP, body))

    slot_last()

    for r in range(HOLDERS):
        for j in range(1, experts):
            home_a_copy(r, j).wait_send()
    each(chunks, lambda c: grads_x.sent(c, HOPS - 1))
    slot_finish()

    def body(c):
        straight_finish(c)
        straight_sent(c)

    each(chunks, body)
    for d, sign in WAYS:
        for t in range(d, HOPS):
            slot_copy(d, t, sign).wait_send()
    for j in range(1, experts):
        last_copy(j).wait_send()


def on_device(
    section_acts,
    fwd_routes,
    fwd_gates,
    section_grads,
    bwd_routes,
    bwd_gates,
    saved_proj,
    w_gate,
    w_up,
    w_down,
):
    experts = lax.axis_size("expert") // GROUP
    _, tokens, model = section_acts.shape
    cap, hidden = saved_proj.shape[3], w_gate.shape[3]
    width = model // CHUNKS
    sources = saved_proj.shape[1]
    spread = experts * cap
    lanes = 2 * spread
    size = model // HOLDERS
    whole = (tokens, model)
    by_slice = (experts, HOLDERS, cap, size)
    by_chunk = (experts, CHUNKS, cap, width)
    blocks = (CHUNKS, experts, cap, width)
    hids = (PAIRS, 2, spread, hidden)
    dma = pltpu.SemaphoreType.DMA
    hbm = pl.BlockSpec(memory_space=pltpu.HBM)
    vmem = pl.BlockSpec(memory_space=pltpu.VMEM)

    def as_row(array):
        return array.reshape(1, tokens)

    def two(*shape):
        return [dma(shape), dma(shape)]

    shapes = [
        whole,
        whole,
        by_chunk,
        by_slice,
        (GROUP,) + blocks,
        by_slice,
        (GROUP, experts, cap, size),
        (GROUP, hidden, size),
        (GROUP,) + hids,
        (2, HOPS) + hids,
        (GROUP,) + hids,
        (GROUP, experts, cap, size),
        (HOLDERS, experts, cap, size),
        (GROUP,) + blocks,
        (2, HOPS) + blocks,
        (HOLDERS, experts, cap, size),
        (CHUNKS, 3, experts, cap, width),
        (model, 2 * hidden),
        (sources, cap, 2 * hidden),
    ]
    slots = [(PAIRS, 8, lanes), (2, HOPS, 8, lanes), (2, HOPS, 8, lanes), (8, lanes)]
    slots.append((experts, 8, lanes))

    out_a, out_b, out_g = pl.pallas_call(
        kernel,
        out_shape=(
            pltpu.VMEM(section_acts.shape, bf16),
            pltpu.VMEM(section_grads.shape, bf16),
            pltpu.VMEM((1, tokens), f32),
        ),
        in_specs=[hbm, hbm, vmem, vmem, vmem, vmem, hbm, hbm, hbm, hbm],
        out_specs=(vmem, vmem, vmem),
        scratch_shapes=[pltpu.VMEM(shape, bf16) for shape in shapes]
        + [pltpu.VMEM(shape, f32) for shape in slots]
        + [dma((3,))]
        + two(2)
        + two(2, experts - 1)
        + [dma((HOLDERS,)), dma((GROUP,))] * 2
        + two(2, HOPS * CHUNKS)
        + two(2, HOPS * PAIRS)
        + two(2, HOPS * PAIRS)
        + [dma((GROUP,)), dma((HOLDERS,))]
        + two(HOLDERS, experts - 1)
        + two(2, HOPS * CHUNKS)
        + [dma((CHUNKS, 3, experts)), dma((CHUNKS,))]
        + two(2, HOPS)
        + two(experts - 1),
        compiler_params=pltpu.CompilerParams(
            collective_id=0, has_side_effects=True, vmem_limit_bytes=56 * 2**20
        ),
        cost_estimate=pl.CostEstimate(
            flops=2 * 2 * GROUP * spread * model * 3 * hidden,
            bytes_accessed=2 * 3 * model * hidden + 8 * tokens * model,
            transcendentals=2 * GROUP * spread * hidden,
        ),
        name="relay_experts",
    )(
        section_acts,
        section_grads,
        as_row(fwd_routes),
        as_row(fwd_gates),
        as_row(bwd_routes),
        as_row(bwd_gates),
        saved_proj,
        w_gate,
        w_up,
        w_down,
    )
    return out_a, out_b, out_g.reshape(1, tokens, 1)


def solution(mesh):
    tokens = P("pipe", "expert", None)
    weights = P("pipe", "expert", None, None)
    placed = (tokens,) * 6 + (P("pipe", None, "expert", None, None),) + (weights,) * 3
    return jax.shard_map(
        on_device, mesh=mesh, in_specs=placed, out_specs=(tokens,) * 3, check_vma=False
    )
```

```python
import functools

import jax
import jax.numpy as jnp
from jax import lax
from jax.experimental import pallas as pl
from jax.experimental.pallas import tpu as pltpu
from jax.sharding import PartitionSpec as P

GROUP = 8
CHUNKS = 4
PAIRS = GROUP // 2
LANES = 128
HOLDERS = GROUP // 2
HOPS = 4
MESH = pl.DeviceIdType.MESH
WAYS = ((0, 1), (1, -1))
f32 = jnp.float32
bf16 = jnp.bfloat16


def nt_dot(a, b):
    return lax.dot_general(a, b, (((1,), (1,)), ((), ())), preferred_element_type=f32)


def column_of(row):
    count = row.shape[1]
    shape = (count, count)
    eye = lax.broadcasted_iota(jnp.int32, shape, 0) == lax.broadcasted_iota(jnp.int32, shape, 1)
    return jnp.sum(jnp.where(eye, jnp.broadcast_to(row, shape), 0.0), axis=1, keepdims=True)


def row_of(column):
    count = column.shape[0]
    shape = (count, count)
    eye = lax.broadcasted_iota(jnp.int32, shape, 0) == lax.broadcasted_iota(jnp.int32, shape, 1)
    return jnp.sum(jnp.where(eye, jnp.broadcast_to(column, shape), 0.0), axis=0, keepdims=True)


def place_matrices(route_row, experts, cap):
    tokens = route_row.shape[1]
    slots = experts * cap
    routes = route_row.astype(f32)
    column = column_of(routes)
    at = lax.broadcasted_iota(jnp.int32, (tokens, tokens), 0)
    other = lax.broadcasted_iota(jnp.int32, (tokens, tokens), 1)
    slot = lax.broadcasted_iota(jnp.int32, (slots, tokens), 0)
    named = jnp.broadcast_to(routes, (slots, tokens)) == (slot // cap).astype(f32)
    before = jnp.dot(
        jnp.where(named, 1.0, 0.0).astype(bf16),
        jnp.where(at < other, 1.0, 0.0).astype(bf16),
        preferred_element_type=f32,
    )
    pack = jnp.where(named & (before == (slot % cap).astype(f32)), 1.0, 0.0).astype(bf16)
    slot = lax.broadcasted_iota(jnp.int32, (tokens, slots), 1)
    named = jnp.broadcast_to(column, (tokens, slots)) == (slot // cap).astype(f32)
    before = jnp.dot(
        jnp.where(other < at, 1.0, 0.0).astype(bf16),
        jnp.where(named, 1.0, 0.0).astype(bf16),
        preferred_element_type=f32,
    )
    unpack = jnp.where(named & (before == (slot % cap).astype(f32)), 1.0, 0.0).astype(bf16)
    return pack, unpack


def kernel(
    acts,
    grads,
    routes_a,
    gates_a,
    routes_b,
    gates_b,
    kept,
    w_gate,
    w_up,
    w_down,
    results,
    out_g,
    in_a,
    in_b,
    packed_a,
    packed_b,
    rows_a,
    local_b,
    cot_b,
    held,
    dhid_part,
    dhid_sums,
    hid_all,
    slice_part,
    slice_got,
    part_b,
    sums_b,
    back_a,
    straight,
    both_w,
    saved,
    slot_own,
    slot_sent,
    slot_got,
    slot_fold,
    slot_back,
    load_sem,
    pipe_send,
    pipe_recv,
    spread_send,
    spread_recv,
    deal_send,
    deal_recv,
    cot_send,
    cot_recv,
    rows_send,
    rows_recv,
    dhid_send,
    dhid_recv,
    hid_send,
    hid_recv,
    slice_send,
    slice_recv,
    home_a_send,
    home_a_recv,
    fold_send,
    fold_recv,
    straight_send,
    straight_recv,
    slot_send,
    slot_recv,
    last_send,
    last_recv,
):
    stage = lax.axis_index("pipe")
    stages = lax.axis_size("pipe")
    index = lax.axis_index("expert")
    x = index // GROUP
    y = index % GROUP
    experts, chunks, cap, width = packed_a.shape
    model, hidden = both_w.shape[0], both_w.shape[1] // 2
    spread = experts * cap
    size = model // HOLDERS
    turn = stage % 2
    holds = y % 2 == turn
    passes = y % 2 != turn
    mine = y // 2

    def holder(r):
        return 2 * r + turn

    def at_y(yy):
        return {"expert": x * GROUP + yy}

    def column(xx):
        return {"expert": xx * GROUP + y}

    def beside(j, by):
        return {"expert": (x + j) % experts * GROUP + (y + GROUP + by) % GROUP}

    def ring(by):
        return {"expert": x * GROUP + (y + GROUP + by) % GROUP}

    def along(by):
        return {"pipe": (stage + stages + by) % stages}

    def remote(src, dst, send, recv, device):
        return pltpu.make_async_remote_copy(
            src_ref=src,
            dst_ref=dst,
            send_sem=send,
            recv_sem=recv,
            device_id=device,
            device_id_type=MESH,
        )

    def each(count, body, first=0):
        lax.fori_loop(first, count, lambda c, carry: (body(c), carry)[1], 0)

    def columns(c):
        return pl.ds(c * width if isinstance(c, int) else pl.multiple_of(c * width, LANES), width)

    barrier = pltpu.get_barrier_semaphore()
    partners = [along(1), along(-1)] + [ring(j) for j in range(1, GROUP)]
    partners += [column((x + j) % experts) for j in range(1, experts)]
    partners += [beside(j, sign) for j in range(1, experts) for _, sign in WAYS]
    for partner in partners:
        pl.semaphore_signal(barrier, inc=1, device_id=partner, device_id_type=MESH)
    pl.semaphore_wait(barrier, len(partners))

    def pipe_copy(ab):
        source, target = ((acts, in_a), (grads, in_b))[ab]
        return remote(
            source.at[0], target, pipe_send.at[ab], pipe_recv.at[ab], along(1 - 2 * ab)
        )

    for ab in (0, 1):
        pipe_copy(ab).start()

    def to_holder(r, source, target, send, recv):
        return remote(source, target.at[y], send.at[r], recv.at[y], at_y(holder(r)))

    def to_self(r, source, target, send):
        return pltpu.make_async_copy(source, target.at[y], send.at[r])

    def hold_start(r, source, *rest):
        pl.when(holder(r) != y)(lambda: to_holder(r, source, *rest).start())
        pl.when(holder(r) == y)(lambda: to_self(r, source, *rest[:2]).start())

    def hold_sent(r, source, *rest):
        pl.when(holder(r) != y)(lambda: to_holder(r, source, *rest).wait_send())

    def hold_own(r, source, *rest):
        pl.when(holder(r) == y)(lambda: to_self(r, source, *rest[:2]).wait())

    def hold_got(target, send, recv):
        def body(g):
            got = target.at[g]
            pl.when(g != y)(
                lambda: remote(got, got, send.at[0], recv.at[g], at_y(g)).wait_recv()
            )

        pl.when(holds)(lambda: each(GROUP, body))

    def deal(r):
        source = w_down.at[0, 0, :, pl.ds(r * size, size)]
        return r, source, held, deal_send, deal_recv

    def cot(r):
        return r, local_b.at[:, r], cot_b, cot_send, cot_recv

    for r in range(HOLDERS):
        hold_start(*deal(r))
    loads = [
        pltpu.make_async_copy(w_gate.at[0, 0], both_w.at[:, pl.ds(0, hidden)], load_sem.at[0]),
        pltpu.make_async_copy(w_up.at[0, 0], both_w.at[:, pl.ds(hidden, hidden)], load_sem.at[1]),
        pltpu.make_async_copy(kept.at[0, :, 0], saved, load_sem.at[2]),
    ]
    for load in loads:
        load.start()

    @pl.when(passes)
    def _():
        dhid_part[y] = jnp.zeros(dhid_part.shape[1:], bf16)

    pack_a, unpack_a = place_matrices(routes_a[...], experts, cap)
    pack_b, unpack_b = place_matrices(routes_b[...], experts, cap)
    gate_a = column_of(gates_a[...])
    gate_b = column_of(gates_b[...].astype(bf16).astype(f32))

    def spread_copy(ab, j):
        to = (x + j) % experts
        return remote(
            (packed_a, packed_b)[ab].at[to],
            (rows_a.at[y, :, x], local_b.at[x])[ab],
            spread_send.at[ab, j - 1],
            spread_recv.at[ab, j - 1],
            column(to),
        )

    def spread_wait(ab):
        for j in range(1, experts):
            sender = (x + experts - j) % experts
            got = (rows_a.at[y, :, sender], local_b.at[sender])[ab]
            remote(
                got, got, spread_send.at[ab, j - 1], spread_recv.at[ab, j - 1], column(x)
            ).wait_recv()

    def packed_rows(pack, source, start, size):
        chosen = jnp.dot(pack, source[:, start : start + size], preferred_element_type=f32)
        return chosen.astype(bf16).reshape(experts, cap, size)

    pipe_copy(0).wait_recv()
    for c in range(chunks):
        packed_a[:, c] = packed_rows(pack_a, in_a, c * width, width)
    for j in range(1, experts):
        spread_copy(0, j).start()
    rows_a[y, :, x] = packed_a[x]
    pipe_copy(1).wait_recv()
    for r in range(HOLDERS):
        packed_b[:, r] = packed_rows(pack_b, in_b, r * size, size)
    for j in range(1, experts):
        spread_copy(1, j).start()
    local_b[x] = packed_b[x]

    def halves(ref, d, t, far):
        half = ref.shape[0] // 2
        return ref.at[pl.ds(d * half, half)] if t == far else ref

    class Gather:
        def __init__(self, blocks, send, recv):
            self.blocks, self.send, self.recv = blocks, send, recv
            self.count = blocks.shape[1]

        def copy(self, t, c, d, sign, on=0, part=False):
            at = self.blocks.at[(y + GROUP - sign * (t + on)) % GROUP, c]
            at = halves(at, d, t, t if part else HOPS - 1)
            k = t * self.count + c
            return remote(at, at, self.send.at[d, k], self.recv.at[d, k], ring(sign))

        def step(self, t, c):
            for d, sign in WAYS:
                if t:
                    self.copy(t - 1, c, d, sign, 1).wait_recv()
                self.copy(t, c, d, sign).start()

        def last(self, c):
            for d, sign in WAYS:
                self.copy(HOPS - 1, c, d, sign, 1).wait_recv()

        def sent(self, c):
            for t in range(HOPS):
                for d, sign in WAYS:
                    self.copy(t, c, d, sign).wait_send()

    class HolderGather(Gather):
        def step(self, t, c):
            for d, sign in WAYS:
                if t == 1 or t == 2:
                    self.copy(t - 1, c, d, sign, 1).wait_recv()
                if t < 2:
                    self.copy(t, c, d, sign).start()
                elif t == 2:
                    pl.when(holds)(lambda: self.copy(2, c, d, sign, 0, True).start())
                    pl.when(passes)(lambda: self.copy(2, c, d, sign).start())
                else:
                    pl.when(holds)(lambda: self.copy(2, c, d, sign, 1).wait_recv())

                    @pl.when(passes)
                    def _():
                        self.copy(2, c, d, sign, 1, True).wait_recv()
                        self.copy(3, c, d, sign, 0, True).start()

        def last(self, c):
            for d, sign in WAYS:
                pl.when(holds)(lambda: self.copy(3, c, d, sign, 1, True).wait_recv())

        def sent(self, c):
            for d, sign in WAYS:
                for t in (0, 1):
                    self.copy(t, c, d, sign).wait_send()
                pl.when(holds)(lambda: self.copy(2, c, d, sign, 0, True).wait_send())

                @pl.when(passes)
                def _():
                    self.copy(2, c, d, sign).wait_send()
                    self.copy(3, c, d, sign, 0, True).wait_send()

    class Fold:
        def __init__(self, part, sums, send, recv):
            self.part, self.sums, self.send, self.recv = part, sums, send, recv
            self.count = part.shape[1]

        def copy(self, t, c, d, sign):
            at = self.part.at[(y + GROUP + sign * (HOPS - t)) % GROUP, c]
            k = t * self.count + c
            return remote(
                halves(at, d, t, 0),
                halves(self.sums.at[d, t, c], d, t, 0),
                self.send.at[d, k],
                self.recv.at[d, k],
                ring(sign),
            )

        def step(self, t, c, straight=None):
            half = self.part.shape[2] // 2
            for d, sign in WAYS:
                block = (y + GROUP + sign * (HOPS - t)) % GROUP
                if t:
                    self.copy(t - 1, c, d, sign).wait_recv()
                    at = pl.ds(d * half, half) if t == 1 else pl.ds(0, 2 * half)
                    self.part[block, c, at] = (
                        self.part[block, c, at].astype(f32)
                        + self.sums[d, t - 1, c, at].astype(f32)
                    ).astype(bf16)
                if straight is None:
                    self.copy(t, c, d, sign).start()
                else:
                    straight(c, d, sign, block)

        def total(self, c):
            for d, sign in WAYS:
                self.copy(HOPS - 1, c, d, sign).wait_recv()
            return (
                self.part[y, c].astype(f32)
                + self.sums[0, HOPS - 1, c].astype(f32)
                + self.sums[1, HOPS - 1, c].astype(f32)
            )

        def sent(self, c, hops=HOPS):
            for t in range(hops):
                for d, sign in WAYS:
                    self.copy(t, c, d, sign).wait_send()

    class HolderFold(Fold):
        def onward(self, t, c, d, sign, part=False, at=None):
            k = t * self.count + c
            source = self.sums.at[d, t if at is None else at, c]
            target = self.sums.at[d, t, c]
            return remote(
                halves(source, d, t, t if part else HOPS),
                halves(target, d, t, t if part else HOPS),
                self.send.at[d, k],
                self.recv.at[d, k],
                ring(sign),
            )

        def step(self, t, c):
            half = self.part.shape[2] // 2
            for d, sign in WAYS:

                @pl.when(holds)
                def _():
                    if t >= 2:
                        self.onward(t - 1, c, d, sign, t == 2).wait_recv()
                        block = (y + GROUP + sign * (HOPS - t)) % GROUP
                        at = pl.ds(d * half, half) if t == 2 else pl.ds(0, 2 * half)
                        self.part[block, c, at] = (
                            self.part[block, c, at].astype(f32)
                            + self.sums[d, t - 1, c, at].astype(f32)
                        ).astype(bf16)
                    self.copy(t, c, d, sign).start()

                if t:

                    @pl.when(passes)
                    def _():
                        self.onward(t - 1, c, d, sign, t == 1).wait_recv()
                        self.onward(t, c, d, sign, t == 1, t - 1).start()

        def sent(self, c):
            for d, sign in WAYS:

                @pl.when(holds)
                def _():
                    for t in range(HOPS):
                        self.copy(t, c, d, sign).wait_send()

                @pl.when(passes)
                def _():
                    for t in range(1, HOPS):
                        self.onward(t, c, d, sign, t == 1, t - 1).wait_send()

    rows = Gather(rows_a, rows_send, rows_recv)
    hids = HolderGather(hid_all, hid_send, hid_recv)
    dhids = HolderFold(dhid_part, dhid_sums, dhid_send, dhid_recv)
    grads_x = Fold(part_b, sums_b, fold_send, fold_recv)

    def dhid_partial(p):
        here = cot_b[pl.ds(2 * p, 2)].reshape(2 * spread, size)
        dhid = nt_dot(here, held[...].reshape(GROUP * hidden, size)).astype(bf16)
        for g in range(GROUP):
            dhid_part[g, p] = dhid[:, g * hidden : (g + 1) * hidden].reshape(2, spread, hidden)

    def forward(p):
        pre = jnp.zeros((2 * spread, 2 * hidden), f32)
        for c in range(chunks):
            pre += jnp.dot(
                rows_a[pl.ds(2 * p, 2), c].reshape(2 * spread, width),
                both_w[pl.ds(c * width, width), :],
                preferred_element_type=f32,
            )
        pre_g, pre_u = pre[:, :hidden], pre[:, hidden:]
        hid = (pre_g * jax.nn.sigmoid(pre_g) * pre_u).astype(bf16)
        hid_all[y, p] = hid.reshape(2, spread, hidden)

    def forward_out(p):
        hid = jnp.concatenate(
            [hid_all[g, p].reshape(2 * spread, hidden) for g in range(GROUP)], axis=1
        )
        done = jnp.dot(
            hid, held[...].reshape(GROUP * hidden, size), preferred_element_type=f32
        )
        slice_part[pl.ds(2 * p, 2)] = done.astype(bf16).reshape(2, experts, cap, size)

    def backward(p):
        dhid = dhids.total(p).reshape(2 * spread, hidden)
        both = jnp.concatenate(
            [saved[j * GROUP + 2 * p + i] for i in (0, 1) for j in range(experts)], axis=0
        ).astype(f32)
        sg, su = both[:, :hidden], both[:, hidden:]
        sig = jax.nn.sigmoid(sg)
        act = sg * sig
        hid = (act * su).astype(bf16).astype(f32)
        slot_row = jnp.sum((hid * dhid).T, axis=0, keepdims=True)
        slot_own[p] = jnp.broadcast_to(slot_row, slot_own.shape[1:])
        d_g = (dhid * su * sig * (1.0 + sg * (1.0 - sig))).astype(bf16)
        d_u = (dhid * act).astype(bf16)
        d_both = jnp.concatenate([d_g, d_u], axis=1)
        for c in range(chunks):
            part_b[pl.ds(2 * p, 2), c] = (
                nt_dot(d_both, both_w[pl.ds(c * width, width), :])
                .astype(bf16)
                .reshape(2, experts, cap, width)
            )

    def slice_copy(b):
        return remote(
            slice_part.at[b], slice_got.at[mine], slice_send.at[b], slice_recv.at[mine], at_y(b)
        )

    def slice_out(p):
        forward_out(p)
        for b in (2 * p, 2 * p + 1):
            pl.when(b != y)(lambda: slice_copy(b).start())

    def home_a_copy(r, j):
        to = (x + j) % experts
        return remote(
            slice_got.at[r, to],
            back_a.at[r, x],
            home_a_send.at[r, j - 1],
            home_a_recv.at[r, j - 1],
            column(to),
        )

    def home_a(r):
        @pl.when(holder(r) != y)
        def _():
            got = slice_got.at[r]
            remote(got, got, slice_send.at[0], slice_recv.at[r], ring(1)).wait_recv()

        for j in range(1, experts):
            home_a_copy(r, j).start()
        back_a[r, x] = slice_got[r, x]

    def finish_a(r):
        for j in range(1, experts):
            got = back_a.at[r, (x + experts - j) % experts]
            remote(
                got, got, home_a_send.at[r, j - 1], home_a_recv.at[r, j - 1], column(x)
            ).wait_recv()
        picked = jnp.dot(
            unpack_a, back_a[r].reshape(spread, size), preferred_element_type=f32
        )
        at = slice(r * size, (r + 1) * size)
        results[0, :, at] = (in_a[:, at].astype(f32) + gate_a * picked).astype(bf16)

    def straight_copy(c, d, j, sign, block):
        return remote(
            part_b.at[block, c, (x + j) % experts],
            straight.at[c, d, x],
            straight_send.at[c, d, j],
            straight_recv.at[c],
            beside(j, sign),
        )

    def straight_own(c):
        return pltpu.make_async_copy(
            part_b.at[y, c, x], straight.at[c, 2, x], straight_recv.at[c]
        )

    def straight_mine(c):
        straight_own(c).start()
        for j in range(1, experts):
            straight_copy(c, 2, j, 0, y).start()

    def straight_last(c, d, sign, block):
        for j in range(experts):
            straight_copy(c, d, j, sign, block).start()

    def straight_sent(c):
        for d, sign in WAYS:
            block = (y + GROUP + sign) % GROUP
            for j in range(experts):
                straight_copy(c, d, j, sign, block).wait_send()
        for j in range(1, experts):
            straight_copy(c, 2, j, 0, y).wait_send()

    def straight_finish(c):
        got = straight.at[c]
        remote(
            got, got, straight_send.at[c, 0, 0], straight_recv.at[c], column(x)
        ).wait_recv()
        picked = jnp.zeros((in_b.shape[0], width), f32)
        for d in range(3):
            rows_d = straight[c, d].reshape(spread, width)
            picked += jnp.dot(unpack_b, rows_d, preferred_element_type=f32)
        results[1, :, columns(c)] = (in_b[:, columns(c)].astype(f32) + gate_b * picked).astype(bf16)

    def slot_copy(d, t, sign):
        return remote(
            slot_sent.at[d, t],
            slot_got.at[d, t],
            slot_send.at[d, t],
            slot_recv.at[d, t],
            ring(sign),
        )

    def slot_step(t):
        for d, sign in WAYS:
            if t < d:
                continue
            pair = ((y + GROUP + sign * (HOPS - t)) % GROUP) // 2
            if t > d:
                slot_copy(d, t - 1, sign).wait_recv()
                slot_sent[d, t] = slot_own[pair] + slot_got[d, t - 1]
            else:
                slot_sent[d, t] = slot_own[pair]
            slot_copy(d, t, sign).start()

    def last_copy(j):
        return remote(
            slot_fold,
            slot_back.at[x],
            last_send.at[j - 1],
            last_recv.at[j - 1],
            column((x + j) % experts),
        )

    def slot_last():
        for d, sign in WAYS:
            slot_copy(d, HOPS - 1, sign).wait_recv()
        slot_fold[...] = slot_own[y // 2] + slot_got[0, HOPS - 1] + slot_got[1, HOPS - 1]
        for j in range(1, experts):
            last_copy(j).start()
        slot_back[x] = slot_fold[...]

    def slot_finish():
        for j in range(1, experts):
            got = slot_back.at[(x + experts - j) % experts]
            remote(
                got, got, last_send.at[j - 1], last_recv.at[j - 1], column(x)
            ).wait_recv()
        tokens = routes_b.shape[1]
        lanes = slot_back.shape[2]
        routes = column_of(routes_b[...].astype(f32))
        lane = lax.broadcasted_iota(jnp.int32, (tokens, spread), 1)
        taken = jnp.where(unpack_b > 0, (lane % cap).astype(f32), 0.0)
        slot = jnp.sum(taken, axis=1, keepdims=True)
        lane = lax.broadcasted_iota(jnp.int32, (tokens, lanes), 1)
        first = (y % 2) * spread + x * cap
        here = jnp.broadcast_to(slot, (tokens, lanes)) == (lane - first).astype(f32)
        total = jnp.zeros((tokens, lanes), f32)
        for e in range(experts):
            values = jnp.broadcast_to(slot_back[e][0:1], (tokens, lanes))
            total += jnp.where(here & (routes == float(e)), values, 0.0)
        out_g[...] = row_of(jnp.sum(total, axis=1, keepdims=True))

    spread_wait(0)
    for t in range(HOPS):
        each(chunks, functools.partial(rows.step, t))
    spread_wait(1)
    for r in range(HOLDERS):
        hold_start(*cot(r))
    for load in loads:
        load.wait()
    each(chunks, rows.last)

    def body(p):
        forward(p)
        hids.step(0, p)

    each(PAIRS, body)
    for r in range(HOLDERS):
        hold_own(*deal(r))
        hold_own(*cot(r))
    hold_got(held, deal_send, deal_recv)
    hold_got(cot_b, cot_send, cot_recv)

    def body(p):
        pl.when(holds)(lambda: dhid_partial(p))
        dhids.step(0, p)
        hids.step(1, p)

    each(PAIRS, body)

    def body(p):
        hids.step(2, p)
        dhids.step(1, p)

    each(PAIRS, body)

    def body(p):
        hids.step(3, p)
        dhids.step(2, p)

    each(PAIRS, body)

    def body(p):
        dhids.step(3, p)
        hids.last(p)
        pl.when(holds)(lambda: slice_out(p))

    each(PAIRS, body)

    @pl.when(holds)
    def _():
        slice_got[mine] = slice_part[y]

    backward((y // 2 + PAIRS // 2) % PAIRS)
    each(chunks, lambda c: grads_x.step(0, c))
    backward((y // 2 + PAIRS // 2 + 3 - 2 * (y % 2)) % PAIRS)
    backward((y // 2 + PAIRS // 2 + 1 + 2 * (y % 2)) % PAIRS)
    backward(y // 2)
    slot_step(0)
    each(chunks, straight_mine)
    each(chunks, lambda c: grads_x.step(1, c))
    slot_step(1)
    for r in range(HOLDERS):
        home_a(r)
    each(chunks, lambda c: grads_x.step(2, c))
    slot_step(2)
    each(chunks, lambda c: grads_x.step(3, c, straight_last))
    slot_step(3)
    for r in range(HOLDERS):
        finish_a(r)

    for ab in (0, 1):
        pipe_copy(ab).wait_send()
        for j in range(1, experts):
            spread_copy(ab, j).wait_send()
    for r in range(HOLDERS):
        hold_sent(*deal(r))
        hold_sent(*cot(r))
    each(chunks, rows.sent)
    each(PAIRS, dhids.sent)
    each(PAIRS, hids.sent)

    def body(b):
        pl.when(b != y)(lambda: slice_copy(b).wait_send())

    pl.when(holds)(lambda: each(GROUP, body))

    slot_last()

    for r in range(HOLDERS):
        for j in range(1, experts):
            home_a_copy(r, j).wait_send()
    each(chunks, lambda c: grads_x.sent(c, HOPS - 1))
    slot_finish()

    def body(c):
        straight_finish(c)
        straight_sent(c)

    each(chunks, body)
    for d, sign in WAYS:
        for t in range(d, HOPS):
            slot_copy(d, t, sign).wait_send()
    for j in range(1, experts):
        last_copy(j).wait_send()


def on_device(
    section_acts,
    fwd_routes,
    fwd_gates,
    section_grads,
    bwd_routes,
    bwd_gates,
    saved_proj,
    w_gate,
    w_up,
    w_down,
):
    experts = lax.axis_size("expert") // GROUP
    _, tokens, model = section_acts.shape
    cap, hidden = saved_proj.shape[3], w_gate.shape[3]
    width = model // CHUNKS
    sources = saved_proj.shape[1]
    spread = experts * cap
    lanes = 2 * spread
    size = model // HOLDERS
    whole = (tokens, model)
    by_slice = (experts, HOLDERS, cap, size)
    by_chunk = (experts, CHUNKS, cap, width)
    blocks = (CHUNKS, experts, cap, width)
    hids = (PAIRS, 2, spread, hidden)
    dma = pltpu.SemaphoreType.DMA
    hbm = pl.BlockSpec(memory_space=pltpu.HBM)
    vmem = pl.BlockSpec(memory_space=pltpu.VMEM)

    def as_row(array):
        return array.reshape(1, tokens)

    def two(*shape):
        return [dma(shape), dma(shape)]

    shapes = [
        whole,
        whole,
        by_chunk,
        by_slice,
        (GROUP,) + blocks,
        by_slice,
        (GROUP, experts, cap, size),
        (GROUP, hidden, size),
        (GROUP,) + hids,
        (2, HOPS) + hids,
        (GROUP,) + hids,
        (GROUP, experts, cap, size),
        (HOLDERS, experts, cap, size),
        (GROUP,) + blocks,
        (2, HOPS) + blocks,
        (HOLDERS, experts, cap, size),
        (CHUNKS, 3, experts, cap, width),
        (model, 2 * hidden),
        (sources, cap, 2 * hidden),
    ]
    slots = [(PAIRS, 8, lanes), (2, HOPS, 8, lanes), (2, HOPS, 8, lanes), (8, lanes)]
    slots.append((experts, 8, lanes))

    results, out_g = pl.pallas_call(
        kernel,
        out_shape=(
            pltpu.VMEM((2, tokens, model), bf16),
            pltpu.VMEM((1, tokens), f32),
        ),
        in_specs=[hbm, hbm, vmem, vmem, vmem, vmem, hbm, hbm, hbm, hbm],
        out_specs=(vmem, vmem),
        scratch_shapes=[pltpu.VMEM(shape, bf16) for shape in shapes]
        + [pltpu.VMEM(shape, f32) for shape in slots]
        + [dma((3,))]
        + two(2)
        + two(2, experts - 1)
        + [dma((HOLDERS,)), dma((GROUP,))] * 2
        + two(2, HOPS * CHUNKS)
        + two(2, HOPS * PAIRS)
        + two(2, HOPS * PAIRS)
        + [dma((GROUP,)), dma((HOLDERS,))]
        + two(HOLDERS, experts - 1)
        + two(2, HOPS * CHUNKS)
        + [dma((CHUNKS, 3, experts)), dma((CHUNKS,))]
        + two(2, HOPS)
        + two(experts - 1),
        compiler_params=pltpu.CompilerParams(
            collective_id=0, has_side_effects=True, vmem_limit_bytes=56 * 2**20
        ),
        cost_estimate=pl.CostEstimate(
            flops=2 * 2 * GROUP * spread * model * 3 * hidden,
            bytes_accessed=2 * 3 * model * hidden + 8 * tokens * model,
            transcendentals=2 * GROUP * spread * hidden,
        ),
        name="relay_experts",
    )(
        section_acts,
        section_grads,
        as_row(fwd_routes),
        as_row(fwd_gates),
        as_row(bwd_routes),
        as_row(bwd_gates),
        saved_proj,
        w_gate,
        w_up,
        w_down,
    )
    return results[:1], results[1:], out_g.reshape(1, tokens, 1)


def solution(mesh):
    tokens = P("pipe", "expert", None)
    weights = P("pipe", "expert", None, None)
    placed = (tokens,) * 6 + (P("pipe", None, "expert", None, None),) + (weights,) * 3
    return jax.shard_map(
        on_device, mesh=mesh, in_specs=placed, out_specs=(tokens,) * 3, check_vma=False
    )
```
